128 devices in a mesh: dp: 2 (over y_hi), fsdp: 64 (over y_lo, z, x, core).
Axes of the slice: x: 4, y: 4 (y_hi: 2, y_lo: 2; y = y_hi * 2 + y_lo), z: 4, core: 2. Of those that a mesh axis runs over, the one named last changes fastest.
Arguments:
- tokens: bfloat16 [65536, 768], P(('dp', 'fsdp')), may hold values from -6 to 6
- lengths: int32 [128, 16], replicated, may hold values from 1 to 64, as said below
- ln1_gain: bfloat16 [768], P('fsdp'), may hold values from 0.5 to 1.5
- ln1_bias: bfloat16 [768], P('fsdp'), may hold values from -3 to 3
- w_qkv: bfloat16 [768, 2304], P('fsdp'), may hold values from -0.21875 to 0.21875
- q_bias: bfloat16 [768], P('fsdp'), may hold values from -3 to 3
- v_bias: bfloat16 [768], P('fsdp'), may hold values from -3 to 3
- w_out: bfloat16 [768, 768], P('fsdp'), may hold values from -1.25 to 1.25
- out_bias: bfloat16 [768], P('fsdp'), may hold values from -3 to 3
- ln2_gain: bfloat16 [768], P('fsdp'), may hold values from 0.5 to 1.5
- ln2_bias: bfloat16 [768], P('fsdp'), may hold values from -3 to 3
- w_in: bfloat16 [768, 3072], P('fsdp'), may hold values from -0.21875 to 0.21875
- in_bias: bfloat16 [3072], P('fsdp'), may hold values from -3 to 3
- w_back: bfloat16 [3072, 768], P('fsdp'), may hold values from -0.15625 to 0.15625
- back_bias: bfloat16 [768], P('fsdp'), may hold values from -3 to 3
- cotangent: bfloat16 [65536, 768], P(('dp', 'fsdp')), may hold values from -6 to 6
Outputs:
- hidden: bfloat16 [65536, 768], P(('dp', 'fsdp'))
- input_grad: float32 [65536, 768], P(('dp', 'fsdp'))
- ln1_gain_grad: float32 [768], P('fsdp')
- ln1_bias_grad: float32 [768], P('fsdp')
- w_qkv_grad: float32 [768, 2304], P('fsdp')
- q_bias_grad: float32 [768], P('fsdp')
- v_bias_grad: float32 [768], P('fsdp')
- w_out_grad: float32 [768, 768], P('fsdp')
- out_bias_grad: float32 [768], P('fsdp')
- ln2_gain_grad: float32 [768], P('fsdp')
- ln2_bias_grad: float32 [768], P('fsdp')
- w_in_grad: float32 [768, 3072], P('fsdp')
- in_bias_grad: float32 [3072], P('fsdp')
- w_back_grad: float32 [3072, 768], P('fsdp')
- back_bias_grad: float32 [768], P('fsdp')
The draws below stay inside these ranges and needn't reach their ends.
Inputs may be any that keep to these rules, and one draw needn't show every extreme that they name: Each row holds the 16 caption lengths of one packed sequence, adding up to 512; every row's longest caption is exactly 64.
All inputs are finite; a program needn't handle non-finite values.
Results may differ from the reference program's by a relative error of at most 0.012.
Values may be sent and summed in bfloat16 or wider, within the bound.
No kernel may reach another device: no remote copies, remote signals or barrier semaphores. Data moves between devices by JAX's collectives and lax.ppermute only.
A program may use at most 192 MiB of HBM per device.

```python
import math
import jax
import jax.numpy as jnp
from jax import lax

D = 768
HEADS = 12
HEAD_DIM = 64
FF = 3072
LEN = 512
NSEG = 16
CAP = 64
SEQUENCES = 128
TOKENS = 65536


def spread_lengths(key, total, count, reach):
    base = total // count
    extra = total % count
    index = jnp.arange(count, dtype=jnp.int32)
    start = base[:, None] + (index[None, :] < extra[:, None]).astype(jnp.int32)
    shifts = jax.random.randint(key, (total.shape[0], count), 0, reach, dtype=jnp.int32)
    return start + shifts - jnp.roll(shifts, -1, axis=1)


def draw_lengths(key, part):
    key = jax.random.fold_in(key, 7)
    key_off, key_first, key_second = jax.random.split(key, 3)
    offset = jax.random.randint(key_off, (SEQUENCES,), 1, CAP, dtype=jnp.int32)
    reach = max(1, CAP // 4)
    first = spread_lengths(key_first, LEN // 2 - offset, NSEG // 2, reach)
    second = spread_lengths(key_second, LEN // 2 + offset - CAP, NSEG // 2 - 1, reach)
    middle = jnp.full((SEQUENCES, 1), CAP, dtype=jnp.int32)
    return jnp.concatenate([first, middle, second], axis=1).astype(jnp.int32)


def block_levels(own_key, extent, pieces, least, largest):
    level, own = 1.0, jax.random.fold_in(own_key, 6)
    for position, blocks in pieces:
        draws = jnp.exp(jax.random.uniform(jax.random.fold_in(own, position), (blocks,), jnp.float32, least / len(pieces), largest / len(pieces)))
        level = level * jnp.repeat(draws, extent[position] // blocks).reshape([-1 if axis == position else 1 for axis in range(len(extent))])
    return level


def gaussian(rng, extent, deviation, most, shards=(), kind=jnp.bfloat16):
    values = deviation * jax.random.normal(rng, extent, jnp.float32)
    if shards:
        values = values * block_levels(rng, extent, shards, -0.22, 0.18)
    return jnp.clip(values, -most, most).astype(kind)


def setup_inputs(seed: int = 0) -> dict:
    key_of = jax.random.split(jax.random.key(seed), 17)
    tokens = gaussian(key_of[0], (TOKENS, D), 1.0, 6.0, ((0, 128),))
    lengths = draw_lengths(jax.random.fold_in(key_of[16], 71), 0)
    ln1_gain = jnp.clip(1.0 + 0.1 * jax.random.normal(key_of[2], (D,), jnp.float32), 0.5, 1.5).astype(jnp.bfloat16)
    ln1_bias = gaussian(key_of[3], (D,), 0.5, 3.0, ((0, 64),))
    w_qkv = gaussian(key_of[4], (D, 3 * D), D ** -0.5, 0.21875, ((0, 64),))
    q_bias = gaussian(key_of[5], (D,), 0.5, 3.0, ((0, 64),))
    v_bias = gaussian(key_of[6], (D,), 0.5, 3.0, ((0, 64),))
    w_out = gaussian(key_of[7], (D, D), (D // 32) ** -0.5, 1.25, ((0, 64),))
    out_bias = gaussian(key_of[8], (D,), 0.5, 3.0, ((0, 64),))
    ln2_gain = jnp.clip(1.0 + 0.1 * jax.random.normal(key_of[9], (D,), jnp.float32), 0.5, 1.5).astype(jnp.bfloat16)
    ln2_bias = gaussian(key_of[10], (D,), 0.5, 3.0, ((0, 64),))
    w_in = gaussian(key_of[11], (D, FF), D ** -0.5, 0.21875, ((0, 64),))
    in_bias = gaussian(key_of[12], (FF,), 0.5, 3.0, ((0, 64),))
    w_back = gaussian(key_of[13], (FF, D), (FF // 2) ** -0.5, 0.15625, ((0, 64),))
    back_bias = gaussian(key_of[14], (D,), 0.5, 3.0, ((0, 64),))
    cotangent = gaussian(key_of[15], (TOKENS, D), 1.0, 6.0, ((0, 128),))
    return {"tokens": tokens, "lengths": lengths, "ln1_gain": ln1_gain, "ln1_bias": ln1_bias, "w_qkv": w_qkv, "q_bias": q_bias, "v_bias": v_bias, "w_out": w_out, "out_bias": out_bias, "ln2_gain": ln2_gain, "ln2_bias": ln2_bias, "w_in": w_in, "in_bias": in_bias, "w_back": w_back, "back_bias": back_bias, "cotangent": cotangent}


@jax.custom_vjp
def low(v):
    return lax.optimization_barrier(v.astype(jnp.bfloat16)).astype(jnp.float32)

@jax.custom_vjp
def low_back(v):
    return v

def low_keep(v):
    return (low(v), None)

def low_pass(kept, grad):
    return (grad,)

def back_keep(v):
    return (v, None)

def back_low(kept, grad):
    return (low(grad),)
low.defvjp(low_keep, low_pass)
low_back.defvjp(back_keep, back_low)
HIGHEST = lax.Precision.HIGHEST

def layer_norm(values, gain, shift):
    centre = values - lax.optimization_barrier(jnp.mean(values, axis=-1, keepdims=True))
    scale = lax.rsqrt(lax.optimization_barrier(jnp.mean(centre * centre, axis=-1, keepdims=True)) + 1e-05)
    return centre * scale * gain + shift

def block(values, captions, weights):
    g1, s1, wqkv, qb, vb, wo, ob, g2, s2, w1, bi1, w2, b2 = weights
    batch, length, width = values.shape
    act1 = low(layer_norm(values, g1, s1))
    proj = jnp.einsum('bti,ij->btj', act1, wqkv, precision=HIGHEST)
    proj = proj + jnp.concatenate([qb, jnp.zeros_like(qb), vb])
    proj = low(low_back(proj))
    query = proj[..., :width].reshape(batch, length, HEADS, HEAD_DIM)
    keys = proj[..., width:2 * width].reshape(batch, length, HEADS, HEAD_DIM)
    vals = proj[..., 2 * width:].reshape(batch, length, HEADS, HEAD_DIM)
    scores = jnp.einsum('bqhd,bkhd->bhqk', query, keys, precision=HIGHEST) * HEAD_DIM ** (-0.5)
    scores = low_back(scores)
    allowed = captions[:, None, :, None] == captions[:, None, None, :]
    scores = jnp.where(allowed, scores, -1e+30)
    top = lax.optimization_barrier(jnp.max(scores, axis=-1, keepdims=True))
    expo = jnp.exp(scores - top)
    probs = expo / lax.optimization_barrier(jnp.sum(expo, axis=-1, keepdims=True))
    mixed = jnp.einsum('bhqk,bkhd->bqhd', low(probs), vals, precision=HIGHEST).reshape(batch, length, width)
    mixed = low(low_back(mixed))
    branch = jnp.einsum('bti,ij->btj', mixed, wo, precision=HIGHEST) + ob
    middle = values + low_back(branch)
    act2 = low(layer_norm(middle, g2, s2))
    pre = low_back(jnp.einsum('bti,ij->btj', act2, w1, precision=HIGHEST) + bi1)
    gact = low(jax.nn.gelu(pre, approximate=False))
    branch2 = jnp.einsum('bti,ij->btj', gact, w2, precision=HIGHEST) + b2
    return middle + low_back(branch2)

def reference(tokens, lengths, ln1_gain, ln1_bias, w_qkv, q_bias, v_bias, w_out, out_bias, ln2_gain, ln2_bias, w_in, in_bias, w_back, back_bias, cotangent):
    width = tokens.shape[1]
    count = tokens.shape[0] // LEN
    group = math.gcd(count, 8)
    ends = jnp.cumsum(lengths, axis=1)
    place = jnp.arange(LEN, dtype=jnp.int32)
    captions = lax.optimization_barrier(jnp.sum((ends[:, None, :] <= place[None, :, None]).astype(jnp.int32), axis=-1))
    weights = tuple((w.astype(jnp.float32) for w in (ln1_gain, ln1_bias, w_qkv, q_bias, v_bias, w_out, out_bias, ln2_gain, ln2_bias, w_in, in_bias, w_back, back_bias)))
    values = tokens.astype(jnp.float32).reshape(count, LEN, width)
    grads_in = cotangent.astype(jnp.float32).reshape(count, LEN, width)

    def forward(inputs, params):

        def one(item):
            return block(item[0], item[1], params)
        step = jax.checkpoint(one)
        result = lax.map(step, (inputs.reshape(count // group, group, LEN, width), captions.reshape(count // group, group, LEN)))
        return result.reshape(count, LEN, width)
    output, pull = jax.vjp(forward, values, weights)
    d_values, d_w = pull(grads_in)
    return (output.reshape(-1, width).astype(jnp.bfloat16), d_values.reshape(-1, width), d_w[0], d_w[1], d_w[2], d_w[3], d_w[4], d_w[5], d_w[6], d_w[7], d_w[8], d_w[9], d_w[10], d_w[11], d_w[12])
```

```python
import functools
import itertools

import jax
import jax.numpy as jnp
from jax import lax
from jax.experimental import pallas as pl
from jax.experimental.pallas import tpu as pltpu
from jax.sharding import PartitionSpec as P

HEADS = 12
HEAD_DIM = 64
LEN = 512
WIDTH = 768
FF = 3072
AXES = ("dp", "fsdp")
F32 = jnp.float32
BF16 = jnp.bfloat16

EVERY = [(y, z, x, c) for y in range(4) for z in range(4) for x in range(4) for c in range(2)]


def index_of(y, z, x, c):
    y, z, x, c = y % 4, z % 4, x % 4, c % 2
    return (y // 2) * 64 + (((y % 2) * 4 + z) * 4 + x) * 2 + c


def moves(by, by_second=None):
    steps = (by, by if by_second is None else by_second)
    return [(index_of(*at), index_of(*(a + s for a, s in zip(at, steps[at[3]])))) for at in EVERY]


Y_RING = moves((1, 0, 0, 0), (-1, 0, 0, 0))
Z_RING = moves((0, 1, 0, 0), (0, -1, 0, 0))
X_RING = moves((0, 0, 1, 0), (0, 0, -1, 0))
Z_BY = {k: moves((0, k, 0, 0)) for k in (1, 2, 3)}
CORES = moves((0, 0, 0, 1))
REPLICA = moves((2, 0, 0, 0))
SPREAD = [
    [
        (index_of(y, z, x, c), index_of(y, z, 2 * (x % 2) + c - k, x // 2))
        for y, z, x, c in EVERY
    ]
    for k in range(4)
]
COLLECT = [[(b, a) for a, b in pairs] for pairs in SPREAD]


def send(array, pairs):
    return lax.ppermute(array, AXES, pairs)


def here():
    at = lax.axis_index("fsdp")
    core, x, z, y = at % 2, (at // 2) % 4, (at // 8) % 4, at // 32
    return y, z, x, core, 1 - 2 * core


def pick(array, at, axis=0):
    return lax.dynamic_index_in_dim(array, at, axis, keepdims=False)


def half_block(shard):
    x = here()[2]
    got = [send(shard, SPREAD[k]) for k in range(4)]
    ring = jnp.stack(got + got[:3])
    return lax.dynamic_slice_in_dim(ring, (4 - x) % 4, 4, 0).reshape(48, shard.shape[1])


def place_pieces(pieces, slots, columns):
    lead = [p.shape[:-2] for p in pieces]
    parts = [
        (n, at) for n, dims in enumerate(lead) for at in itertools.product(*(range(d) for d in dims))
    ]
    count = len(parts)
    starts = [sum(columns[:i]) for i in range(len(columns))]

    def kernel(slots_ref, *refs):
        ins, outs, sem = refs[: len(pieces)], refs[len(pieces) : -1], refs[-1]
        copies = []
        for i, (n, at) in enumerate(parts):
            for o, (start, size) in enumerate(zip(starts, columns)):
                copies.append(
                    pltpu.make_async_copy(
                        ins[n].at[(*at, slice(None), pl.ds(start, size))],
                        outs[o].at[slots_ref[i]],
                        sem.at[i * len(columns) + o],
                    )
                )
        for copy in copies:
            copy.start()
        for copy in copies:
            copy.wait()

    made = pl.pallas_call(
        kernel,
        out_shape=[jax.ShapeDtypeStruct((count, 48, n), BF16) for n in columns],
        in_specs=[pl.BlockSpec(memory_space=pltpu.SMEM)]
        + [pl.BlockSpec(memory_space=pl.ANY)] * len(pieces),
        out_specs=[pl.BlockSpec(memory_space=pl.ANY)] * len(columns),
        scratch_shapes=[pltpu.SemaphoreType.DMA((count * len(columns),))],
        name="place_pieces",
    )(slots, *pieces)
    return [m.reshape(count * 48, n) for m, n in zip(made, columns)]


def gather_rows(shard, columns):
    y, z, x, core, sign = here()
    own, side = [half_block(shard)], []
    for t in range(4):
        if t < 3:
            own.append(send(own[t], Z_RING))
        side.append(send(own[t], Y_RING))
    mine = own + side
    other = [send(p, CORES) for p in mine]
    slots = []
    for half, way in ((core, sign), (1 - core, -sign)):
        for row in (y, 1 - y):
            for t in range(4):
                slots.append((row * 4 + (z - way * t) % 4) * 2 + half)
    return place_pieces(mine + other, jnp.stack(slots), columns)


def gather_back(shard):
    y, z, x, core, sign = here()
    pair = jnp.stack([shard, send(shard, Y_RING)])
    quad = jnp.stack([pair] + [send(pair, Z_BY[k]) for k in (1, 2, 3)])
    mine = [quad]
    for t in range(3):
        mine.append(send(mine[t], X_RING))
    other = [send(p, CORES) for p in mine]
    slots = []
    for half, way in ((core, sign), (1 - core, -sign)):
        for t in range(4):
            for k in range(4):
                for row in (y, 1 - y):
                    at = (row * 4 + (z - k) % 4) * 4 + (x - way * t) % 4
                    slots.append(at * 2 + half)
    return place_pieces(mine + other, jnp.stack(slots), [shard.shape[1]])[0]


def over_replicas(share):
    share = lax.reduce_precision(share, 8, 7)
    return share + send(share.astype(BF16), REPLICA).astype(F32)


def reduce_rows(grad):
    y, z, x, core, sign = here()
    n = grad.shape[1]
    halves = grad.reshape(8, 2, 48, n)
    got = send(pick(halves, 1 - core, 1).astype(BF16), CORES)
    kept = (pick(halves, core, 1) + got.astype(F32)).reshape(2, 4, 48, n)
    mine, theirs = pick(kept, y), pick(kept, 1 - y)
    passed = None
    for t in range(1, 5):
        at = (z - sign * t) % 4
        total = pick(mine, at) + send(pick(theirs, at).astype(BF16), Y_RING).astype(F32)
        if passed is not None:
            total = total + passed.astype(F32)
        if t < 4:
            passed = send(total.astype(BF16), Z_RING)
    pieces = total.astype(BF16).reshape(4, 12, n)
    share = sum(send(pick(pieces, (x + k) % 4), COLLECT[k]).astype(F32) for k in range(4))
    return over_replicas(share)


def reduce_back(grad):
    y, z, x, core, sign = here()
    n = grad.shape[1]
    parts = grad.reshape(2, 4, 4, 2, 48, n)
    got = send(pick(parts, 1 - core, 3).astype(BF16), CORES)
    kept = pick(parts, core, 3) + got.astype(F32)
    passed = None
    for t in range(1, 5):
        total = pick(kept, (x - sign * t) % 4, 2)
        if passed is not None:
            total = total + passed.astype(F32)
        if t < 4:
            passed = send(total.astype(BF16), X_RING)
    low = total.astype(BF16)
    total = pick(total, z, 1) + sum(
        send(pick(low, (z + k) % 4, 1), Z_BY[k]).astype(F32) for k in (1, 2, 3)
    )
    share = pick(total, y) + send(pick(total, 1 - y).astype(BF16), Y_RING).astype(F32)
    return over_replicas(share)


def layer_norm(values, gain, shift):
    centre = values - jnp.mean(values, axis=-1, keepdims=True)
    scale = lax.rsqrt(jnp.mean(centre * centre, axis=-1, keepdims=True) + 1e-05)
    normed = centre * scale
    return (normed * gain + shift, normed, scale)


def norm_back(d_out, normed, scale, gain):
    gain_grad = jnp.sum(d_out * normed, axis=0)
    shift_grad = jnp.sum(d_out, axis=0)
    expand = d_out * gain
    d_in = scale * (
        expand
        - jnp.mean(expand, axis=-1, keepdims=True)
        - normed * jnp.mean(expand * normed, axis=-1, keepdims=True)
    )
    return (d_in, gain_grad, shift_grad)


def dot(a, b, dims):
    return lax.dot_general(a, b, (dims, ((), ())), preferred_element_type=F32)


def attention_probs(query, keys, allowed, logsum):
    scores = jnp.einsum("qhd,khd->hqk", query, keys, preferred_element_type=F32) * HEAD_DIM ** (-0.5)
    scores = jnp.where(allowed[None], scores, -1e30)
    if logsum is None:
        top = jnp.max(scores, axis=-1, keepdims=True)
        logsum = top + jnp.log(jnp.sum(jnp.exp(scores - top), axis=-1, keepdims=True))
    return (jnp.exp(scores - logsum), logsum)


def shards(tokens, lengths, g1, s1, wqkv, qb, vb, wo, ob, g2, s2, w1, bi1, w2, b2, cotangent):
    device = lax.axis_index("dp") * 64 + lax.axis_index("fsdp")
    ends = jnp.cumsum(lax.dynamic_index_in_dim(lengths, device, 0, keepdims=False))
    ids = jnp.sum((ends[None, :] <= jnp.arange(LEN, dtype=jnp.int32)[:, None]).astype(jnp.int32), -1)
    allowed = ids[:, None] == ids[None, :]
    vectors = jnp.stack([g1, s1, qb, vb, ob, g2, s2, b2], axis=1)
    vectors = jnp.concatenate([vectors, bi1.reshape(12, 4)], axis=1)
    vectors = jnp.pad(vectors, ((0, 0), (0, 128 - 12)))
    wqkv, vectors = gather_rows(jnp.concatenate([wqkv, vectors], axis=1), [3 * WIDTH, 128])
    wo, w1 = gather_rows(jnp.concatenate([wo, w1], axis=1), [WIDTH, FF])
    w2 = gather_back(w2)
    rows = vectors.T.astype(F32)
    g1, s1, qb, vb, ob, g2, s2, b2 = (rows[i] for i in range(8))
    bi1 = vectors[:, 8:12].reshape(FF).astype(F32)

    values = tokens.astype(F32)
    normed_out, normed1, scale1 = layer_norm(values, g1, s1)
    act1 = normed_out.astype(BF16)
    bias = jnp.concatenate([qb, jnp.zeros((WIDTH,), F32), vb])
    proj = (dot(act1, wqkv, ((1,), (0,))) + bias).astype(BF16)
    query, keys, vals = (
        proj[:, i * WIDTH : (i + 1) * WIDTH].reshape(LEN, HEADS, HEAD_DIM) for i in range(3)
    )
    probs, logsum = attention_probs(query, keys, allowed, None)
    mixed = (
        jnp.einsum("hqk,khd->qhd", probs.astype(BF16), vals, preferred_element_type=F32)
        .astype(BF16)
        .reshape(LEN, WIDTH)
    )
    middle = values + dot(mixed, wo, ((1,), (0,))) + ob
    normed_out2, normed2, scale2 = layer_norm(middle, g2, s2)
    act2 = normed_out2.astype(BF16)
    pre = dot(act2, w1, ((1,), (0,))) + bi1
    gact = jax.nn.gelu(pre, approximate=False).astype(BF16)
    result = middle + dot(gact, w2, ((1,), (0,))) + b2

    d_up = cotangent
    grad_w2 = dot(gact, d_up, ((0,), (0,)))
    back_share = reduce_back(grad_w2)
    grad_b2 = jnp.sum(d_up.astype(F32), axis=0)
    d_gact = dot(d_up, w2, ((1,), (1,)))
    d_pre = jax.vjp(lambda a: jax.nn.gelu(a, approximate=False), pre)[1](d_gact)[0].astype(BF16)
    grad_bi1 = jnp.sum(d_pre.astype(F32), axis=0)
    grad_w1 = dot(act2, d_pre, ((0,), (0,)))
    in_share = reduce_rows(grad_w1)
    d_act2 = dot(d_pre, w1, ((1,), (1,)))
    d_mid_ln, grad_g2, grad_s2 = norm_back(d_act2, normed2, scale2, g2)
    d_middle = cotangent.astype(F32) + d_mid_ln
    d_branch = d_middle.astype(BF16)
    grad_wo = dot(mixed, d_branch, ((0,), (0,)))
    grad_ob = jnp.sum(d_branch.astype(F32), axis=0)
    d_mixed = dot(d_branch, wo, ((1,), (1,))).astype(BF16).reshape(LEN, HEADS, HEAD_DIM)

    probs, unused = attention_probs(query, keys, allowed, logsum)
    d_probs = jnp.einsum("qhd,khd->hqk", d_mixed, vals, preferred_element_type=F32)
    d_scores = (probs * (d_probs - jnp.sum(probs * d_probs, axis=-1, keepdims=True))).astype(BF16)
    scale = HEAD_DIM ** (-0.5)
    d_query = jnp.einsum("hqk,khd->qhd", d_scores, keys, preferred_element_type=F32) * scale
    d_keys = jnp.einsum("hqk,qhd->khd", d_scores, query, preferred_element_type=F32) * scale
    d_vals = jnp.einsum("hqk,qhd->khd", probs.astype(BF16), d_mixed, preferred_element_type=F32)
    d_proj = jnp.concatenate(
        [d.reshape(LEN, WIDTH) for d in (d_query, d_keys, d_vals)], axis=1
    ).astype(BF16)
    grad_qb = jnp.sum(d_proj[:, :WIDTH].astype(F32), axis=0)
    grad_vb = jnp.sum(d_proj[:, 2 * WIDTH :].astype(F32), axis=0)
    grad_wqkv = dot(act1, d_proj, ((0,), (0,)))
    d_act1 = dot(d_proj, wqkv, ((1,), (1,)))
    d_in_ln, grad_g1, grad_s1 = norm_back(d_act1, normed1, scale1, g1)
    d_input = d_middle + d_in_ln
    columns = jnp.stack([grad_g1, grad_s1, grad_qb, grad_vb, grad_ob, grad_g2, grad_s2, grad_b2], 1)
    columns = jnp.concatenate([columns, grad_bi1.reshape(WIDTH, 4)], axis=1)
    columns = jnp.pad(columns, ((0, 0), (0, 128 - 12)))
    rest = reduce_rows(jnp.concatenate([grad_wqkv, grad_wo, columns], axis=1))
    own = rest[:, 4 * WIDTH :]
    return (
        result.astype(BF16),
        d_input,
        own[:, 0],
        own[:, 1],
        rest[:, : 3 * WIDTH],
        own[:, 2],
        own[:, 3],
        rest[:, 3 * WIDTH : 4 * WIDTH],
        own[:, 4],
        own[:, 5],
        own[:, 6],
        in_share,
        own[:, 8:12].reshape(48),
        back_share,
        own[:, 7],
    )


def solution(mesh):
    rows, whole = P(AXES, None), P()
    vector, matrix = P("fsdp"), P("fsdp", None)
    weights = (
        vector, vector, matrix, vector, vector, matrix, vector,
        vector, vector, matrix, vector, matrix, vector,
    )
    return jax.shard_map(
        shards,
        mesh=mesh,
        in_specs=(rows, whole, *weights, rows),
        out_specs=(rows, rows, *weights),
        check_vma=False,
    )
```

```python
import functools
import itertools

import jax
import jax.numpy as jnp
from jax import lax
from jax.experimental import pallas as pl
from jax.experimental.pallas import tpu as pltpu
from jax.sharding import PartitionSpec as P

HEADS = 12
HEAD_DIM = 64
LEN = 512
WIDTH = 768
FF = 3072
AXES = ("dp", "fsdp")
F32 = jnp.float32
BF16 = jnp.bfloat16

EVERY = [(y, z, x, c) for y in range(4) for z in range(4) for x in range(4) for c in range(2)]


def index_of(y, z, x, c):
    y, z, x, c = y % 4, z % 4, x % 4, c % 2
    return (y // 2) * 64 + (((y % 2) * 4 + z) * 4 + x) * 2 + c


def moves(by, by_second=None):
    steps = (by, by if by_second is None else by_second)
    return [(index_of(*at), index_of(*(a + s for a, s in zip(at, steps[at[3]])))) for at in EVERY]


Y_RING = moves((1, 0, 0, 0), (-1, 0, 0, 0))
Z_RING = moves((0, 1, 0, 0), (0, -1, 0, 0))
X_RING = moves((0, 0, 1, 0), (0, 0, -1, 0))
Z_BY = {k: moves((0, k, 0, 0)) for k in (1, 2, 3)}
CORES = moves((0, 0, 0, 1))
REPLICA = moves((2, 0, 0, 0))
SPREAD = [
    [
        (index_of(y, z, x, c), index_of(y, z, 2 * (x % 2) + c - k, x // 2))
        for y, z, x, c in EVERY
    ]
    for k in range(4)
]
COLLECT = [[(b, a) for a, b in pairs] for pairs in SPREAD]


def send(array, pairs):
    return lax.ppermute(array, AXES, pairs)


def here():
    at = lax.axis_index("fsdp")
    core, x, z, y = at % 2, (at // 2) % 4, (at // 8) % 4, at // 32
    return y, z, x, core, 1 - 2 * core


def pick(array, at, axis=0):
    return lax.dynamic_index_in_dim(array, at, axis, keepdims=False)


def half_block(shard):
    x = here()[2]
    got = [send(shard, SPREAD[k]) for k in range(4)]
    ring = jnp.stack(got + got[:3])
    return lax.dynamic_slice_in_dim(ring, (4 - x) % 4, 4, 0).reshape(48, shard.shape[1])


def row_slots():
    y, z, x, core, sign = here()
    slots = []
    for half, way in ((core, sign), (1 - core, -sign)):
        for row in (y, 1 - y):
            for t in range(4):
                slots.append((row * 4 + (z - way * t) % 4) * 2 + half)
    return jnp.stack(slots)


def gather_rows(shard):
    own, side = [half_block(shard)], []
    for t in range(4):
        if t < 3:
            own.append(send(own[t], Z_RING))
        side.append(send(own[t], Y_RING))
    mine = own + side
    return mine + [send(p, CORES) for p in mine]


def back_slots():
    y, z, x, core, sign = here()
    slots = []
    for half, way in ((core, sign), (1 - core, -sign)):
        for t in range(4):
            for k in range(4):
                for row in (y, 1 - y):
                    at = (row * 4 + (z - k) % 4) * 4 + (x - way * t) % 4
                    slots.append(at * 2 + half)
    return jnp.stack(slots)


def gather_back(shard):
    pair = jnp.stack([shard, send(shard, Y_RING)])
    quad = jnp.stack([pair] + [send(pair, Z_BY[k]) for k in (1, 2, 3)])
    mine = [quad]
    for t in range(3):
        mine.append(send(mine[t], X_RING))
    return mine + [send(p, CORES) for p in mine]


def over_replicas(share):
    share = lax.reduce_precision(share, 8, 7)
    return share + send(share.astype(BF16), REPLICA).astype(F32)


def reduce_rows(give, keep):
    y, z, x, core, sign = here()
    n = give.shape[1]
    got = send(give, CORES)
    kept = (keep.astype(F32) + got.astype(F32)).reshape(2, 4, 48, n)
    theirs = send(pick(kept, 1 - y).astype(BF16), Y_RING)
    total = pick(kept, y) + theirs.astype(F32)
    low = total.astype(BF16)
    total = pick(total, z) + sum(
        send(pick(low, (z + k) % 4), Z_BY[k]).astype(F32) for k in (1, 2, 3)
    )
    pieces = total.astype(BF16).reshape(4, 12, n)
    share = sum(send(pick(pieces, (x + k) % 4), COLLECT[k]).astype(F32) for k in range(4))
    return over_replicas(share)


def reduce_back(give, keep):
    y, z, x, core, sign = here()
    n = give.shape[1]
    got = send(give, CORES)
    kept = (keep.astype(F32) + got.astype(F32)).reshape(2, 4, 4, 48, n)
    passed = None
    for t in range(1, 5):
        total = pick(kept, (x - sign * t) % 4, 2)
        if passed is not None:
            total = total + passed.astype(F32)
        if t < 4:
            passed = send(total.astype(BF16), X_RING)
    low = total.astype(BF16)
    total = pick(total, z, 1) + sum(
        send(pick(low, (z + k) % 4, 1), Z_BY[k]).astype(F32) for k in (1, 2, 3)
    )
    share = pick(total, y) + send(pick(total, 1 - y).astype(BF16), Y_RING).astype(F32)
    return over_replicas(share)


HALF = 48
BLOCKS = WIDTH // (2 * HALF)
WINDOWS = (0, 64, 192, 256)
VMEM = pl.BlockSpec(memory_space=pltpu.VMEM)
SMEM = pl.BlockSpec(memory_space=pltpu.SMEM)
ANY = pl.BlockSpec(memory_space=pl.ANY)
PARAMS = pltpu.CompilerParams(vmem_limit_bytes=60 * 1024 * 1024)
CHUNK_ONE = 3 * WIDTH + 128
CHUNK_TWO = FF + WIDTH


def dot(a, b):
    return lax.dot_general(a, b, (((1,), (0,)), ((), ())), preferred_element_type=F32)


def dot_nt(a, b):
    return lax.dot_general(a, b, (((1,), (1,)), ((), ())), preferred_element_type=F32)


def dot_tn(a, b):
    return lax.dot_general(a, b, (((0,), (0,)), ((), ())), preferred_element_type=F32)


def normed(values):
    centre = values - jnp.mean(values, axis=-1, keepdims=True)
    scale = lax.rsqrt(jnp.mean(centre * centre, axis=-1, keepdims=True) + 1e-05)
    return centre * scale, scale


def norm_back(d_out, hat, scale, gain):
    expand = d_out * gain
    d_in = scale * (
        expand
        - jnp.mean(expand, axis=-1, keepdims=True)
        - hat * jnp.mean(expand * hat, axis=-1, keepdims=True)
    )
    gain_grad = jnp.sum(d_out * hat, axis=0, keepdims=True)
    return d_in, gain_grad, jnp.sum(d_out, axis=0, keepdims=True)


def rows_at(start, size, step=16):
    return pl.ds(pl.multiple_of(start, step), size)


def piece_copies(slots_ref, pieces, target, sems, first, columns=None):
    copies = []
    for ref in pieces:
        for at in itertools.product(*(range(d) for d in ref.shape[:-2])):
            n = len(copies)
            source = ref.at[at] if at else ref
            if columns is not None:
                source = source.at[:, pl.ds(*columns)]
            copies.append(
                pltpu.make_async_copy(
                    source, target.at[rows_at(slots_ref[n] * HALF, HALF)], sems.at[first + n]
                )
            )
    return copies


def split_rows(place_ref, natural, split):
    core = place_ref[0]
    for b in range(BLOCKS):
        for part, half in ((0, 1 - core), (1, core)):
            split[pl.ds(part * WIDTH // 2 + b * HALF, HALF), :] = natural[
                rows_at(b * 2 * HALF + half * HALF, HALF), :
            ]


def head_masks(rows):
    lane = lax.broadcasted_iota(jnp.int32, (rows, 128), 1)
    return lane < HEAD_DIM


def two_heads(pair):
    low = head_masks(pair.shape[0])
    zero = jnp.zeros_like(pair)
    return jnp.concatenate([jnp.where(low, pair, zero), jnp.where(low, zero, pair)], axis=0)


def fill_bias(place_ref, lengths_ref, bias):
    ends, total = [], jnp.int32(0)
    for k in range(16):
        total = total + lengths_ref[place_ref[1], k]
        ends.append(total)

    def ids(shape, dim, start):
        at = lax.broadcasted_iota(jnp.int32, shape, dim) + start
        return sum((at >= end).astype(jnp.int32) for end in ends)

    for i, start in enumerate(WINDOWS):
        queries, keys = ids((128, 1), 0, i * 128), ids((1, 256), 1, start)
        bias[i] = jnp.where(queries == keys, 0.0, -1e30).astype(F32)


def first_kernel(slots, place, lengths, tokens, *refs):
    pieces = refs[:16]
    proj, mixed, logsum, vec, rows, weight, bias, sems = refs[16:]
    copies = piece_copies(slots, pieces, weight, sems, 0, (0, 3 * WIDTH))
    copies += piece_copies(slots, pieces, vec, sems, 16, (3 * WIDTH, 128))
    for copy in copies:
        copy.start()
    fill_bias(place, lengths, bias)
    hat, unused = normed(tokens[...].astype(F32))
    for copy in copies:
        copy.wait()
    rows[...] = vec[...].astype(F32).T[:16]
    act = (hat * rows[0:1, :] + rows[1:2, :]).astype(BF16)

    def project(n, carry):
        at = rows_at(n * 256, 256, 256)
        kind = n // 3
        inside = rows_at((n - kind * 3) * 256, 256, 256)
        add = jnp.where(kind == 0, rows[2:3, inside], rows[3:4, inside])
        add = jnp.where(kind == 1, jnp.zeros_like(add), add)
        proj[:, at] = (dot(act, weight[:, at]) + add).astype(BF16)
        return carry

    lax.fori_loop(0, 9, project, 0)
    logsum[...] = jnp.zeros_like(logsum)
    lane = lax.broadcasted_iota(jnp.int32, (128, 128), 1)

    def attend(p, carry):
        col = p * 128
        for i, start in enumerate(WINDOWS):
            here_rows, keys_at = pl.ds(i * 128, 128), pl.ds(start, 256)
            query = two_heads(proj[here_rows, rows_at(col, 128, 128)] * HEAD_DIM ** (-0.5))
            keys = proj[keys_at, rows_at(WIDTH + col, 128, 128)]
            vals = two_heads(proj[keys_at, rows_at(2 * WIDTH + col, 128, 128)])
            scores = dot_nt(query, keys).reshape(2, 128, 256) + bias[i][None]
            top = jnp.max(scores, axis=-1, keepdims=True)
            expo = jnp.exp(scores - top)
            total = jnp.sum(expo, axis=-1, keepdims=True)
            probs = (expo * (1.0 / total)).astype(BF16)
            both = jnp.concatenate([probs[0], probs[1]], axis=1)
            mixed[here_rows, rows_at(col, 128, 128)] = dot(both, vals).astype(BF16)
            summed = top + jnp.log(total)
            old = logsum[here_rows, :]
            old = jnp.where(lane == 2 * p, summed[0], old)
            logsum[here_rows, :] = jnp.where(lane == 2 * p + 1, summed[1], old)
        return carry

    lax.fori_loop(0, HEADS // 2, attend, 0)


def run_first(slots, place, lengths, tokens, pieces):
    return pl.pallas_call(
        first_kernel,
        out_shape=[
            jax.ShapeDtypeStruct((LEN, 3 * WIDTH), BF16),
            jax.ShapeDtypeStruct((LEN, WIDTH), BF16),
            jax.ShapeDtypeStruct((LEN, 128), F32),
            jax.ShapeDtypeStruct((WIDTH, 128), BF16),
            jax.ShapeDtypeStruct((16, WIDTH), F32),
        ],
        in_specs=[SMEM, SMEM, SMEM, VMEM] + [ANY] * 16,
        out_specs=[VMEM] * 5,
        scratch_shapes=[
            pltpu.VMEM((WIDTH, 3 * WIDTH), BF16),
            pltpu.VMEM((4, 128, 256), F32),
            pltpu.SemaphoreType.DMA((32,)),
        ],
        compiler_params=PARAMS,
        cost_estimate=pl.CostEstimate(flops=8 * 10**9, bytes_accessed=10**7, transcendentals=0),
        name="attention_forward",
    )(slots, place, lengths, tokens, *pieces)


def gelu_pair(x):
    expo = jnp.exp(-0.5 * x * x)
    t = 1.0 / (1.0 + (0.3275911 * 0.5**0.5) * jnp.abs(x))
    poly = 0.5 * 1.061405429
    for c in (-1.453152027, 1.421413741, -0.284496736, 0.254829592):
        poly = poly * t + 0.5 * c
    tail = poly * t * expo
    phi = jnp.where(x >= 0, 1.0 - tail, tail)
    return x * phi, phi + x * (expo * 0.3989422804014327)


def middle_kernel(slots, back_slots, place, tokens, mixed, cot, rows, in_bias, *refs):
    pieces, backs = refs[:16], refs[16:24]
    hidden, g1, d_mixed, vector_grads, in_bias_grad = refs[24:29]
    give, keep, give_back, keep_back = refs[29:33]
    w_out, w_in, w_back, x1, hat, scale, act, act_t, acc, d_act, turned, flip, gact, d_pre, sems = refs[33:]
    j = pl.program_id(0)
    out_copies = piece_copies(slots, pieces, w_out, sems, 0, (FF, WIDTH))
    in_copies = piece_copies(slots, pieces, w_in, sems, 16, (0, FF))
    back_copies = piece_copies(back_slots, backs, w_back, sems, 32)

    @pl.when(j == 0)
    def _():
        for copy in out_copies + in_copies + back_copies:
            copy.start()
        for copy in out_copies:
            copy.wait()
        for n in range(3):
            at = pl.ds(n * 256, 256)
            x1[:, at] = tokens[:, at].astype(F32) + (dot(mixed[...], w_out[:, at]) + rows[4:5, at])
        hat[...], scale[...] = normed(x1[...])
        act[...] = (hat[...] * rows[5:6, :] + rows[6:7, :]).astype(BF16)
        turned[...] = act[...].T
        split_rows(place, turned, act_t)
        acc[...] = jnp.zeros_like(acc)
        d_act[...] = jnp.zeros_like(d_act)
        for copy in in_copies + back_copies:
            copy.wait()

    @pl.when(j < 4)
    def _():
        base = j * WIDTH

        def units(n, carry):
            local, at = rows_at(n * 256, 256, 256), rows_at(base + n * 256, 256, 256)
            pre = dot(act[...], w_in[:, at]) + in_bias[:, at]
            d_gact = dot_nt(cot[...], w_back[at, :])
            value, slope = gelu_pair(pre)
            gact[:, local] = value.astype(BF16)
            d_low = (d_gact * slope).astype(BF16)
            d_pre[:, local] = d_low
            in_bias_grad[:, at] = jnp.sum(d_low.astype(F32), axis=0, keepdims=True)
            turned[local, :] = value.astype(BF16).T
            return carry

        lax.fori_loop(0, 3, units, 0)
        here_rows = rows_at(base, WIDTH, 256)

        def sums(n, carry):
            at = rows_at(n * 256, 256, 256)
            acc[:, at] += dot(gact[...], w_back[here_rows, at])
            d_act[:, at] += dot_nt(d_pre[...], w_in[at, here_rows])
            made = dot(act_t[...], d_pre[:, at]).astype(BF16)
            give[:, at] = made[: WIDTH // 2]
            keep[:, at] = made[WIDTH // 2 :]
            return carry

        lax.fori_loop(0, 3, sums, 0)
        split_rows(place, turned, flip)

        def back_sums(n, carry):
            at = rows_at(n * 256, 256, 256)
            made = dot(flip[...], cot[:, at]).astype(BF16)
            give_back[:, at] = made[: WIDTH // 2]
            keep_back[:, at] = made[WIDTH // 2 :]
            return carry

        lax.fori_loop(0, 3, back_sums, 0)

    @pl.when(j == 4)
    def _():
        hidden[...] = (x1[...] + (acc[...] + rows[7:8, :])).astype(BF16)
        cot_wide = cot[...].astype(F32)
        d_in, gain_grad, bias_grad = norm_back(d_act[...], hat[...], scale[...], rows[5:6, :])
        total = cot_wide + d_in
        g1[...] = total
        low = total.astype(BF16)
        gact[...] = low
        turned[...] = mixed[...].T
        split_rows(place, turned, act_t)
        for n in range(3):
            at = pl.ds(n * 256, 256)
            made = dot(act_t[...], gact[:, at]).astype(BF16)
            give[:, at] = made[: WIDTH // 2]
            keep[:, at] = made[WIDTH // 2 :]
            d_mixed[:, at] = dot_nt(low, w_out[at, :]).astype(BF16)
        vector_grads[...] = jnp.concatenate(
            [
                jnp.sum(low.astype(F32), axis=0, keepdims=True),
                gain_grad,
                bias_grad,
                jnp.sum(cot_wide, axis=0, keepdims=True),
                jnp.zeros((4, WIDTH), F32),
            ],
            axis=0,
        )


def run_middle(slots, back_slots, place, tokens, mixed, cot, rows, in_bias, pieces, backs):
    full = lambda *shape: pl.BlockSpec(shape, lambda j: (0,) * len(shape))
    wide = pl.BlockSpec((WIDTH // 2, WIDTH), lambda j: (0, j))
    tall = pl.BlockSpec((WIDTH // 2, WIDTH), lambda j: (jnp.minimum(j, 3), 0))
    return pl.pallas_call(
        middle_kernel,
        grid=(5,),
        out_shape=[
            jax.ShapeDtypeStruct((LEN, WIDTH), BF16),
            jax.ShapeDtypeStruct((LEN, WIDTH), F32),
            jax.ShapeDtypeStruct((LEN, WIDTH), BF16),
            jax.ShapeDtypeStruct((8, WIDTH), F32),
            jax.ShapeDtypeStruct((1, FF), F32),
            jax.ShapeDtypeStruct((WIDTH // 2, CHUNK_TWO), BF16),
            jax.ShapeDtypeStruct((WIDTH // 2, CHUNK_TWO), BF16),
            jax.ShapeDtypeStruct((FF // 2, WIDTH), BF16),
            jax.ShapeDtypeStruct((FF // 2, WIDTH), BF16),
        ],
        in_specs=[SMEM, SMEM, SMEM]
        + [full(LEN, WIDTH)] * 3
        + [full(16, WIDTH), full(1, FF)]
        + [ANY] * 24,
        out_specs=[full(LEN, WIDTH)] * 3 + [full(8, WIDTH), full(1, FF), wide, wide, tall, tall],
        scratch_shapes=[
            pltpu.VMEM((WIDTH, WIDTH), BF16),
            pltpu.VMEM((WIDTH, FF), BF16),
            pltpu.VMEM((FF, WIDTH), BF16),
            pltpu.VMEM((LEN, WIDTH), F32),
            pltpu.VMEM((LEN, WIDTH), F32),
            pltpu.VMEM((LEN, 1), F32),
            pltpu.VMEM((LEN, WIDTH), BF16),
            pltpu.VMEM((WIDTH, LEN), BF16),
            pltpu.VMEM((LEN, WIDTH), F32),
            pltpu.VMEM((LEN, WIDTH), F32),
            pltpu.VMEM((WIDTH, LEN), BF16),
            pltpu.VMEM((WIDTH, LEN), BF16),
            pltpu.VMEM((LEN, WIDTH), BF16),
            pltpu.VMEM((LEN, WIDTH), BF16),
            pltpu.SemaphoreType.DMA((96,)),
        ],
        compiler_params=PARAMS,
        cost_estimate=pl.CostEstimate(flops=20 * 10**9, bytes_accessed=3 * 10**7, transcendentals=0),
        name="feed_forward",
    )(slots, back_slots, place, tokens, mixed, cot, rows, in_bias, *pieces, *backs)


def last_kernel(slots, place, lengths, tokens, proj, logsum, d_mixed, g1, rows, *refs):
    pieces = refs[:16]
    d_input, vector_grads, give, keep = refs[16:20]
    weight, bias, d_proj, d_keys, d_vals, d_act, turned, act_t, sems = refs[20:]
    copies = piece_copies(slots, pieces, weight, sems, 0, (0, 3 * WIDTH))
    for copy in copies:
        copy.start()
    fill_bias(place, lengths, bias)
    lane = lax.broadcasted_iota(jnp.int32, (128, 128), 1)

    def attend(p, carry):
        col = p * 128
        own = rows_at(col, 128, 128)
        d_keys[...] = jnp.zeros_like(d_keys)
        d_vals[...] = jnp.zeros_like(d_vals)
        for i, start in enumerate(WINDOWS):
            here_rows, keys_at = pl.ds(i * 128, 128), pl.ds(start, 256)
            query = two_heads(proj[here_rows, own] * HEAD_DIM ** (-0.5))
            keys = proj[keys_at, rows_at(WIDTH + col, 128, 128)]
            vals = proj[keys_at, rows_at(2 * WIDTH + col, 128, 128)]
            d_mix = two_heads(d_mixed[here_rows, own])
            sums = logsum[here_rows, :]
            summed = jnp.stack(
                [
                    jnp.sum(jnp.where(lane == 2 * p + n, sums, 0.0), axis=-1, keepdims=True)
                    for n in range(2)
                ]
            )
            scores = dot_nt(query, keys).reshape(2, 128, 256) + bias[i][None]
            probs = jnp.exp(scores - summed)
            d_probs = dot_nt(d_mix, vals).reshape(2, 128, 256)
            mean = jnp.sum(probs * d_probs, axis=-1, keepdims=True)
            d_scores = (probs * (d_probs - mean)).astype(BF16)
            both = jnp.concatenate([d_scores[0], d_scores[1]], axis=1)
            d_query = dot(both, two_heads(keys)) * HEAD_DIM ** (-0.5)
            d_proj[here_rows, own] = d_query.astype(BF16)
            d_keys[keys_at, :] += dot_tn(d_scores.reshape(256, 256), query)
            d_vals[keys_at, :] += dot_tn(probs.astype(BF16).reshape(256, 256), d_mix)
        d_proj[:, rows_at(WIDTH + col, 128, 128)] = d_keys[...].astype(BF16)
        d_proj[:, rows_at(2 * WIDTH + col, 128, 128)] = d_vals[...].astype(BF16)
        return carry

    lax.fori_loop(0, HEADS // 2, attend, 0)
    for copy in copies:
        copy.wait()
    hat, scale = normed(tokens[...].astype(F32))
    act = (hat * rows[0:1, :] + rows[1:2, :]).astype(BF16)
    turned[...] = act.T
    split_rows(place, turned, act_t)

    def back(n, carry):
        at = rows_at(n * 256, 256, 256)
        d_act[:, at] = dot_nt(d_proj[...], weight[at, :])
        return carry

    lax.fori_loop(0, 3, back, 0)
    d_in, gain_grad, bias_grad = norm_back(d_act[...], hat, scale, rows[0:1, :])
    d_input[...] = g1[...] + d_in

    def grads(n, carry):
        at = rows_at(n * 256, 256, 256)
        made = dot(act_t[...], d_proj[:, at]).astype(BF16)
        give[:, at] = made[: WIDTH // 2]
        keep[:, at] = made[WIDTH // 2 :]
        return carry

    lax.fori_loop(0, 9, grads, 0)
    vector_grads[...] = jnp.concatenate(
        [
            gain_grad,
            bias_grad,
            jnp.sum(d_proj[:, :WIDTH].astype(F32), axis=0, keepdims=True),
            jnp.sum(d_proj[:, 2 * WIDTH :].astype(F32), axis=0, keepdims=True),
            jnp.zeros((4, WIDTH), F32),
        ],
        axis=0,
    )


def run_last(slots, place, lengths, tokens, proj, logsum, d_mixed, g1, rows, pieces):
    return pl.pallas_call(
        last_kernel,
        out_shape=[
            jax.ShapeDtypeStruct((LEN, WIDTH), F32),
            jax.ShapeDtypeStruct((8, WIDTH), F32),
            jax.ShapeDtypeStruct((WIDTH // 2, 3 * WIDTH), BF16),
            jax.ShapeDtypeStruct((WIDTH // 2, 3 * WIDTH), BF16),
        ],
        in_specs=[SMEM, SMEM, SMEM] + [VMEM] * 6 + [ANY] * 16,
        out_specs=[VMEM] * 4,
        scratch_shapes=[
            pltpu.VMEM((WIDTH, 3 * WIDTH), BF16),
            pltpu.VMEM((4, 128, 256), F32),
            pltpu.VMEM((LEN, 3 * WIDTH), BF16),
            pltpu.VMEM((LEN, 128), F32),
            pltpu.VMEM((LEN, 128), F32),
            pltpu.VMEM((LEN, WIDTH), F32),
            pltpu.VMEM((WIDTH, LEN), BF16),
            pltpu.VMEM((WIDTH, LEN), BF16),
            pltpu.SemaphoreType.DMA((16,)),
        ],
        compiler_params=PARAMS,
        cost_estimate=pl.CostEstimate(flops=12 * 10**9, bytes_accessed=10**7, transcendentals=0),
        name="attention_backward",
    )(slots, place, lengths, tokens, proj, logsum, d_mixed, g1, rows, *pieces)


def shards(tokens, lengths, g1, s1, wqkv, qb, vb, wo, ob, g2, s2, w1, bi1, w2, b2, cotangent):
    y, z, x, core, sign = here()
    place = jnp.stack([core, lax.axis_index("dp") * 64 + lax.axis_index("fsdp")])
    vectors = jnp.stack([g1, s1, qb, vb, ob, g2, s2, b2], axis=1)
    vectors = jnp.concatenate([vectors, bi1.reshape(12, 4)], axis=1)
    vectors = jnp.pad(vectors, ((0, 0), (0, 128 - 12)))
    pieces_one = gather_rows(jnp.concatenate([wqkv, vectors], axis=1))
    pieces_two = gather_rows(jnp.concatenate([w1, wo], axis=1))
    backs = gather_back(w2)
    slots = row_slots()

    proj, mixed, logsum, vec, rows = run_first(slots, place, lengths, tokens, pieces_one)
    in_bias = vec[:, 8:12].reshape(1, FF).astype(F32)
    hidden, d_middle, d_mixed, grads_two, in_bias_grad, give, keep, give_back, keep_back = run_middle(
        slots, back_slots(), place, tokens, mixed, cotangent, rows, in_bias, pieces_two, backs
    )
    back_share = reduce_back(give_back, keep_back)
    share_two = reduce_rows(give, keep)
    d_input, grads_one, give, keep = run_last(
        slots, place, lengths, tokens, proj, logsum, d_mixed, d_middle, rows, pieces_one
    )
    columns = jnp.concatenate([grads_one[:4], grads_two[:4]], axis=0).T
    columns = jnp.concatenate([columns, in_bias_grad.reshape(WIDTH, 4)], axis=1)
    columns = jnp.pad(columns, ((0, 0), (0, 128 - 12))).astype(BF16).reshape(8, 2, 48, 128)
    give = jnp.concatenate([give, pick(columns, 1 - core, 1).reshape(WIDTH // 2, 128)], axis=1)
    keep = jnp.concatenate([keep, pick(columns, core, 1).reshape(WIDTH // 2, 128)], axis=1)
    share_one = reduce_rows(give, keep)
    own = share_one[:, 3 * WIDTH :]
    return (
        hidden,
        d_input,
        own[:, 0],
        own[:, 1],
        share_one[:, : 3 * WIDTH],
        own[:, 2],
        own[:, 3],
        share_two[:, FF:],
        own[:, 4],
        own[:, 5],
        own[:, 6],
        share_two[:, :FF],
        own[:, 8:12].reshape(48),
        back_share,
        own[:, 7],
    )


def solution(mesh):
    rows, whole = P(AXES, None), P()
    vector, matrix = P("fsdp"), P("fsdp", None)
    weights = (
        vector, vector, matrix, vector, vector, matrix, vector,
        vector, vector, matrix, vector, matrix, vector,
    )
    return jax.shard_map(
        shards,
        mesh=mesh,
        in_specs=(rows, whole, *weights, rows),
        out_specs=(rows, rows, *weights),
        check_vma=False,
    )
```

```python
import functools
import itertools

import jax
import jax.numpy as jnp
from jax import lax
from jax.experimental import pallas as pl
from jax.experimental.pallas import tpu as pltpu
from jax.sharding import PartitionSpec as P

HEADS = 12
HEAD_DIM = 64
LEN = 512
WIDTH = 768
FF = 3072
AXES = ("dp", "fsdp")
F32 = jnp.float32
BF16 = jnp.bfloat16

EVERY = [(y, z, x, c) for y in range(4) for z in range(4) for x in range(4) for c in range(2)]


def index_of(y, z, x, c):
    y, z, x, c = y % 4, z % 4, x % 4, c % 2
    return (y // 2) * 64 + (((y % 2) * 4 + z) * 4 + x) * 2 + c


def moves(by, by_second=None):
    steps = (by, by if by_second is None else by_second)
    return [(index_of(*at), index_of(*(a + s for a, s in zip(at, steps[at[3]])))) for at in EVERY]


Y_RING = moves((1, 0, 0, 0), (-1, 0, 0, 0))
Z_RING = moves((0, 1, 0, 0), (0, -1, 0, 0))
X_RING = moves((0, 0, 1, 0), (0, 0, -1, 0))
Z_BY = {k: moves((0, k, 0, 0)) for k in (1, 2, 3)}
CORES = moves((0, 0, 0, 1))
REPLICA = moves((2, 0, 0, 0))
SPREAD = [
    [
        (index_of(y, z, x, c), index_of(y, z, 2 * (x % 2) + c - k, x // 2))
        for y, z, x, c in EVERY
    ]
    for k in range(4)
]
COLLECT = [[(b, a) for a, b in pairs] for pairs in SPREAD]


def send(array, pairs):
    return lax.ppermute(array, AXES, pairs)


def here():
    at = lax.axis_index("fsdp")
    core, x, z, y = at % 2, (at // 2) % 4, (at // 8) % 4, at // 32
    return y, z, x, core, 1 - 2 * core


def pick(array, at, axis=0):
    return lax.dynamic_index_in_dim(array, at, axis, keepdims=False)


YZ = [(row, z) for row in range(2) for z in range(4)]
YZ_BY = {(row, z): moves((row, z, 0, 0), (-row, z, 0, 0)) for row, z in YZ}
X_BY = {k: moves((0, 0, k, 0)) for k in (1, 2, 3)}


def half_block(shard):
    x = here()[2]
    got = [send(shard, SPREAD[k]) for k in range(4)]
    ring = jnp.stack(got + got[:3])
    return lax.dynamic_slice_in_dim(ring, (4 - x) % 4, 4, 0).reshape(48, shard.shape[1])


def row_slots():
    y, z, x, core, sign = here()
    slots = []
    for half, way in ((core, sign), (1 - core, -sign)):
        for row in (y, 1 - y):
            for t in range(4):
                slots.append((row * 4 + (z - way * t) % 4) * 2 + half)
    return jnp.stack(slots)


def back_slots():
    y, z, x, core, sign = here()
    slots = []
    for half, way in ((core, sign), (1 - core, -sign)):
        for t in range(4):
            for k in range(4):
                for row in (y, 1 - y):
                    at = (row * 4 + (z - k) % 4) * 4 + (x - way * t) % 4
                    slots.append(at * 2 + half)
    return jnp.stack(slots)


def all_done(*arrays):
    return lax.optimization_barrier(arrays)


def gather(shard, back):
    pair = jnp.stack([back, send(back, Y_RING)])
    own = [half_block(shard)]
    quads = [jnp.stack([pair] + [send(pair, Z_BY[k]) for k in (1, 2, 3)])]
    side, over_own, over_side, over_quads = [], [], [], []
    for t in range(4):
        now = [own[t], *side[t - 1 : t]]
        if t:
            now.append(quads[t - 1])
        now = all_done(*now)
        if t < 3:
            own.append(send(now[0], Z_RING))
        side.append(send(now[0], Y_RING))
        if t:
            quads.append(send(now[2], X_RING))
            over_side.append(send(now[1], CORES))
        over_own.append(send(now[0], CORES))
        done = [own[-1], side[-1], quads[-1]]
        if t:
            done.append(over_side[-1])
        done.append(over_own[-1])
        done = all_done(*done)
        own[-1], side[-1], quads[-1] = done[:3]
        if t:
            over_side[-1] = done[3]
        over_own[-1] = done[-1]
    over_side.append(send(side[3], CORES))
    over_quads = [send(q, CORES) for q in quads]
    return own + side + over_own + over_side, quads + over_quads


def over_replicas(share):
    share = lax.reduce_precision(share, 8, 7)
    return share + send(share.astype(BF16), REPLICA).astype(F32)


def core_sum(give, keep):
    got = send(give, CORES)
    return keep.astype(F32) + got.astype(F32)


def to_owner(total):
    x = here()[2]
    pieces = total.astype(BF16).reshape(4, 12, total.shape[1])
    return sum(send(pick(pieces, (x + k) % 4), COLLECT[k]).astype(F32) for k in range(4))


HALF = 48
BLOCKS = WIDTH // (2 * HALF)
WINDOWS = (0, 64, 192, 256)
VMEM = pl.BlockSpec(memory_space=pltpu.VMEM)
SMEM = pl.BlockSpec(memory_space=pltpu.SMEM)
ANY = pl.BlockSpec(memory_space=pl.ANY)
PARAMS = pltpu.CompilerParams(vmem_limit_bytes=60 * 1024 * 1024)
COST = pl.CostEstimate(flops=10**6, bytes_accessed=10**5, transcendentals=0)
CHUNK_ONE = 3 * WIDTH + 128
CHUNK_TWO = FF + WIDTH


def dot(a, b):
    return lax.dot_general(a, b, (((1,), (0,)), ((), ())), preferred_element_type=F32)


def dot_nt(a, b):
    return lax.dot_general(a, b, (((1,), (1,)), ((), ())), preferred_element_type=F32)


def dot_tn(a, b):
    return lax.dot_general(a, b, (((0,), (0,)), ((), ())), preferred_element_type=F32)


def normed(values):
    centre = values - jnp.mean(values, axis=-1, keepdims=True)
    scale = lax.rsqrt(jnp.mean(centre * centre, axis=-1, keepdims=True) + 1e-05)
    return centre * scale, scale


def norm_back(d_out, hat, scale, gain):
    expand = d_out * gain
    d_in = scale * (
        expand
        - jnp.mean(expand, axis=-1, keepdims=True)
        - hat * jnp.mean(expand * hat, axis=-1, keepdims=True)
    )
    gain_grad = jnp.sum(d_out * hat, axis=0, keepdims=True)
    return d_in, gain_grad, jnp.sum(d_out, axis=0, keepdims=True)


def rows_at(start, size, step=16):
    return pl.ds(pl.multiple_of(start, step), size)


def piece_copies(slots_ref, pieces, target, sems, first, columns=None):
    copies = []
    for ref in pieces:
        for at in itertools.product(*(range(d) for d in ref.shape[:-2])):
            n = len(copies)
            source = ref.at[at] if at else ref
            if columns is not None:
                source = source.at[:, pl.ds(*columns)]
            copies.append(
                pltpu.make_async_copy(
                    source, target.at[rows_at(slots_ref[n] * HALF, HALF)], sems.at[first + n]
                )
            )
    return copies


def split_rows(place_ref, natural, split):
    core = place_ref[0]
    for b in range(BLOCKS):
        for part, half in ((0, 1 - core), (1, core)):
            split[pl.ds(part * WIDTH // 2 + b * HALF, HALF), :] = natural[
                rows_at(b * 2 * HALF + half * HALF, HALF), :
            ]


def head_masks(rows):
    lane = lax.broadcasted_iota(jnp.int32, (rows, 128), 1)
    return lane < HEAD_DIM


def two_heads(pair):
    low = head_masks(pair.shape[0])
    zero = jnp.zeros_like(pair)
    return jnp.concatenate([jnp.where(low, pair, zero), jnp.where(low, zero, pair)], axis=0)


def fill_bias(place_ref, lengths_ref, bias):
    ends, total = [], jnp.int32(0)
    for k in range(16):
        total = total + lengths_ref[place_ref[1], k]
        ends.append(total)

    def ids(shape, dim, start):
        at = lax.broadcasted_iota(jnp.int32, shape, dim) + start
        return sum((at >= end).astype(jnp.int32) for end in ends)

    for i, start in enumerate(WINDOWS):
        queries, keys = ids((128, 1), 0, i * 128), ids((1, 256), 1, start)
        bias[i] = jnp.where(queries == keys, 0.0, -1e30).astype(F32)


def pack_kernel(*refs):
    vectors, in_bias, w_qkv, w_in, w_out, out, made = refs[:8], *refs[8:]
    rows = w_qkv.shape[0]
    same = lax.broadcasted_iota(jnp.int32, (rows, rows), 0) == lax.broadcasted_iota(
        jnp.int32, (rows, rows), 1
    )
    lane = lax.broadcasted_iota(jnp.int32, (rows, 128), 1)
    total = jnp.zeros((rows, 128), F32)
    for i, ref in enumerate(vectors):
        wide = jnp.broadcast_to(ref[...].astype(F32), (rows, rows))
        column = jnp.sum(jnp.where(same, wide, 0.0), axis=1, keepdims=True)
        total = jnp.where(lane == i, column, total)
    made[...] = total
    made[0:1, 16:64] = in_bias[...].astype(F32)
    out[:, : 3 * WIDTH] = w_qkv[...]
    out[:, 3 * WIDTH : CHUNK_ONE] = made[...].astype(BF16)
    out[:, CHUNK_ONE : CHUNK_ONE + FF] = w_in[...]
    out[:, CHUNK_ONE + FF :] = w_out[...]


def pack(vectors, in_bias, w_qkv, w_in, w_out):
    return pl.pallas_call(
        pack_kernel,
        out_shape=jax.ShapeDtypeStruct((12, CHUNK_ONE + CHUNK_TWO), BF16),
        in_specs=[VMEM] * 12,
        out_specs=VMEM,
        scratch_shapes=[pltpu.VMEM((12, 128), F32)],
        name="pack",
    )(*(v.reshape(1, 12) for v in vectors), in_bias.reshape(1, 48), w_qkv, w_in, w_out)


def first_kernel(slots, place, lengths, tokens, *refs):
    pieces = refs[:16]
    proj, mixed, logsum, in_bias, rows, weight, vec, wide, bias, sems = refs[16:]
    copies = piece_copies(slots, pieces, weight, sems, 0, (0, 3 * WIDTH))
    copies += piece_copies(slots, pieces, vec, sems, 16, (3 * WIDTH, 128))
    for copy in copies:
        copy.start()
    fill_bias(place, lengths, bias)
    hat, unused = normed(tokens[...].astype(F32))
    for copy in copies:
        copy.wait()
    wide[...] = vec[...].astype(F32)
    rows[...] = wide[...].T[:16]
    for n in range(64):
        in_bias[:, n * 48 : (n + 1) * 48] = wide[n * 12 : n * 12 + 1, 16:64]
    act = (hat * rows[0:1, :] + rows[1:2, :]).astype(BF16)
    for n in range(9):
        at = pl.ds(n * 256, 256)
        made = dot(act, weight[:, at])
        if n // 3 != 1:
            made = made + rows[2 + n // 6 : 3 + n // 6, (n % 3) * 256 : (n % 3 + 1) * 256]
        proj[:, at] = made.astype(BF16)
    logsum[...] = jnp.zeros_like(logsum)
    lane = lax.broadcasted_iota(jnp.int32, (128, 128), 1)

    def attend(p, carry):
        col = p * 128
        for i, start in enumerate(WINDOWS):
            here_rows, keys_at = pl.ds(i * 128, 128), pl.ds(start, 256)
            query = two_heads(proj[here_rows, rows_at(col, 128, 128)] * HEAD_DIM ** (-0.5))
            keys = proj[keys_at, rows_at(WIDTH + col, 128, 128)]
            vals = two_heads(proj[keys_at, rows_at(2 * WIDTH + col, 128, 128)])
            scores = dot_nt(query, keys).reshape(2, 128, 256) + bias[i][None]
            top = jnp.max(scores, axis=-1, keepdims=True)
            expo = jnp.exp(scores - top)
            total = jnp.sum(expo, axis=-1, keepdims=True)
            probs = (expo * (1.0 / total)).astype(BF16)
            both = jnp.concatenate([probs[0], probs[1]], axis=1)
            mixed[here_rows, rows_at(col, 128, 128)] = dot(both, vals).astype(BF16)
            summed = top + jnp.log(total)
            old = logsum[here_rows, :]
            old = jnp.where(lane == 2 * p, summed[0], old)
            logsum[here_rows, :] = jnp.where(lane == 2 * p + 1, summed[1], old)
        return carry

    lax.fori_loop(0, HEADS // 2, attend, 0)


def run_first(slots, place, lengths, tokens, pieces):
    return pl.pallas_call(
        first_kernel,
        out_shape=[
            jax.ShapeDtypeStruct((LEN, 3 * WIDTH), BF16),
            jax.ShapeDtypeStruct((LEN, WIDTH), BF16),
            jax.ShapeDtypeStruct((LEN, 128), F32),
            jax.ShapeDtypeStruct((1, FF), F32),
            jax.ShapeDtypeStruct((16, WIDTH), F32),
        ],
        in_specs=[SMEM, SMEM, SMEM, VMEM] + [ANY] * 16,
        out_specs=[VMEM] * 5,
        scratch_shapes=[
            pltpu.VMEM((WIDTH, 3 * WIDTH), BF16),
            pltpu.VMEM((WIDTH, 128), BF16),
            pltpu.VMEM((WIDTH, 128), F32),
            pltpu.VMEM((4, 128, 256), F32),
            pltpu.SemaphoreType.DMA((32,)),
        ],
        compiler_params=PARAMS,
        cost_estimate=COST,
        name="attention_forward",
    )(slots, place, lengths, tokens, *pieces)


def gelu_pair(x):
    expo = jnp.exp(-0.5 * x * x)
    t = 1.0 / (1.0 + (0.3275911 * 0.5**0.5) * jnp.abs(x))
    poly = 0.5 * 1.061405429
    for c in (-1.453152027, 1.421413741, -0.284496736, 0.254829592):
        poly = poly * t + 0.5 * c
    tail = poly * t * expo
    phi = jnp.where(x >= 0, 1.0 - tail, tail)
    return x * phi, phi + x * (expo * 0.3989422804014327)


def feed_kernel(slots, back_slots, place, tokens, mixed, cot, rows, in_bias, *refs):
    pieces, backs = refs[:16], refs[16:24]
    hidden, hat, scale, d_act, in_bias_grad, w_out, give, keep, give_back, keep_back = refs[24:34]
    w_in, w_back, x1, act, act_t, acc, turned, flip, gact, d_pre, sems = refs[34:]
    j = pl.program_id(0)
    out_copies = piece_copies(slots, pieces, w_out, sems, 0, (CHUNK_ONE + FF, WIDTH))
    in_copies = piece_copies(slots, pieces, w_in, sems, 16, (CHUNK_ONE, FF))
    back_copies = piece_copies(back_slots, backs, w_back, sems, 32)

    @pl.when(j == 0)
    def _():
        for copy in out_copies + in_copies + back_copies:
            copy.start()
        for copy in out_copies:
            copy.wait()
        for n in range(3):
            at = pl.ds(n * 256, 256)
            x1[:, at] = tokens[:, at].astype(F32) + (dot(mixed[...], w_out[:, at]) + rows[4:5, at])
        hat[...], scale[...] = normed(x1[...])
        act[...] = (hat[...] * rows[5:6, :] + rows[6:7, :]).astype(BF16)
        turned[...] = act[...].T
        split_rows(place, turned, act_t)
        acc[...] = jnp.zeros_like(acc)
        d_act[...] = jnp.zeros_like(d_act)
        for copy in in_copies + back_copies:
            copy.wait()

    base = j * WIDTH

    def units(n, carry):
        local, at = rows_at(n * 256, 256, 256), rows_at(base + n * 256, 256, 256)
        pre = dot(act[...], w_in[:, at]) + in_bias[:, at]
        d_gact = dot_nt(cot[...], w_back[at, :])
        value, slope = gelu_pair(pre)
        gact[:, local] = value.astype(BF16)
        d_low = (d_gact * slope).astype(BF16)
        d_pre[:, local] = d_low
        in_bias_grad[:, at] = jnp.sum(d_low.astype(F32), axis=0, keepdims=True)
        turned[local, :] = value.astype(BF16).T
        return carry

    lax.fori_loop(0, 3, units, 0)
    here_rows = rows_at(base, WIDTH, 256)
    split_rows(place, turned, flip)

    def sums(n, carry):
        at = rows_at(n * 256, 256, 256)
        acc[:, at] += dot(gact[...], w_back[here_rows, at])
        d_act[:, at] += dot_nt(d_pre[...], w_in[at, here_rows])
        made = dot(flip[...], cot[:, at]).astype(BF16)
        give_back[:, at] = made[: WIDTH // 2]
        keep_back[:, at] = made[WIDTH // 2 :]
        made = dot(act_t[...], d_pre[:, at]).astype(BF16)
        give[:, at] = made[: WIDTH // 2]
        keep[:, at] = made[WIDTH // 2 :]
        return carry

    lax.fori_loop(0, 3, sums, 0)

    @pl.when(j == 3)
    def _():
        hidden[...] = (x1[...] + (acc[...] + rows[7:8, :])).astype(BF16)


def run_feed(slots, back_slots, place, tokens, mixed, cot, rows, in_bias, pieces, backs):
    full = lambda *shape: pl.BlockSpec(shape, lambda j: (0,) * len(shape))
    wide = pl.BlockSpec((WIDTH // 2, WIDTH), lambda j: (0, j))
    tall = pl.BlockSpec((WIDTH // 2, WIDTH), lambda j: (j, 0))
    return pl.pallas_call(
        feed_kernel,
        grid=(4,),
        out_shape=[
            jax.ShapeDtypeStruct((LEN, WIDTH), BF16),
            jax.ShapeDtypeStruct((LEN, WIDTH), F32),
            jax.ShapeDtypeStruct((LEN, 1), F32),
            jax.ShapeDtypeStruct((LEN, WIDTH), F32),
            jax.ShapeDtypeStruct((1, FF), F32),
            jax.ShapeDtypeStruct((WIDTH, WIDTH), BF16),
            jax.ShapeDtypeStruct((WIDTH // 2, FF), BF16),
            jax.ShapeDtypeStruct((WIDTH // 2, FF), BF16),
            jax.ShapeDtypeStruct((FF // 2, WIDTH), BF16),
            jax.ShapeDtypeStruct((FF // 2, WIDTH), BF16),
        ],
        in_specs=[SMEM, SMEM, SMEM]
        + [full(LEN, WIDTH)] * 3
        + [full(16, WIDTH), full(1, FF)]
        + [ANY] * 24,
        out_specs=[
            full(LEN, WIDTH),
            full(LEN, WIDTH),
            full(LEN, 1),
            full(LEN, WIDTH),
            full(1, FF),
            full(WIDTH, WIDTH),
            wide,
            wide,
            tall,
            tall,
        ],
        scratch_shapes=[
            pltpu.VMEM((WIDTH, FF), BF16),
            pltpu.VMEM((FF, WIDTH), BF16),
            pltpu.VMEM((LEN, WIDTH), F32),
            pltpu.VMEM((LEN, WIDTH), BF16),
            pltpu.VMEM((WIDTH, LEN), BF16),
            pltpu.VMEM((LEN, WIDTH), F32),
            pltpu.VMEM((WIDTH, LEN), BF16),
            pltpu.VMEM((WIDTH, LEN), BF16),
            pltpu.VMEM((LEN, WIDTH), BF16),
            pltpu.VMEM((LEN, WIDTH), BF16),
            pltpu.SemaphoreType.DMA((96,)),
        ],
        compiler_params=PARAMS,
        cost_estimate=COST,
        name="feed_forward",
    )(slots, back_slots, place, tokens, mixed, cot, rows, in_bias, *pieces, *backs)


def feed_back_kernel(place, cot, hat, scale, d_act, rows, mixed, w_out, *refs):
    g1, d_mixed, vector_grads, give, keep, turned, mixed_t = refs
    cot_wide = cot[...].astype(F32)
    d_in, gain_grad, bias_grad = norm_back(d_act[...], hat[...], scale[...], rows[5:6, :])
    total = cot_wide + d_in
    g1[...] = total
    low = total.astype(BF16)
    turned[...] = mixed[...].T
    split_rows(place, turned, mixed_t)
    for n in range(3):
        at = pl.ds(n * 256, 256)
        d_mixed[:, at] = dot_nt(low, w_out[at, :]).astype(BF16)
        made = dot(mixed_t[...], low[:, n * 256 : (n + 1) * 256]).astype(BF16)
        give[:, at] = made[: WIDTH // 2]
        keep[:, at] = made[WIDTH // 2 :]
    vector_grads[...] = jnp.concatenate(
        [
            jnp.sum(low.astype(F32), axis=0, keepdims=True),
            gain_grad,
            bias_grad,
            jnp.sum(cot_wide, axis=0, keepdims=True),
            jnp.zeros((4, WIDTH), F32),
        ],
        axis=0,
    )


def run_feed_back(place, *arrays):
    return pl.pallas_call(
        feed_back_kernel,
        out_shape=[
            jax.ShapeDtypeStruct((LEN, WIDTH), F32),
            jax.ShapeDtypeStruct((LEN, WIDTH), BF16),
            jax.ShapeDtypeStruct((8, WIDTH), F32),
            jax.ShapeDtypeStruct((WIDTH // 2, WIDTH), BF16),
            jax.ShapeDtypeStruct((WIDTH // 2, WIDTH), BF16),
        ],
        in_specs=[SMEM] + [VMEM] * len(arrays),
        out_specs=[VMEM] * 5,
        scratch_shapes=[pltpu.VMEM((WIDTH, LEN), BF16)] * 2,
        compiler_params=PARAMS,
        cost_estimate=COST,
        name="feed_backward",
    )(place, *arrays)


def attend_back_kernel(place, lengths, proj, logsum, d_mixed, d_proj, bias, d_keys, d_vals):
    fill_bias(place, lengths, bias)
    lane = lax.broadcasted_iota(jnp.int32, (128, 128), 1)

    def attend(p, carry):
        col = p * 128
        own = rows_at(col, 128, 128)
        d_keys[...] = jnp.zeros_like(d_keys)
        d_vals[...] = jnp.zeros_like(d_vals)
        for i, start in enumerate(WINDOWS):
            here_rows, keys_at = pl.ds(i * 128, 128), pl.ds(start, 256)
            query = two_heads(proj[here_rows, own] * HEAD_DIM ** (-0.5))
            keys = proj[keys_at, rows_at(WIDTH + col, 128, 128)]
            vals = proj[keys_at, rows_at(2 * WIDTH + col, 128, 128)]
            d_mix = two_heads(d_mixed[here_rows, own])
            sums = logsum[here_rows, :]
            summed = jnp.stack(
                [
                    jnp.sum(jnp.where(lane == 2 * p + n, sums, 0.0), axis=-1, keepdims=True)
                    for n in range(2)
                ]
            )
            scores = dot_nt(query, keys).reshape(2, 128, 256) + bias[i][None]
            probs = jnp.exp(scores - summed)
            d_probs = dot_nt(d_mix, vals).reshape(2, 128, 256)
            mean = jnp.sum(probs * d_probs, axis=-1, keepdims=True)
            d_scores = (probs * (d_probs - mean)).astype(BF16)
            both = jnp.concatenate([d_scores[0], d_scores[1]], axis=1)
            d_query = dot(both, two_heads(keys)) * HEAD_DIM ** (-0.5)
            d_proj[here_rows, own] = d_query.astype(BF16)
            d_keys[keys_at, :] += dot_tn(d_scores.reshape(256, 256), query)
            d_vals[keys_at, :] += dot_tn(probs.astype(BF16).reshape(256, 256), d_mix)
        d_proj[:, rows_at(WIDTH + col, 128, 128)] = d_keys[...].astype(BF16)
        d_proj[:, rows_at(2 * WIDTH + col, 128, 128)] = d_vals[...].astype(BF16)
        return carry

    lax.fori_loop(0, HEADS // 2, attend, 0)


def run_attend_back(place, lengths, proj, logsum, d_mixed):
    return pl.pallas_call(
        attend_back_kernel,
        out_shape=jax.ShapeDtypeStruct((LEN, 3 * WIDTH), BF16),
        in_specs=[SMEM, SMEM] + [VMEM] * 3,
        out_specs=VMEM,
        scratch_shapes=[
            pltpu.VMEM((4, 128, 256), F32),
            pltpu.VMEM((LEN, 128), F32),
            pltpu.VMEM((LEN, 128), F32),
        ],
        compiler_params=PARAMS,
        cost_estimate=COST,
        name="attention_backward",
    )(place, lengths, proj, logsum, d_mixed)


def project_back_kernel(slots, place, tokens, d_proj, g1, rows, grads_two, in_bias, *refs):
    pieces = refs[:16]
    d_input, give, keep, weight, d_act, turned, act_t, natural, sems = refs[16:]
    copies = piece_copies(slots, pieces, weight, sems, 0, (0, 3 * WIDTH))
    for copy in copies:
        copy.start()
    hat, scale = normed(tokens[...].astype(F32))
    turned[...] = (hat * rows[0:1, :] + rows[1:2, :]).astype(BF16).T
    split_rows(place, turned, act_t)
    for n in range(9):
        at = pl.ds(n * 256, 256)
        made = dot(act_t[...], d_proj[:, at]).astype(BF16)
        give[:, at] = made[: WIDTH // 2]
        keep[:, at] = made[WIDTH // 2 :]
    for copy in copies:
        copy.wait()
    for n in range(3):
        at = pl.ds(n * 256, 256)
        d_act[:, at] = dot_nt(d_proj[...], weight[at, :])
    d_in, gain_grad, bias_grad = norm_back(d_act[...], hat, scale, rows[0:1, :])
    d_input[...] = g1[...] + d_in
    made = jnp.concatenate(
        [
            gain_grad,
            bias_grad,
            jnp.sum(d_proj[:, :WIDTH].astype(F32), axis=0, keepdims=True),
            jnp.sum(d_proj[:, 2 * WIDTH :].astype(F32), axis=0, keepdims=True),
            grads_two[:4, :],
            jnp.zeros((120, WIDTH), F32),
        ],
        axis=0,
    )
    natural[...] = made.T
    for n in range(64):
        natural[n * 12 : n * 12 + 1, 16:64] = in_bias[:, n * 48 : (n + 1) * 48]
    core = place[0]
    for b in range(BLOCKS):
        for out, half in ((give, 1 - core), (keep, core)):
            out[b * HALF : (b + 1) * HALF, 3 * WIDTH :] = natural[
                rows_at(b * 2 * HALF + half * HALF, HALF), :
            ].astype(BF16)


def run_project_back(slots, place, tokens, d_proj, g1, rows, grads_two, in_bias, pieces):
    return pl.pallas_call(
        project_back_kernel,
        out_shape=[
            jax.ShapeDtypeStruct((LEN, WIDTH), F32),
            jax.ShapeDtypeStruct((WIDTH // 2, CHUNK_ONE), BF16),
            jax.ShapeDtypeStruct((WIDTH // 2, CHUNK_ONE), BF16),
        ],
        in_specs=[SMEM, SMEM] + [VMEM] * 6 + [ANY] * 16,
        out_specs=[VMEM] * 3,
        scratch_shapes=[
            pltpu.VMEM((WIDTH, 3 * WIDTH), BF16),
            pltpu.VMEM((LEN, WIDTH), F32),
            pltpu.VMEM((WIDTH, LEN), BF16),
            pltpu.VMEM((WIDTH, LEN), BF16),
            pltpu.VMEM((WIDTH, 128), F32),
            pltpu.SemaphoreType.DMA((16,)),
        ],
        compiler_params=PARAMS,
        cost_estimate=COST,
        name="project_backward",
    )(slots, place, tokens, d_proj, g1, rows, grads_two, in_bias, *pieces)


def run_split(name, starts, groups, columns):
    widths = [arrays[0].shape[1] for arrays in columns]
    counts = [len(arrays) for arrays in columns]

    def kernel(starts_ref, *refs):
        ins, outs = refs[: sum(counts)], refs[sum(counts) :]
        n = 0
        for out, (blocks, kind) in zip(outs, groups):
            for b in range(blocks):
                at = rows_at(starts_ref[n] * HALF, HALF)
                n += 1
                first, column = 0, 0
                for width, count in zip(widths, counts):
                    total = ins[first][at, :].astype(F32)
                    for ref in ins[first + 1 : first + count]:
                        total = total + ref[at, :].astype(F32)
                    out[b * HALF : (b + 1) * HALF, column : column + width] = total.astype(kind)
                    first, column = first + count, column + width

    return pl.pallas_call(
        kernel,
        out_shape=[
            jax.ShapeDtypeStruct((blocks * HALF, sum(widths)), kind) for blocks, kind in groups
        ],
        in_specs=[SMEM] + [VMEM] * sum(counts),
        out_specs=[VMEM] * len(groups),
        compiler_params=pltpu.CompilerParams(vmem_limit_bytes=40 * 1024 * 1024),
        cost_estimate=COST,
        name=name,
    )(jnp.stack(starts).astype(jnp.int32), *(a for arrays in columns for a in arrays))


def shards(tokens, lengths, g1, s1, wqkv, qb, vb, wo, ob, g2, s2, w1, bi1, w2, b2, cotangent):
    y, z, x, core, sign = here()
    place = jnp.stack([core, lax.axis_index("dp") * 64 + lax.axis_index("fsdp"), y, z])
    pieces, backs = gather(pack((g1, s1, qb, vb, ob, g2, s2, b2), bi1, wqkv, w1, wo), w2)
    slots, slots_b = row_slots(), back_slots()

    proj, mixed, logsum, in_bias, rows = run_first(slots, place, lengths, tokens, pieces)
    hidden, hat, scale, d_act, in_bias_grad, w_out, give_i, keep_i, give_b, keep_b = run_feed(
        slots, slots_b, place, tokens, mixed, cotangent, rows, in_bias, pieces, backs
    )
    got_i, got_b = send(give_i, CORES), send(give_b, CORES)
    d_middle, d_mixed, grads_two, give_o, keep_o = run_feed_back(
        place, cotangent, hat, scale, d_act, rows, mixed, w_out
    )
    d_mixed, give_o, got_i, got_b = all_done(d_mixed, give_o, got_i, got_b)
    got_o = send(give_o, CORES)

    starts = [(1 - y) * 4 + k for k in range(4)] + [y * 4 + k for k in range(4)]
    theirs, mine = run_split("sum_cores_in", starts, [(4, BF16), (4, BF16)], [(keep_i, got_i)])
    starts = [yz * 4 + (x + k) % 4 for k in (0, 1, 3, 2) for yz in range(8)]
    own_b, up, down, far_up, far_down = run_split(
        "sum_cores_back",
        starts,
        [(8, F32), (8, BF16), (8, BF16), (4, BF16), (4, BF16)],
        [(keep_b, got_b)],
    )
    d_mixed, theirs, own_b, far_up, far_down, got_o = all_done(
        d_mixed, theirs, own_b, far_up, far_down, got_o
    )
    from_y = send(theirs, Y_RING)
    near_up, near_down = send(far_up, X_BY[1]), send(far_down, X_BY[3])
    d_proj = run_attend_back(place, lengths, proj, logsum, d_mixed)
    d_proj, from_y, near_up, near_down = all_done(d_proj, from_y, near_up, near_down)

    up = jnp.concatenate([up[:192] + near_up, up[192:]], axis=0)
    down = jnp.concatenate([down[:192], down[192:] + near_down], axis=0)
    starts = [(z + k) % 4 for k in range(4)]
    own_i, *parts = run_split("sum_y", starts, [(1, F32)] + [(1, BF16)] * 3, [(mine, from_y)])
    d_proj, up, down, own_i, *parts = all_done(d_proj, up, down, own_i, *parts)
    from_z_i = [send(p, Z_BY[k]) for p, k in zip(parts, (1, 2, 3))]
    from_x = [send(up, X_BY[1]), send(down, X_BY[3])]
    d_input, give_q, keep_q = run_project_back(
        slots, place, tokens, d_proj, d_middle, rows, grads_two, in_bias_grad, pieces
    )
    give_q, from_x, from_z_i = all_done(give_q, from_x, from_z_i)
    got_q = send(give_q, CORES)

    starts = [yy * 4 + (z + k) % 4 for k in range(4) for yy in range(2)]
    own_b, *parts = run_split(
        "sum_x", starts, [(2, F32)] + [(2, BF16)] * 3, [(own_b, *from_x)]
    )
    from_z = [send(p, Z_BY[k]) for p, k in zip(parts, (1, 2, 3))]

    starts = [(y ^ row) * 4 + (z + k) % 4 for row, k in YZ]
    own_1, *parts = run_split(
        "sum_cores_rest",
        starts,
        [(1, F32)] + [(1, BF16)] * 7,
        [(keep_q, got_q), (keep_o, got_o)],
    )
    from_yz = [send(p, YZ_BY[at]) for p, at in zip(parts, YZ[1:])]
    total = own_b + sum(p.astype(F32) for p in from_z)
    total = total.reshape(2, 48, WIDTH)
    back_share = pick(total, y) + send(pick(total, 1 - y).astype(BF16), Y_RING).astype(F32)

    share_one = own_1 + sum(p.astype(F32) for p in from_yz)
    share_two = own_i + sum(p.astype(F32) for p in from_z_i)
    share = over_replicas(to_owner(jnp.concatenate([share_one, share_two], axis=1)))
    back_share = over_replicas(back_share)
    own = share[:, 3 * WIDTH : 3 * WIDTH + 128]
    return (
        hidden,
        d_input,
        own[:, 0],
        own[:, 1],
        share[:, : 3 * WIDTH],
        own[:, 2],
        own[:, 3],
        share[:, 3 * WIDTH + 128 : 4 * WIDTH + 128],
        own[:, 4],
        own[:, 5],
        own[:, 6],
        share[:, 4 * WIDTH + 128 :],
        own[0, 16:64],
        back_share,
        own[:, 7],
    )


def solution(mesh):
    rows, whole = P(AXES, None), P()
    vector, matrix = P("fsdp"), P("fsdp", None)
    weights = (
        vector, vector, matrix, vector, vector, matrix, vector,
        vector, vector, matrix, vector, matrix, vector,
    )
    return jax.shard_map(
        shards,
        mesh=mesh,
        in_specs=(rows, whole, *weights, rows),
        out_specs=(rows, rows, *weights),
        check_vma=False,
    )
```

```python
import functools
import itertools

import jax
import jax.numpy as jnp
from jax import lax
from jax.experimental import pallas as pl
from jax.experimental.pallas import tpu as pltpu
from jax.sharding import PartitionSpec as P

HEADS = 12
HEAD_DIM = 64
LEN = 512
WIDTH = 768
FF = 3072
AXES = ("dp", "fsdp")
F32 = jnp.float32
BF16 = jnp.bfloat16

EVERY = [(y, z, x, c) for y in range(4) for z in range(4) for x in range(4) for c in range(2)]


def index_of(y, z, x, c):
    y, z, x, c = y % 4, z % 4, x % 4, c % 2
    return (y // 2) * 64 + (((y % 2) * 4 + z) * 4 + x) * 2 + c


def moves(by, by_second=None):
    steps = (by, by if by_second is None else by_second)
    return [(index_of(*at), index_of(*(a + s for a, s in zip(at, steps[at[3]])))) for at in EVERY]


Y_RING = moves((1, 0, 0, 0), (-1, 0, 0, 0))
Z_RING = moves((0, 1, 0, 0), (0, -1, 0, 0))
X_RING = moves((0, 0, 1, 0), (0, 0, -1, 0))
Z_BY = {k: moves((0, k, 0, 0)) for k in (1, 2, 3)}
CORES = moves((0, 0, 0, 1))
REPLICA = moves((2, 0, 0, 0))
SPREAD = [
    [
        (index_of(y, z, x, c), index_of(y, z, 2 * (x % 2) + c - k, x // 2))
        for y, z, x, c in EVERY
    ]
    for k in range(4)
]
COLLECT = [[(b, a) for a, b in pairs] for pairs in SPREAD]


def send(array, pairs):
    return lax.ppermute(array, AXES, pairs)


def here():
    at = lax.axis_index("fsdp")
    core, x, z, y = at % 2, (at // 2) % 4, (at // 8) % 4, at // 32
    return y, z, x, core, 1 - 2 * core


def pick(array, at, axis=0):
    return lax.dynamic_index_in_dim(array, at, axis, keepdims=False)


YZ = [(row, z) for row in range(2) for z in range(4)]
YZ_ORDER = [(0, 2), (1, 0), (0, 1), (0, 3), (1, 1), (1, 3), (1, 2), (0, 0)]
YZ_BY = {(row, z): moves((row, z, 0, 0), (-row, z, 0, 0)) for row, z in YZ}
X_BY = {k: moves((0, 0, k, 0)) for k in (1, 2, 3)}


def half_block(shard):
    x = here()[2]
    got = [send(shard, SPREAD[k]) for k in range(4)]
    ring = jnp.stack(got + got[:3])
    return lax.dynamic_slice_in_dim(ring, (4 - x) % 4, 4, 0).reshape(48, shard.shape[1])


def all_done(*arrays):
    return lax.optimization_barrier(arrays)


PAD = 16


def gather(pack_shard, back):
    by_z = [send(back, Z_BY[k]) for k in (1, 2, 3)]
    shard, *by_z = all_done(pack_shard(), *by_z)
    quad = jnp.concatenate([back, *by_z], axis=0)
    by_y = send(quad, Y_RING)
    own = [half_block(shard)]
    quads = [jnp.concatenate([quad, by_y, jnp.zeros((PAD, WIDTH), BF16)], axis=0)]
    side, over_own, over_side = [], [], []
    for t in range(4):
        now = [own[t], *side[t - 1 : t]]
        if t < 3:
            now.append(quads[t])
        now = all_done(*now)
        if t < 3:
            quads.append(send(now[-1], X_RING))
            own.append(send(now[0], Z_RING))
        side.append(send(now[0], Y_RING))
        if t:
            over_side.append(send(now[1], CORES))
        over_own.append(send(now[0], CORES))
        done = [own[-1], side[-1], over_own[-1]]
        if t < 3:
            done.append(quads[-1])
        if t:
            done.append(over_side[-1])
        done = list(all_done(*done))
        own[-1], side[-1], over_own[-1] = done[:3]
        if t < 3:
            quads[-1] = done[3]
        if t:
            over_side[-1] = done[-1]
    over_side.append(send(side[3], CORES))
    return own + side + over_own + over_side, quads + [send(q, CORES) for q in quads]


def over_replicas(share):
    share = lax.reduce_precision(share, 8, 7)
    return share + send(share.astype(BF16), REPLICA).astype(F32)


def to_owner(total):
    x = here()[2]
    pieces = total.reshape(4, 12, total.shape[-1])
    return sum(send(pick(pieces, (x + k) % 4), COLLECT[k]).astype(F32) for k in range(4))


HALF = 48
BLOCKS = WIDTH // (2 * HALF)
WINDOWS = (0, 0, 64, 128, 192, 256, 320, 320)
SPAN = 192
GROUP = 4 * HEAD_DIM
VMEM = pl.BlockSpec(memory_space=pltpu.VMEM)
SMEM = pl.BlockSpec(memory_space=pltpu.SMEM)
ANY = pl.BlockSpec(memory_space=pl.ANY)


def limit(mib):
    return pltpu.CompilerParams(vmem_limit_bytes=mib * 1024 * 1024)


COST = pl.CostEstimate(flops=10**6, bytes_accessed=10**5, transcendentals=0)
CHUNK_ONE = 3 * WIDTH + 128
CHUNK_TWO = FF + WIDTH


def dot(a, b):
    return lax.dot_general(a, b, (((1,), (0,)), ((), ())), preferred_element_type=F32)


def dot_nt(a, b):
    return lax.dot_general(a, b, (((1,), (1,)), ((), ())), preferred_element_type=F32)


def dot_tn(a, b):
    return lax.dot_general(a, b, (((0,), (0,)), ((), ())), preferred_element_type=F32)


def normed(values):
    centre = values - jnp.mean(values, axis=-1, keepdims=True)
    scale = lax.rsqrt(jnp.mean(centre * centre, axis=-1, keepdims=True) + 1e-05)
    return centre * scale, scale


def norm_back(d_out, hat, scale, gain):
    expand = d_out * gain
    d_in = scale * (
        expand
        - jnp.mean(expand, axis=-1, keepdims=True)
        - hat * jnp.mean(expand * hat, axis=-1, keepdims=True)
    )
    gain_grad = jnp.sum(d_out * hat, axis=0, keepdims=True)
    return d_in, gain_grad, jnp.sum(d_out, axis=0, keepdims=True)


def rows_at(start, size, step=16):
    return pl.ds(pl.multiple_of(start, step), size)


def places(place_ref):
    core, y, z, x = (place_ref[n] for n in (0, 2, 3, 4))
    return core, y, z, x, 1 - 2 * core


def around(at, step):
    return lax.rem(at + step + 8, 4)


def row_slots(place_ref):
    core, y, z, x, sign = places(place_ref)
    return [
        (row * 4 + around(z, -way * t)) * 2 + half
        for half, way in ((core, sign), (1 - core, -sign))
        for row in (y, 1 - y)
        for t in range(4)
    ]


def back_slots(place_ref):
    core, y, z, x, sign = places(place_ref)
    return [
        ((row * 4 + around(z, -k)) * 4 + around(x, -way * t)) * 2 + half
        for half, way in ((core, sign), (1 - core, -sign))
        for t in range(4)
        for row in (y, 1 - y)
        for k in range(4)
    ]


def piece_copies(slots, pieces, target, sems, first, columns=None):
    copies = []
    each = len(slots) // len(pieces)
    for n, slot in enumerate(slots):
        source = pieces[n // each].at[pl.ds(n % each * HALF, HALF), :]
        if columns is not None:
            source = source.at[:, pl.ds(*columns)]
        copies.append(
            pltpu.make_async_copy(
                source, target.at[rows_at(slot * HALF, HALF)], sems.at[first + n]
            )
        )
    return copies


def split_rows(place_ref, made):
    columns = made.shape[1]
    parts = made.astype(BF16).reshape(BLOCKS, 2, HALF, columns)
    first, second = (parts[:, n].reshape(BLOCKS * HALF, columns) for n in range(2))
    low = place_ref[0] == 0
    return lax.select(low, second, first), lax.select(low, first, second)


def head_of(rows):
    return lax.broadcasted_iota(jnp.int32, (rows, GROUP), 1) // HEAD_DIM


def four_heads(group):
    head, zero = head_of(group.shape[0]), jnp.zeros_like(group)
    return jnp.concatenate([jnp.where(head == h, group, zero) for h in range(4)], axis=0)


def one_of_four(wide):
    n = wide.shape[0] // 4
    head, result = head_of(n), wide[:n]
    for h in range(1, 4):
        result = jnp.where(head == h, wide[h * n : (h + 1) * n], result)
    return result


def fill_bias(place_ref, lengths_ref, bias):
    ends, total = [], jnp.int32(0)
    for k in range(16):
        total = total + lengths_ref[k, place_ref[1]]
        ends.append(total)

    def ids(at):
        return sum((at >= end).astype(jnp.int32) for end in ends)

    keys = ids(lax.broadcasted_iota(jnp.int32, (LEN, 1), 0))
    lane = lax.broadcasted_iota(jnp.int32, (1, GROUP), 1) % HEAD_DIM
    for i, start in enumerate(WINDOWS):
        same = keys[start : start + SPAN] == ids(lane + i * 64)
        bias[i] = jnp.where(same, 0.0, -1e30).astype(F32)


def pack_kernel(*refs):
    vectors, in_bias, w_qkv, w_in, w_out, out, made = refs[:8], *refs[8:]
    rows = w_qkv.shape[0]
    same = lax.broadcasted_iota(jnp.int32, (rows, rows), 0) == lax.broadcasted_iota(
        jnp.int32, (rows, rows), 1
    )
    lane = lax.broadcasted_iota(jnp.int32, (rows, 128), 1)
    total = jnp.zeros((rows, 128), F32)
    for i, ref in enumerate(vectors):
        wide = jnp.broadcast_to(ref[...].astype(F32), (rows, rows))
        column = jnp.sum(jnp.where(same, wide, 0.0), axis=1, keepdims=True)
        total = jnp.where(lane == i, column, total)
    made[...] = total
    made[0:1, 16:64] = in_bias[...].astype(F32)
    out[:, : 3 * WIDTH] = w_qkv[...]
    out[:, 3 * WIDTH : CHUNK_ONE] = made[...].astype(BF16)
    out[:, CHUNK_ONE : CHUNK_ONE + FF] = w_in[...]
    out[:, CHUNK_ONE + FF :] = w_out[...]


def pack(vectors, in_bias, w_qkv, w_in, w_out):
    return pl.pallas_call(
        pack_kernel,
        out_shape=jax.ShapeDtypeStruct((12, CHUNK_ONE + CHUNK_TWO), BF16),
        in_specs=[VMEM] * 12,
        out_specs=VMEM,
        scratch_shapes=[pltpu.VMEM((12, 128), F32)],
        name="pack",
    )(*(v.reshape(1, 12) for v in vectors), in_bias.reshape(1, 48), w_qkv, w_in, w_out)


def first_kernel(place, lengths, tokens, *refs):
    pieces = refs[:16]
    proj_out, mixed, logsum, in_bias, rows, proj, weight, vec, wide, bias, sems = refs[16:]
    slots = row_slots(place)
    copies = piece_copies(slots, pieces, weight, sems, 0, (0, 3 * WIDTH))
    copies += piece_copies(slots, pieces, vec, sems, 16, (3 * WIDTH, 128))
    for copy in copies:
        copy.start()
    fill_bias(place, lengths, bias)
    hat, unused = normed(tokens[...].astype(F32))
    for copy in copies:
        copy.wait()
    wide[...] = vec[...].astype(F32)
    rows[...] = wide[...].T[:16]
    for n in range(64):
        in_bias[:, n * 48 : (n + 1) * 48] = wide[n * 12 : n * 12 + 1, 16:64]
    act = (hat * rows[0:1, :] + rows[1:2, :]).astype(BF16)
    for n in range(9):
        at = pl.ds(n * 256, 256)
        made = dot(act, weight[:, at])
        if n // 3 != 1:
            made = made + rows[2 + n // 6 : 3 + n // 6, (n % 3) * 256 : (n % 3 + 1) * 256]
        proj[:, at] = made.astype(BF16)
    out_copy = pltpu.make_async_copy(proj, proj_out, sems.at[32])
    out_copy.start()
    for p in range(HEADS // 4):
        query_at, keys_at, vals_at = (pl.ds(n * WIDTH + p * GROUP, GROUP) for n in range(3))
        for i, start in enumerate(WINDOWS):
            here_rows, near = pl.ds(i * 64, 64), pl.ds(start, SPAN)
            query = four_heads(proj[here_rows, query_at] * HEAD_DIM ** (-0.5))
            scores = dot_nt(proj[near, keys_at], query) + bias[i]
            top = jnp.max(scores, axis=0, keepdims=True)
            expo = jnp.exp(scores - top)
            total = jnp.sum(expo, axis=0, keepdims=True)
            probs = (expo * (1.0 / total)).astype(BF16)
            mixed[here_rows, query_at] = one_of_four(dot_tn(probs, proj[near, vals_at])).astype(BF16)
            logsum[p * 8 + i : p * 8 + i + 1, :] = top + jnp.log(total)
    out_copy.wait()


def run_first(place, lengths, tokens, pieces):
    return pl.pallas_call(
        first_kernel,
        out_shape=[
            jax.ShapeDtypeStruct((LEN, 3 * WIDTH), BF16),
            jax.ShapeDtypeStruct((LEN, WIDTH), BF16),
            jax.ShapeDtypeStruct((24, 256), F32),
            jax.ShapeDtypeStruct((1, FF), F32),
            jax.ShapeDtypeStruct((16, WIDTH), F32),
        ],
        in_specs=[SMEM, SMEM, VMEM] + [ANY] * 16,
        out_specs=[ANY] + [VMEM] * 4,
        scratch_shapes=[
            pltpu.VMEM((LEN, 3 * WIDTH), BF16),
            pltpu.VMEM((WIDTH, 3 * WIDTH), BF16),
            pltpu.VMEM((WIDTH, 128), BF16),
            pltpu.VMEM((WIDTH, 128), F32),
            pltpu.VMEM((8, SPAN, GROUP), F32),
            pltpu.SemaphoreType.DMA((33,)),
        ],
        compiler_params=limit(60),
        cost_estimate=COST,
        name="attention_forward",
    )(place, lengths, tokens, *pieces)


def gelu_pair(x):
    phi = 0.5 + 0.5 * lax.erf(x * 0.5**0.5)
    return x * phi, phi + x * (jnp.exp(x * (x * -0.5)) * 0.3989422804014327)


def feed_kernel(place, tokens, mixed, cot, rows, in_bias, *refs):
    pieces, backs = refs[:16], refs[16:24]
    hidden, hat, scale, d_act, in_bias_grad, w_out, give, keep, give_back, keep_back = refs[24:34]
    w_in, w_back, x1, act, acc, gact_0, gact_1, d_pre_0, d_pre_1 = refs[34:43]
    made_give, made_keep, made_give_back, made_keep_back, sems, out_sems = refs[43:]
    gact, d_pre = (gact_0, gact_1), (d_pre_0, d_pre_1)
    slots = row_slots(place)
    out_copies = piece_copies(slots, pieces, w_out, sems, 0, (CHUNK_ONE + FF, WIDTH))
    in_copies = piece_copies(slots, pieces, w_in, sems, 16, (CHUNK_ONE, FF))
    back_copies = piece_copies(back_slots(place), backs, w_back, sems, 32)
    for copy in out_copies + in_copies + back_copies:
        copy.start()
    for copy in out_copies:
        copy.wait()
    for n in range(3):
        at = pl.ds(n * 256, 256)
        x1[:, at] = tokens[:, at].astype(F32) + (dot(mixed[...], w_out[:, at]) + rows[4:5, at])
    hat[...], scale[...] = normed(x1[...])
    act[...] = (hat[...] * rows[5:6, :] + rows[6:7, :]).astype(BF16)
    for copy in in_copies + back_copies:
        copy.wait()

    def units(j, n):
        local, at = pl.ds(n * 256, 256), pl.ds(j * WIDTH + n * 256, 256)
        value, slope = gelu_pair(dot(act[...], w_in[:, at]) + in_bias[:, at])
        gact[j % 2][:, local] = value.astype(BF16)
        d_low = (dot_nt(cot[...], w_back[at, :]) * slope).astype(BF16)
        d_pre[j % 2][:, local] = d_low
        in_bias_grad[:, at] = jnp.sum(d_low.astype(F32), axis=0, keepdims=True)

    def sums(j, n):
        at, block, half = pl.ds(n * 256, 256), pl.ds(j * WIDTH, WIDTH), pl.ds(j * 384, 384)
        forward = dot(gact[j % 2][...], w_back[block, at])
        backward = dot_nt(d_pre[j % 2][...], w_in[at, block])
        acc[:, at] = forward if j == 0 else acc[:, at] + forward
        d_act[:, at] = backward if j == 0 else d_act[:, at] + backward
        wide = pl.ds(j * WIDTH + n * 256, 256)
        made_give[:, wide], made_keep[:, wide] = split_rows(
            place, dot_tn(act[...], d_pre[j % 2][:, at])
        )
        made_give_back[half, at], made_keep_back[half, at] = split_rows(
            place, dot_tn(gact[j % 2][...], cot[:, at])
        )

    copies = []
    for j in range(5):
        for n in range(3):
            if j < 4:
                units(j, n)
            if j:
                sums(j - 1, n)
        if j:
            wide, half = pl.ds((j - 1) * WIDTH, WIDTH), pl.ds((j - 1) * 384, 384)
            for made, out, at in (
                (made_give, give, (slice(None), wide)),
                (made_give_back, give_back, (half, slice(None))),
                (made_keep, keep, (slice(None), wide)),
                (made_keep_back, keep_back, (half, slice(None))),
            ):
                copies.append(
                    pltpu.make_async_copy(made.at[at], out.at[at], out_sems.at[len(copies)])
                )
                copies[-1].start()
    hidden[...] = (x1[...] + (acc[...] + rows[7:8, :])).astype(BF16)
    for copy in copies:
        copy.wait()


def run_feed(place, tokens, mixed, cot, rows, in_bias, pieces, backs):
    return pl.pallas_call(
        feed_kernel,
        out_shape=[
            jax.ShapeDtypeStruct((LEN, WIDTH), BF16),
            jax.ShapeDtypeStruct((LEN, WIDTH), F32),
            jax.ShapeDtypeStruct((LEN, 1), F32),
            jax.ShapeDtypeStruct((LEN, WIDTH), F32),
            jax.ShapeDtypeStruct((1, FF), F32),
            jax.ShapeDtypeStruct((WIDTH, WIDTH), BF16),
            jax.ShapeDtypeStruct((WIDTH // 2, FF), BF16),
            jax.ShapeDtypeStruct((WIDTH // 2, FF), BF16),
            jax.ShapeDtypeStruct((FF // 2, WIDTH), BF16),
            jax.ShapeDtypeStruct((FF // 2, WIDTH), BF16),
        ],
        in_specs=[SMEM] + [VMEM] * 5 + [ANY] * 24,
        out_specs=[VMEM] * 6 + [ANY] * 4,
        scratch_shapes=[
            pltpu.VMEM((WIDTH, FF), BF16),
            pltpu.VMEM((FF, WIDTH), BF16),
            pltpu.VMEM((LEN, WIDTH), F32),
            pltpu.VMEM((LEN, WIDTH), BF16),
            pltpu.VMEM((LEN, WIDTH), F32),
            pltpu.VMEM((LEN, WIDTH), BF16),
            pltpu.VMEM((LEN, WIDTH), BF16),
            pltpu.VMEM((LEN, WIDTH), BF16),
            pltpu.VMEM((LEN, WIDTH), BF16),
            pltpu.VMEM((WIDTH // 2, FF), BF16),
            pltpu.VMEM((WIDTH // 2, FF), BF16),
            pltpu.VMEM((FF // 2, WIDTH), BF16),
            pltpu.VMEM((FF // 2, WIDTH), BF16),
            pltpu.SemaphoreType.DMA((96,)),
            pltpu.SemaphoreType.DMA((16,)),
        ],
        compiler_params=limit(60),
        cost_estimate=COST,
        name="feed_forward",
    )(place, tokens, mixed, cot, rows, in_bias, *pieces, *backs)


def feed_back_kernel(place, cot, hat, scale, d_act, rows, mixed, w_out, *refs):
    g1, d_mixed, vector_grads, give, keep = refs
    cot_wide = cot[...].astype(F32)
    d_in, gain_grad, bias_grad = norm_back(d_act[...], hat[...], scale[...], rows[5:6, :])
    total = cot_wide + d_in
    g1[...] = total
    low = total.astype(BF16)
    for n in range(3):
        at = pl.ds(n * 256, 256)
        d_mixed[:, at] = dot_nt(low, w_out[at, :]).astype(BF16)
        give[:, at], keep[:, at] = split_rows(
            place, dot_tn(mixed[...], low[:, n * 256 : (n + 1) * 256])
        )
    vector_grads[...] = jnp.concatenate(
        [
            jnp.sum(low.astype(F32), axis=0, keepdims=True),
            gain_grad,
            bias_grad,
            jnp.sum(cot_wide, axis=0, keepdims=True),
            jnp.zeros((4, WIDTH), F32),
        ],
        axis=0,
    )


def run_feed_back(place, *arrays):
    return pl.pallas_call(
        feed_back_kernel,
        out_shape=[
            jax.ShapeDtypeStruct((LEN, WIDTH), F32),
            jax.ShapeDtypeStruct((LEN, WIDTH), BF16),
            jax.ShapeDtypeStruct((8, WIDTH), F32),
            jax.ShapeDtypeStruct((WIDTH // 2, WIDTH), BF16),
            jax.ShapeDtypeStruct((WIDTH // 2, WIDTH), BF16),
        ],
        in_specs=[SMEM] + [VMEM] * len(arrays),
        out_specs=[VMEM] * 5,
        compiler_params=limit(60),
        cost_estimate=COST,
        name="feed_backward",
    )(place, *arrays)


def attend_back_kernel(place, lengths, proj, logsum, d_mixed, d_proj, bias, d_keys, d_vals):
    fill_bias(place, lengths, bias)

    def attend(p, carry):
        query_at, keys_at, vals_at = (
            rows_at(n * WIDTH + p * GROUP, GROUP, GROUP) for n in range(3)
        )
        d_keys[...] = jnp.zeros_like(d_keys)
        d_vals[...] = jnp.zeros_like(d_vals)
        for i, start in enumerate(WINDOWS):
            here_rows, near = pl.ds(i * 64, 64), pl.ds(start, SPAN)
            query = four_heads(proj[here_rows, query_at] * HEAD_DIM ** (-0.5))
            keys, vals = proj[near, keys_at], proj[near, vals_at]
            d_mix = four_heads(d_mixed[here_rows, query_at])
            probs = jnp.exp(dot_nt(keys, query) + bias[i] - logsum[pl.ds(p * 8 + i, 1), :])
            d_probs = dot_nt(vals, d_mix)
            mean = jnp.sum(probs * d_probs, axis=0, keepdims=True)
            d_scores = (probs * (d_probs - mean)).astype(BF16)
            d_query = one_of_four(dot_tn(d_scores, keys)) * HEAD_DIM ** (-0.5)
            d_proj[here_rows, query_at] = d_query.astype(BF16)
            d_keys[near, :] += dot(d_scores, query)
            d_vals[near, :] += dot(probs.astype(BF16), d_mix)
        d_proj[:, keys_at] = d_keys[...].astype(BF16)
        d_proj[:, vals_at] = d_vals[...].astype(BF16)
        return carry

    lax.fori_loop(0, HEADS // 4, attend, 0)


def run_attend_back(place, lengths, proj, logsum, d_mixed):
    return pl.pallas_call(
        attend_back_kernel,
        out_shape=jax.ShapeDtypeStruct((LEN, 3 * WIDTH), BF16),
        in_specs=[SMEM, SMEM] + [VMEM] * 3,
        out_specs=VMEM,
        scratch_shapes=[
            pltpu.VMEM((8, SPAN, GROUP), F32),
            pltpu.VMEM((LEN, GROUP), F32),
            pltpu.VMEM((LEN, GROUP), F32),
        ],
        compiler_params=limit(60),
        cost_estimate=COST,
        name="attention_backward",
    )(place, lengths, proj, logsum, d_mixed)


def project_back_kernel(place, tokens, d_proj, rows, grads_two, in_bias, *refs):
    pieces = refs[:16]
    d_act, give, keep, made_give, made_keep, weight, natural, sems = refs[16:]
    copies = piece_copies(row_slots(place), pieces, weight, sems, 0, (0, 3 * WIDTH))
    for copy in copies:
        copy.start()
    hat, unused = normed(tokens[...].astype(F32))
    act = (hat * rows[0:1, :] + rows[1:2, :]).astype(BF16)
    outs = []

    def write(start, size):
        for made, out in ((made_give, give), (made_keep, keep)):
            at = pl.ds(start, size)
            outs.append(
                pltpu.make_async_copy(made.at[:, at], out.at[:, at], sems.at[16 + len(outs)])
            )
            outs[-1].start()

    for n in range(9):
        at = pl.ds(n * 256, 256)
        made_give[:, at], made_keep[:, at] = split_rows(place, dot_tn(act, d_proj[:, at]))
        if n % 3 == 2:
            write((n - 2) * 256, WIDTH)
    for copy in copies:
        copy.wait()
    for n in range(3):
        at = pl.ds(n * 256, 256)
        d_act[:, at] = dot_nt(d_proj[...], weight[at, :])
    made = jnp.concatenate(
        [
            jnp.sum(d_act[...] * hat, axis=0, keepdims=True),
            jnp.sum(d_act[...], axis=0, keepdims=True),
            jnp.sum(d_proj[:, :WIDTH].astype(F32), axis=0, keepdims=True),
            jnp.sum(d_proj[:, 2 * WIDTH :].astype(F32), axis=0, keepdims=True),
            grads_two[:4, :],
            jnp.zeros((120, WIDTH), F32),
        ],
        axis=0,
    )
    natural[...] = made.T
    for n in range(64):
        natural[n * 12 : n * 12 + 1, 16:64] = in_bias[:, n * 48 : (n + 1) * 48]
    at = pl.ds(3 * WIDTH, 128)
    made_give[:, at], made_keep[:, at] = split_rows(place, natural[...])
    write(3 * WIDTH, 128)
    for copy in outs:
        copy.wait()


def run_project_back(place, tokens, d_proj, rows, grads_two, in_bias, pieces):
    half = (WIDTH // 2, CHUNK_ONE)
    return pl.pallas_call(
        project_back_kernel,
        out_shape=[
            jax.ShapeDtypeStruct((LEN, WIDTH), F32),
            jax.ShapeDtypeStruct(half, BF16),
            jax.ShapeDtypeStruct(half, BF16),
        ],
        in_specs=[SMEM] + [VMEM] * 5 + [ANY] * 16,
        out_specs=[VMEM, ANY, ANY],
        scratch_shapes=[
            pltpu.VMEM(half, BF16),
            pltpu.VMEM(half, BF16),
            pltpu.VMEM((WIDTH, 3 * WIDTH), BF16),
            pltpu.VMEM((WIDTH, 128), F32),
            pltpu.SemaphoreType.DMA((24,)),
        ],
        compiler_params=limit(60),
        cost_estimate=COST,
        name="project_backward",
    )(place, tokens, d_proj, rows, grads_two, in_bias, *pieces)


def input_grad_kernel(tokens, d_act, g1, rows, d_input):
    hat, scale = normed(tokens[...].astype(F32))
    d_in, unused, unused = norm_back(d_act[...], hat, scale, rows[0:1, :])
    d_input[...] = g1[...] + d_in


def run_input_grad(tokens, d_act, g1, rows):
    return pl.pallas_call(
        input_grad_kernel,
        out_shape=jax.ShapeDtypeStruct((LEN, WIDTH), F32),
        in_specs=[VMEM] * 4,
        out_specs=VMEM,
        compiler_params=limit(60),
        cost_estimate=COST,
        name="input_gradient",
    )(tokens, d_act, g1, rows)


def run_split(name, place, arrays, plan):
    drafts = plan(0, 0, 0, 1)
    shapes = [
        (sum(count for count, unused in parts), HALF, sum(width for width, unused in parts[0][1]))
        for unused, parts in drafts
    ]
    buffers = [
        pltpu.VMEM((count, HALF, width), arrays[i].dtype)
        for unused, parts in drafts
        for count, segments in parts
        for width, sources in segments
        for i, unused, unused in sources
    ]

    def kernel(place_ref, *refs):
        refs = list(refs)
        ins, outs, held, made = (
            [refs.pop(0) for unused in group] for group in (arrays, shapes, buffers, shapes)
        )
        in_sems, out_sems = refs
        unused, y, z, x, sign = places(place_ref)
        plans, copies = plan(y, z, x, sign), []
        for unused, parts in plans:
            for unused, segments in parts:
                for width, sources in segments:
                    for i, index, column in sources:
                        if not isinstance(column, int):
                            column = pl.multiple_of(column, 128)
                        n = len(copies)
                        copies.append(
                            pltpu.make_async_copy(
                                ins[i].at[(*index, slice(None), pl.ds(column, width))],
                                held[n],
                                in_sems.at[n],
                            )
                        )
                        copies[-1].start()
        n, writes = 0, []
        for o, (kind, parts) in enumerate(plans):
            row = 0
            for count, segments in parts:
                column = 0
                for width, sources in segments:
                    total = None
                    for unused in sources:
                        copies[n].wait()
                        value = held[n][...].astype(F32)
                        total = value if total is None else total + value
                        n += 1
                    made[o][row : row + count, :, column : column + width] = total.astype(kind)
                    column += width
                row += count
            writes.append(pltpu.make_async_copy(made[o], outs[o], out_sems.at[o]))
            writes[-1].start()
        for write in writes:
            write.wait()

    return pl.pallas_call(
        kernel,
        out_shape=[jax.ShapeDtypeStruct(s, kind) for s, (kind, unused) in zip(shapes, drafts)],
        in_specs=[SMEM] + [ANY] * len(arrays),
        out_specs=[ANY] * len(shapes),
        scratch_shapes=buffers
        + [pltpu.VMEM(s, kind) for s, (kind, unused) in zip(shapes, drafts)]
        + [pltpu.SemaphoreType.DMA((len(buffers),)), pltpu.SemaphoreType.DMA((len(shapes),))],
        compiler_params=limit(60),
        cost_estimate=COST,
        name=name,
    )(place, *arrays)


def shards(tokens, lengths, g1, s1, wqkv, qb, vb, wo, ob, g2, s2, w1, bi1, w2, b2, cotangent):
    y, z, x, core, sign = here()
    place = jnp.stack([core, lax.axis_index("dp") * 64 + lax.axis_index("fsdp"), y, z, x])
    lengths = lengths.T
    pieces, backs = gather(
        lambda: pack((g1, s1, qb, vb, ob, g2, s2, b2), bi1, wqkv, w1, wo), w2
    )
    proj, mixed, logsum, in_bias, rows = run_first(place, lengths, tokens, pieces)
    hidden, hat, scale, d_act, in_bias_grad, w_out, give_i, keep_i, give_b, keep_b = run_feed(
        place, tokens, mixed, cotangent, rows, in_bias, pieces, backs
    )
    got_i, got_b = send(give_i, CORES), send(give_b, CORES)
    d_middle, d_mixed, grads_two, give_o, keep_o = run_feed_back(
        place, cotangent, hat, scale, d_act, rows, mixed, w_out
    )
    d_mixed, give_o, got_i, got_b = all_done(d_mixed, give_o, got_i, got_b)
    got_o = send(give_o, CORES)

    blocks = lambda a, *lead: a.reshape(*lead, HALF, a.shape[-1])
    whole = (slice(None),)

    def cores(y, z, x, sign):
        own_in = lambda at: [
            (4, [(n, [(i, (pl.ds(at * 4, 4),), 0) for i in ids]) for n, ids in wide])
        ]
        wide = ((FF, (0, 1)), (WIDTH, (2, 3)))
        own_back = lambda at, first=0, count=8: [
            (count, [(WIDTH, [(i, (pl.ds(first, count), at), 0) for i in (4, 5)])])
        ]
        return [
            (BF16, own_in(1 - y)),
            (BF16, own_back(around(x, 2), 0, 4)),
            (BF16, own_back(around(x, 2), 4, 4)),
            (BF16, own_in(y)),
            (BF16, own_back(around(x, 1))),
            (BF16, own_back(around(x, 3))),
            (BF16, own_back(x)),
        ]

    theirs, far_up, far_down, mine, up, down, own_b = run_split(
        "sum_cores",
        place,
        [blocks(a, 8) for a in (keep_i, got_i, keep_o, got_o)]
        + [blocks(a, 8, 4) for a in (keep_b, got_b)],
        cores,
    )
    d_mixed, theirs, far_up, far_down = all_done(d_mixed, theirs, far_up, far_down)
    from_y, near_up, near_down = (
        send(theirs, Y_RING),
        send(far_up, X_BY[1]),
        send(far_down, X_BY[3]),
    )
    d_proj = run_attend_back(place, lengths, proj, logsum, d_mixed)
    d_proj, from_y, near_up, near_down = all_done(d_proj, from_y, near_up, near_down)

    def after_attention(y, z, x, sign):
        both = lambda at: [(1, [(CHUNK_TWO, [(i, (pl.ds(at, 1),), 0) for i in (0, 1)])])]
        part = lambda *sources: (4, [(WIDTH, [(i, (pl.ds(at, 4),), 0) for i, at in sources])])
        return [
            (BF16, both(around(z, 1))),
            (BF16, both(around(z, 3))),
            (BF16, both(around(z, 2))),
            (BF16, [part((2, 0), (3, 0)), part((2, 4))]),
            (BF16, [part((4, 0)), part((4, 4), (5, 0))]),
            (BF16, both(z)),
        ]

    *parts, up, down, own_i = run_split(
        "sum_y", place, (mine, from_y, up, near_up, down, near_down), after_attention
    )
    d_proj, up, down, *parts = all_done(d_proj, up, down, *parts)
    from_z_i = [send(p, Z_BY[k]) for p, k in zip(parts, (1, 3, 2))]
    from_x = [send(up, X_BY[1]), send(down, X_BY[3])]
    d_act, give_q, keep_q = run_project_back(
        place, tokens, d_proj, rows, grads_two, in_bias_grad, pieces
    )
    d_act, give_q, keep_q, from_x, from_z_i = all_done(d_act, give_q, keep_q, from_x, from_z_i)
    got_q = send(give_q, CORES)

    def back_along_z(y, z, x, sign):
        part = lambda at: (1, [(WIDTH, [(i, (pl.ds(at, 1),), 0) for i in range(3)])])
        return [(BF16, [part(around(z, k)), part(4 + around(z, k))]) for k in (1, 3, 2, 0)]

    *parts, own_b = run_split("sum_x", place, (own_b, *from_x), back_along_z)
    from_z = [send(p, Z_BY[k]) for p, k in zip(parts, (1, 3, 2))]

    def cores_rest(y, z, x, sign):
        result = []
        for row, k in YZ_ORDER:
            at = (y * (1 - row) + (1 - y) * row) * 4 + around(z, k)
            result.append((BF16, [(1, [(CHUNK_ONE, [(n, (pl.ds(at, 1),), 0) for n in (0, 1)])])]))
        return result

    *parts, own = run_split(
        "sum_cores_rest", place, [blocks(a, 8) for a in (keep_q, got_q)], cores_rest
    )
    d_act, own, own_b, *rest = all_done(d_act, own, own_b, *parts, *from_z)
    parts, from_z = rest[:7], rest[7:]
    from_yz = [send(p, YZ_BY[at]) for p, at in zip(parts, YZ_ORDER)]
    d_input = run_input_grad(tokens, d_act, d_middle, rows)
    total_b = own_b.astype(F32) + sum(p.astype(F32) for p in from_z)
    from_y = send(pick(total_b, 1 - y).astype(BF16), Y_RING)
    back_share = pick(total_b, y) + from_y.astype(F32)
    d_input, own, back_share, *from_yz = all_done(d_input, own, back_share, *from_yz)

    def last_sum(y, z, x, sign):
        total = lambda width, ids: (width, [(i, whole, 0) for i in ids])
        return [(BF16, [(1, [total(CHUNK_ONE, range(8)), total(CHUNK_TWO, range(8, 12))])])]

    (share,) = run_split("sum_z", place, (own, *from_yz, own_i, *from_z_i), last_sum)
    share, back_share = over_replicas(to_owner(share)), over_replicas(back_share)
    own = share[:, 3 * WIDTH : CHUNK_ONE]
    return (
        hidden,
        d_input,
        own[:, 0],
        own[:, 1],
        share[:, : 3 * WIDTH],
        own[:, 2],
        own[:, 3],
        share[:, CHUNK_ONE + FF :],
        own[:, 4],
        own[:, 5],
        own[:, 6],
        share[:, CHUNK_ONE : CHUNK_ONE + FF],
        own[0, 16:64],
        back_share,
        own[:, 7],
    )


def solution(mesh):
    rows, whole = P(AXES, None), P()
    vector, matrix = P("fsdp"), P("fsdp", None)
    weights = (
        vector, vector, matrix, vector, vector, matrix, vector,
        vector, vector, matrix, vector, matrix, vector,
    )
    return jax.shard_map(
        shards,
        mesh=mesh,
        in_specs=(rows, whole, *weights, rows),
        out_specs=(rows, rows, *weights),
        check_vma=False,
    )
```

```python
import itertools

import jax
import jax.numpy as jnp
import numpy as np
from jax import lax
from jax.experimental import pallas as pl
from jax.experimental.pallas import tpu as pltpu
from jax.sharding import PartitionSpec as P

HEADS = 12
HEAD_DIM = 64
LEN = 512
WIDTH = 768
FF = 3072
AXES = ("dp", "fsdp")
F32 = jnp.float32
BF16 = jnp.bfloat16

EVERY = [(y, z, x, c) for y in range(4) for z in range(4) for x in range(4) for c in range(2)]


def index_of(y, z, x, c):
    y, z, x, c = y % 4, z % 4, x % 4, c % 2
    return (y // 2) * 64 + (((y % 2) * 4 + z) * 4 + x) * 2 + c


def moves(by, by_second=None):
    steps = (by, by if by_second is None else by_second)
    return [(index_of(*at), index_of(*(a + s for a, s in zip(at, steps[at[3]])))) for at in EVERY]


Y_RING = moves((1, 0, 0, 0), (-1, 0, 0, 0))
Z_RING = moves((0, 1, 0, 0), (0, -1, 0, 0))
X_RING = moves((0, 0, 1, 0), (0, 0, -1, 0))
Z_BY = {k: moves((0, k, 0, 0)) for k in (1, 2, 3)}
CORES = moves((0, 0, 0, 1))
REPLICA = moves((2, 0, 0, 0))
SPREAD = [
    [
        (index_of(y, z, x, c), index_of(y, z, 2 * (x % 2) + c - k, x // 2))
        for y, z, x, c in EVERY
    ]
    for k in range(4)
]
COLLECT = [[(b, a) for a, b in pairs] for pairs in SPREAD]


def send(array, pairs):
    return lax.ppermute(array, AXES, pairs)


def here():
    at = lax.axis_index("fsdp")
    core, x, z, y = at % 2, (at // 2) % 4, (at // 8) % 4, at // 32
    return y, z, x, core, 1 - 2 * core


def pick(array, at, axis=0):
    return lax.dynamic_index_in_dim(array, at, axis, keepdims=False)


YZ = [(row, z) for row in range(2) for z in range(4)]
YZ_ORDER = [(0, 2), (1, 0), (0, 1), (0, 3), (1, 1), (1, 3), (1, 2), (0, 0)]
YZ_BY = {(row, z): moves((row, z, 0, 0), (-row, z, 0, 0)) for row, z in YZ}
X_BY = {k: moves((0, 0, k, 0)) for k in (1, 2, 3)}


def half_block(shard):
    x = here()[2]
    got = [send(shard, SPREAD[k]) for k in range(4)]
    ring = jnp.stack(got + got[:3])
    return lax.dynamic_slice_in_dim(ring, (4 - x) % 4, 4, 0).reshape(48, shard.shape[1])


def all_done(*arrays):
    return lax.optimization_barrier(arrays)


PAD = 16


def gather(pack_shard, back, place):
    by_z = [send(back, Z_BY[k]) for k in (1, 2, 3)]
    shard, place, *by_z = all_done(pack_shard(), place, *by_z)
    quad = jnp.concatenate([back, *by_z], axis=0)
    by_y = send(quad, Y_RING)
    own = [half_block(shard)]
    quads = [jnp.concatenate([quad, by_y, jnp.zeros((PAD, WIDTH), BF16)], axis=0)]
    side, over_own, over_side = [], [], []
    for t in range(4):
        now = [own[t], *side[t - 1 : t]]
        if t < 3:
            now.append(quads[t])
        now = all_done(*now)
        if t < 3:
            quads.append(send(now[-1], X_RING))
            own.append(send(now[0], Z_RING))
        side.append(send(now[0], Y_RING))
        if t:
            over_side.append(send(now[1], CORES))
        over_own.append(send(now[0], CORES))
        done = [own[-1], side[-1], over_own[-1]]
        if t < 3:
            done.append(quads[-1])
        if t:
            done.append(over_side[-1])
        done = list(all_done(*done))
        own[-1], side[-1], over_own[-1] = done[:3]
        if t < 3:
            quads[-1] = done[3]
        if t:
            over_side[-1] = done[-1]
    over_side.append(send(side[3], CORES))
    over_side[3], *quads = all_done(over_side[3], *quads)
    backs = quads + [send(q, CORES) for q in quads]
    return own + side + over_own + over_side, backs, place


def over_replicas(share):
    share = lax.reduce_precision(share, 8, 7)
    return share + send(share.astype(BF16), REPLICA).astype(F32)


def to_owner(total):
    x = here()[2]
    pieces = total.reshape(4, 12, total.shape[-1])
    return sum(send(pick(pieces, (x + k) % 4), COLLECT[k]).astype(F32) for k in range(4))


HALF = 48
BLOCKS = WIDTH // (2 * HALF)
WINDOWS = (0, 0, 64, 128, 192, 256, 320, 320)
SPAN = 192
GROUP = 4 * HEAD_DIM
VMEM = pl.BlockSpec(memory_space=pltpu.VMEM)
SMEM = pl.BlockSpec(memory_space=pltpu.SMEM)
ANY = pl.BlockSpec(memory_space=pl.ANY)


def limit(mib):
    return pltpu.CompilerParams(vmem_limit_bytes=mib * 1024 * 1024)


COST = pl.CostEstimate(flops=10**6, bytes_accessed=10**5, transcendentals=0)
URGENT = pl.CostEstimate(flops=3 * 10**10, bytes_accessed=10**5, transcendentals=0)
CHUNK_ONE = 3 * WIDTH + 128
CHUNK_TWO = FF + WIDTH


def dot(a, b):
    return lax.dot_general(a, b, (((1,), (0,)), ((), ())), preferred_element_type=F32)


def dot_nt(a, b):
    return lax.dot_general(a, b, (((1,), (1,)), ((), ())), preferred_element_type=F32)


def dot_tn(a, b):
    return lax.dot_general(a, b, (((0,), (0,)), ((), ())), preferred_element_type=F32)


def normed(values):
    centre = values - jnp.mean(values, axis=-1, keepdims=True)
    scale = lax.rsqrt(jnp.mean(centre * centre, axis=-1, keepdims=True) + 1e-05)
    return centre * scale, scale


def norm_back(d_out, hat, scale, gain):
    expand = d_out * gain
    d_in = scale * (
        expand
        - jnp.mean(expand, axis=-1, keepdims=True)
        - hat * jnp.mean(expand * hat, axis=-1, keepdims=True)
    )
    gain_grad = jnp.sum(d_out * hat, axis=0, keepdims=True)
    return d_in, gain_grad, jnp.sum(d_out, axis=0, keepdims=True)


def rows_at(start, size, step=16):
    return pl.ds(pl.multiple_of(start, step), size)


def places(place_ref):
    core, y, z, x = (place_ref[n] for n in (0, 2, 3, 4))
    return core, y, z, x, 1 - 2 * core


def around(at, step):
    return lax.rem(at + step + 8, 4)


def row_slots(place_ref):
    core, y, z, x, sign = places(place_ref)
    return [
        (row * 4 + around(z, -way * t)) * 2 + half
        for half, way in ((core, sign), (1 - core, -sign))
        for row in (y, 1 - y)
        for t in range(4)
    ]


def back_slots(place_ref):
    core, y, z, x, sign = places(place_ref)
    return [
        ((row * 4 + around(z, -k)) * 4 + around(x, -way * t)) * 2 + half
        for half, way in ((core, sign), (1 - core, -sign))
        for t in range(4)
        for row in (y, 1 - y)
        for k in range(4)
    ]


def piece_copies(slots, pieces, target, sems, first, columns=None):
    copies = []
    each = len(slots) // len(pieces)
    for n, slot in enumerate(slots):
        source = pieces[n // each].at[pl.ds(n % each * HALF, HALF), :]
        if columns is not None:
            source = source.at[:, pl.ds(*columns)]
        copies.append(
            pltpu.make_async_copy(
                source, target.at[rows_at(slot * HALF, HALF)], sems.at[first + n]
            )
        )
    return copies


def split_rows(place_ref, made):
    columns = made.shape[1]
    parts = made.astype(BF16).reshape(BLOCKS, 2, HALF, columns)
    first, second = (parts[:, n].reshape(BLOCKS * HALF, columns) for n in range(2))
    low = place_ref[0] == 0
    return lax.select(low, second, first), lax.select(low, first, second)


def head_of(rows):
    return lax.broadcasted_iota(jnp.int32, (rows, GROUP), 1) // HEAD_DIM


def four_heads(group):
    head, zero = head_of(group.shape[0]), jnp.zeros_like(group)
    return jnp.concatenate([jnp.where(head == h, group, zero) for h in range(4)], axis=0)


def one_of_four(wide):
    n = wide.shape[0] // 4
    head, result = head_of(n), wide[:n]
    for h in range(1, 4):
        result = jnp.where(head == h, wide[h * n : (h + 1) * n], result)
    return result


def fill_bias(place_ref, lengths_ref, bias):
    ends, total = [], jnp.int32(0)
    for k in range(16):
        total = total + lengths_ref[k, place_ref[1]]
        ends.append(total)

    def ids(at):
        return sum((at >= end).astype(jnp.int32) for end in ends)

    keys = ids(lax.broadcasted_iota(jnp.int32, (LEN, 1), 0))
    lane = lax.broadcasted_iota(jnp.int32, (1, GROUP), 1) % HEAD_DIM
    for i, start in enumerate(WINDOWS):
        same = keys[start : start + SPAN] == ids(lane + i * 64)
        bias[i] = jnp.where(same, 0.0, -1e30).astype(F32)


def pack_kernel(*refs):
    vectors, in_bias, w_qkv, w_in, w_out, out, made = refs[:8], *refs[8:]
    rows = w_qkv.shape[0]
    same = lax.broadcasted_iota(jnp.int32, (rows, rows), 0) == lax.broadcasted_iota(
        jnp.int32, (rows, rows), 1
    )
    lane = lax.broadcasted_iota(jnp.int32, (rows, 128), 1)
    total = jnp.zeros((rows, 128), F32)
    for i, ref in enumerate(vectors):
        wide = jnp.broadcast_to(ref[...].astype(F32), (rows, rows))
        column = jnp.sum(jnp.where(same, wide, 0.0), axis=1, keepdims=True)
        total = jnp.where(lane == i, column, total)
    made[...] = total
    made[0:1, 16:64] = in_bias[...].astype(F32)
    out[:, : 3 * WIDTH] = w_qkv[...]
    out[:, 3 * WIDTH : CHUNK_ONE] = made[...].astype(BF16)
    out[:, CHUNK_ONE : CHUNK_ONE + FF] = w_in[...]
    out[:, CHUNK_ONE + FF :] = w_out[...]


def pack(vectors, in_bias, w_qkv, w_in, w_out):
    return pl.pallas_call(
        pack_kernel,
        out_shape=jax.ShapeDtypeStruct((12, CHUNK_ONE + CHUNK_TWO), BF16),
        in_specs=[VMEM] * 12,
        out_specs=VMEM,
        scratch_shapes=[pltpu.VMEM((12, 128), F32)],
        name="pack",
    )(*(v.reshape(1, 12) for v in vectors), in_bias.reshape(1, 48), w_qkv, w_in, w_out)


def first_kernel(place, lengths, tokens, *refs):
    pieces = refs[:16]
    proj_out, mixed, logsum, in_bias, rows, proj, weight, vec, wide, bias, sems = refs[16:]
    slots = row_slots(place)
    copies = piece_copies(slots, pieces, weight, sems, 0, (0, 3 * WIDTH))
    copies += piece_copies(slots, pieces, vec, sems, 16, (3 * WIDTH, 128))
    for copy in copies:
        copy.start()
    fill_bias(place, lengths, bias)
    hat, unused = normed(tokens[...].astype(F32))
    for copy in copies:
        copy.wait()
    wide[...] = vec[...].astype(F32)
    rows[...] = wide[...].T[:16]
    for n in range(64):
        in_bias[:, n * 48 : (n + 1) * 48] = wide[n * 12 : n * 12 + 1, 16:64]
    act = (hat * rows[0:1, :] + rows[1:2, :]).astype(BF16)
    for n in range(9):
        at = pl.ds(n * 256, 256)
        made = dot(act, weight[:, at])
        if n // 3 != 1:
            made = made + rows[2 + n // 6 : 3 + n // 6, (n % 3) * 256 : (n % 3 + 1) * 256]
        proj[:, at] = made.astype(BF16)
    out_copy = pltpu.make_async_copy(proj, proj_out, sems.at[32])
    out_copy.start()
    for p in range(HEADS // 4):
        query_at, keys_at, vals_at = (pl.ds(n * WIDTH + p * GROUP, GROUP) for n in range(3))
        for i, start in enumerate(WINDOWS):
            here_rows, near = pl.ds(i * 64, 64), pl.ds(start, SPAN)
            query = four_heads(proj[here_rows, query_at] * HEAD_DIM ** (-0.5))
            scores = dot_nt(proj[near, keys_at], query) + bias[i]
            top = jnp.max(scores, axis=0, keepdims=True)
            expo = jnp.exp(scores - top)
            total = jnp.sum(expo, axis=0, keepdims=True)
            probs = (expo * (1.0 / total)).astype(BF16)
            mixed[here_rows, query_at] = one_of_four(dot_tn(probs, proj[near, vals_at])).astype(BF16)
            logsum[p * 8 + i : p * 8 + i + 1, :] = top + jnp.log(total)
    out_copy.wait()


def run_first(place, lengths, tokens, pieces):
    return pl.pallas_call(
        first_kernel,
        out_shape=[
            jax.ShapeDtypeStruct((LEN, 3 * WIDTH), BF16),
            jax.ShapeDtypeStruct((LEN, WIDTH), BF16),
            jax.ShapeDtypeStruct((24, 256), F32),
            jax.ShapeDtypeStruct((1, FF), F32),
            jax.ShapeDtypeStruct((16, WIDTH), F32),
        ],
        in_specs=[SMEM, SMEM, VMEM] + [ANY] * 16,
        out_specs=[ANY] + [VMEM] * 4,
        scratch_shapes=[
            pltpu.VMEM((LEN, 3 * WIDTH), BF16),
            pltpu.VMEM((WIDTH, 3 * WIDTH), BF16),
            pltpu.VMEM((WIDTH, 128), BF16),
            pltpu.VMEM((WIDTH, 128), F32),
            pltpu.VMEM((8, SPAN, GROUP), F32),
            pltpu.SemaphoreType.DMA((33,)),
        ],
        compiler_params=limit(60),
        cost_estimate=COST,
        name="attention_forward",
    )(place, lengths, tokens, *pieces)


def gelu_pair(x):
    phi = 0.5 + 0.5 * lax.erf(x * 0.5**0.5)
    return x * phi, phi + x * (jnp.exp(x * (x * -0.5)) * 0.3989422804014327)


def feed_kernel(place, tokens, mixed, cot, rows, in_bias, *refs):
    pieces, backs = refs[:16], refs[16:24]
    hidden, g1, d_mixed, vector_grads, in_bias_grad = refs[24:29]
    give, keep, give_back, keep_back, give_out, keep_out = refs[29:35]
    w_out, w_in, w_back, x1, hat, scale, act, acc, d_act = refs[35:44]
    gact_0, gact_1, d_pre_0, d_pre_1 = refs[44:48]
    made_give, made_keep, made_give_back, made_keep_back, sems, out_sems = refs[48:]
    gact, d_pre = (gact_0, gact_1), (d_pre_0, d_pre_1)
    slots = row_slots(place)
    out_copies = piece_copies(slots, pieces, w_out, sems, 0, (CHUNK_ONE + FF, WIDTH))
    in_copies = piece_copies(slots, pieces, w_in, sems, 16, (CHUNK_ONE, FF))
    back_copies = piece_copies(back_slots(place), backs, w_back, sems, 32)
    for copy in out_copies + in_copies + back_copies:
        copy.start()
    for copy in out_copies:
        copy.wait()
    for n in range(3):
        at = pl.ds(n * 256, 256)
        x1[:, at] = tokens[:, at].astype(F32) + (dot(mixed[...], w_out[:, at]) + rows[4:5, at])
    hat[...], scale[...] = normed(x1[...])
    act[...] = (hat[...] * rows[5:6, :] + rows[6:7, :]).astype(BF16)
    for copy in in_copies + back_copies:
        copy.wait()

    def units(j, n):
        local, at = pl.ds(n * 256, 256), pl.ds(j * WIDTH + n * 256, 256)
        value, slope = gelu_pair(dot(act[...], w_in[:, at]) + in_bias[:, at])
        gact[j % 2][:, local] = value.astype(BF16)
        d_low = (dot_nt(cot[...], w_back[at, :]) * slope).astype(BF16)
        d_pre[j % 2][:, local] = d_low
        in_bias_grad[:, at] = jnp.sum(d_low.astype(F32), axis=0, keepdims=True)

    def sums(j, n):
        at, block, half = pl.ds(n * 256, 256), pl.ds(j * WIDTH, WIDTH), pl.ds(j * 384, 384)
        forward = dot(gact[j % 2][...], w_back[block, at])
        backward = dot_nt(d_pre[j % 2][...], w_in[at, block])
        acc[:, at] = forward if j == 0 else acc[:, at] + forward
        d_act[:, at] = backward if j == 0 else d_act[:, at] + backward
        wide = pl.ds(j * WIDTH + n * 256, 256)
        made_give[:, wide], made_keep[:, wide] = split_rows(
            place, dot_tn(act[...], d_pre[j % 2][:, at])
        )
        made_give_back[half, at], made_keep_back[half, at] = split_rows(
            place, dot_tn(gact[j % 2][...], cot[:, at])
        )

    copies = []
    for j in range(5):
        for n in range(3):
            if j < 4:
                units(j, n)
            if j:
                sums(j - 1, n)
        if j:
            wide, half = pl.ds((j - 1) * WIDTH, WIDTH), pl.ds((j - 1) * 384, 384)
            for made, out, at in (
                (made_give, give, (slice(None), wide)),
                (made_give_back, give_back, (half, slice(None))),
                (made_keep, keep, (slice(None), wide)),
                (made_keep_back, keep_back, (half, slice(None))),
            ):
                copies.append(
                    pltpu.make_async_copy(made.at[at], out.at[at], out_sems.at[len(copies)])
                )
                copies[-1].start()
    hidden[...] = (x1[...] + (acc[...] + rows[7:8, :])).astype(BF16)
    cot_wide = cot[...].astype(F32)
    d_in, gain_grad, bias_grad = norm_back(d_act[...], hat[...], scale[...], rows[5:6, :])
    total = cot_wide + d_in
    g1[...] = total
    low = total.astype(BF16)
    for n in range(3):
        at = pl.ds(n * 256, 256)
        d_mixed[:, at] = dot_nt(low, w_out[at, :]).astype(BF16)
        give_out[:, at], keep_out[:, at] = split_rows(
            place, dot_tn(mixed[...], low[:, n * 256 : (n + 1) * 256])
        )
    vector_grads[...] = jnp.concatenate(
        [
            jnp.sum(low.astype(F32), axis=0, keepdims=True),
            gain_grad,
            bias_grad,
            jnp.sum(cot_wide, axis=0, keepdims=True),
            jnp.zeros((4, WIDTH), F32),
        ],
        axis=0,
    )
    for copy in copies:
        copy.wait()


def run_feed(place, tokens, mixed, cot, rows, in_bias, pieces, backs):
    wide, tall, low = (WIDTH // 2, FF), (FF // 2, WIDTH), (LEN, WIDTH)
    return pl.pallas_call(
        feed_kernel,
        out_shape=[
            jax.ShapeDtypeStruct(low, BF16),
            jax.ShapeDtypeStruct(low, F32),
            jax.ShapeDtypeStruct(low, BF16),
            jax.ShapeDtypeStruct((8, WIDTH), F32),
            jax.ShapeDtypeStruct((1, FF), F32),
            jax.ShapeDtypeStruct(wide, BF16),
            jax.ShapeDtypeStruct(wide, BF16),
            jax.ShapeDtypeStruct(tall, BF16),
            jax.ShapeDtypeStruct(tall, BF16),
            jax.ShapeDtypeStruct((WIDTH // 2, WIDTH), BF16),
            jax.ShapeDtypeStruct((WIDTH // 2, WIDTH), BF16),
        ],
        in_specs=[SMEM] + [VMEM] * 5 + [ANY] * 24,
        out_specs=[VMEM] * 5 + [ANY] * 4 + [VMEM] * 2,
        scratch_shapes=[
            pltpu.VMEM((WIDTH, WIDTH), BF16),
            pltpu.VMEM((WIDTH, FF), BF16),
            pltpu.VMEM((FF, WIDTH), BF16),
            pltpu.VMEM(low, F32),
            pltpu.VMEM(low, F32),
            pltpu.VMEM((LEN, 1), F32),
            pltpu.VMEM(low, BF16),
            pltpu.VMEM(low, F32),
            pltpu.VMEM(low, F32),
        ]
        + [pltpu.VMEM(low, BF16)] * 4
        + [pltpu.VMEM(wide, BF16)] * 2
        + [pltpu.VMEM(tall, BF16)] * 2
        + [pltpu.SemaphoreType.DMA((96,)), pltpu.SemaphoreType.DMA((16,))],
        compiler_params=limit(60),
        cost_estimate=COST,
        name="feed_forward",
    )(place, tokens, mixed, cot, rows, in_bias, *pieces, *backs)


def attend_back_kernel(place, lengths, proj, logsum, d_mixed, d_proj, bias, d_keys, d_vals):
    fill_bias(place, lengths, bias)

    def attend(p, carry):
        query_at, keys_at, vals_at = (
            rows_at(n * WIDTH + p * GROUP, GROUP, GROUP) for n in range(3)
        )
        d_keys[...] = jnp.zeros_like(d_keys)
        d_vals[...] = jnp.zeros_like(d_vals)
        for i, start in enumerate(WINDOWS):
            here_rows, near = pl.ds(i * 64, 64), pl.ds(start, SPAN)
            query = four_heads(proj[here_rows, query_at] * HEAD_DIM ** (-0.5))
            keys, vals = proj[near, keys_at], proj[near, vals_at]
            d_mix = four_heads(d_mixed[here_rows, query_at])
            probs = jnp.exp(dot_nt(keys, query) + bias[i] - logsum[pl.ds(p * 8 + i, 1), :])
            d_probs = dot_nt(vals, d_mix)
            mean = jnp.sum(probs * d_probs, axis=0, keepdims=True)
            d_scores = (probs * (d_probs - mean)).astype(BF16)
            d_query = one_of_four(dot_tn(d_scores, keys)) * HEAD_DIM ** (-0.5)
            d_proj[here_rows, query_at] = d_query.astype(BF16)
            d_keys[near, :] += dot(d_scores, query)
            d_vals[near, :] += dot(probs.astype(BF16), d_mix)
        d_proj[:, keys_at] = d_keys[...].astype(BF16)
        d_proj[:, vals_at] = d_vals[...].astype(BF16)
        return carry

    lax.fori_loop(0, HEADS // 4, attend, 0)


def run_attend_back(place, lengths, proj, logsum, d_mixed):
    return pl.pallas_call(
        attend_back_kernel,
        out_shape=jax.ShapeDtypeStruct((LEN, 3 * WIDTH), BF16),
        in_specs=[SMEM, SMEM] + [VMEM] * 3,
        out_specs=VMEM,
        scratch_shapes=[
            pltpu.VMEM((8, SPAN, GROUP), F32),
            pltpu.VMEM((LEN, GROUP), F32),
            pltpu.VMEM((LEN, GROUP), F32),
        ],
        compiler_params=limit(60),
        cost_estimate=COST,
        name="attention_backward",
    )(place, lengths, proj, logsum, d_mixed)


FIRST_HALVES = np.arange(WIDTH, dtype=np.int32).reshape(BLOCKS, 2, HALF)[:, 0].reshape(1, -1)


def project_back_kernel(place, tokens, tokens_over, d_proj, d_over, rows, grads_two, in_bias, *refs):
    order, pieces = refs[0], refs[1:17]
    d_act, theirs, mine, give, keep, made_theirs, made_mine, weight, natural, sems = refs[17:]
    core, y, unused, unused, unused = places(place)
    copies = piece_copies(row_slots(place), pieces, weight, sems, 0, (0, 3 * WIDTH))
    for copy in copies:
        copy.start()
    half = order[...] + HALF * core
    half = (lax.broadcasted_iota(jnp.int32, (WIDTH, WIDTH // 2), 0) == half).astype(F32)
    half = half.astype(BF16)
    hat, unused = normed(tokens[...].astype(F32))
    hat_over, unused = normed(tokens_over[...].astype(F32))
    act, act_over = (
        dot((h * rows[0:1, :] + rows[1:2, :]).astype(BF16), half).astype(BF16)
        for h in (hat, hat_over)
    )
    outs = []
    for n in range(9):
        at = pl.ds(n * 256, 256)
        made = (dot_tn(act, d_proj[:, at]) + dot_tn(act_over, d_over[:, at])).astype(BF16)
        low, high = made[: 4 * HALF], made[4 * HALF :]
        made_theirs[:, at] = lax.select(y == 0, high, low)
        made_mine[:, at] = lax.select(y == 0, low, high)
        if n % 3 == 2:
            wide = pl.ds((n - 2) * 256, WIDTH)
            for made, out in ((made_theirs, theirs), (made_mine, mine)):
                outs.append(
                    pltpu.make_async_copy(
                        made.at[:, wide], out.at[:, wide], sems.at[16 + len(outs)]
                    )
                )
                outs[-1].start()
    for copy in copies:
        copy.wait()
    for n in range(3):
        at = pl.ds(n * 256, 256)
        d_act[:, at] = dot_nt(d_proj[...], weight[at, :])
    made = jnp.concatenate(
        [
            jnp.sum(d_act[...] * hat, axis=0, keepdims=True),
            jnp.sum(d_act[...], axis=0, keepdims=True),
            jnp.sum(d_proj[:, :WIDTH].astype(F32), axis=0, keepdims=True),
            jnp.sum(d_proj[:, 2 * WIDTH :].astype(F32), axis=0, keepdims=True),
            grads_two[:4, :],
            jnp.zeros((120, WIDTH), F32),
        ],
        axis=0,
    )
    natural[...] = made.T
    for n in range(64):
        natural[n * 12 : n * 12 + 1, 16:64] = in_bias[:, n * 48 : (n + 1) * 48]
    give[...], keep[...] = split_rows(place, natural[...])
    for copy in outs:
        copy.wait()


def run_project_back(place, tokens, tokens_over, d_proj, d_over, rows, grads_two, in_bias, pieces):
    part, vector = (4 * HALF, 3 * WIDTH), (WIDTH // 2, 128)
    return pl.pallas_call(
        project_back_kernel,
        out_shape=[
            jax.ShapeDtypeStruct((LEN, WIDTH), F32),
            jax.ShapeDtypeStruct(part, BF16),
            jax.ShapeDtypeStruct(part, BF16),
            jax.ShapeDtypeStruct(vector, BF16),
            jax.ShapeDtypeStruct(vector, BF16),
        ],
        in_specs=[SMEM] + [VMEM] * 8 + [ANY] * 16,
        out_specs=[VMEM, ANY, ANY, VMEM, VMEM],
        scratch_shapes=[
            pltpu.VMEM(part, BF16),
            pltpu.VMEM(part, BF16),
            pltpu.VMEM((WIDTH, 3 * WIDTH), BF16),
            pltpu.VMEM((WIDTH, 128), F32),
            pltpu.SemaphoreType.DMA((22,)),
        ],
        compiler_params=limit(60),
        cost_estimate=COST,
        name="project_backward",
    )(
        place,
        tokens,
        tokens_over,
        d_proj,
        d_over,
        rows,
        grads_two,
        in_bias,
        jnp.asarray(FIRST_HALVES),
        *pieces,
    )


def input_grad_kernel(tokens, d_act, g1, rows, d_input):
    hat, scale = normed(tokens[...].astype(F32))
    d_in, unused, unused = norm_back(d_act[...], hat, scale, rows[0:1, :])
    d_input[...] = g1[...] + d_in


def run_input_grad(tokens, d_act, g1, rows):
    return pl.pallas_call(
        input_grad_kernel,
        out_shape=jax.ShapeDtypeStruct((LEN, WIDTH), F32),
        in_specs=[VMEM] * 4,
        out_specs=VMEM,
        compiler_params=limit(60),
        cost_estimate=COST,
        name="input_gradient",
    )(tokens, d_act, g1, rows)


def after_kernel(place, *refs):
    for n in range(place.shape[0]):
        refs[-1][n] = place[n]


def run_after(place, *arrays):
    return pl.pallas_call(
        after_kernel,
        out_shape=jax.ShapeDtypeStruct(place.shape, place.dtype),
        in_specs=[SMEM] + [ANY] * len(arrays),
        out_specs=SMEM,
        cost_estimate=URGENT,
        name="after",
    )(place, *arrays)


def run_split(name, place, arrays, plan, cost=COST):
    drafts = plan(0, 0, 0, 1)
    shapes = [
        (sum(count for count, unused in parts), HALF, sum(width for width, unused in parts[0][1]))
        for unused, parts in drafts
    ]
    buffers = [
        pltpu.VMEM((count, HALF, width), arrays[i].dtype)
        for unused, parts in drafts
        for count, segments in parts
        for width, sources in segments
        for i, unused, unused in sources
    ]

    def kernel(place_ref, *refs):
        refs = list(refs)
        ins, outs, held, made = (
            [refs.pop(0) for unused in group] for group in (arrays, shapes, buffers, shapes)
        )
        in_sems, out_sems = refs
        unused, y, z, x, sign = places(place_ref)
        plans, copies = plan(y, z, x, sign), []
        for unused, parts in plans:
            for unused, segments in parts:
                for width, sources in segments:
                    for i, index, column in sources:
                        if not isinstance(column, int):
                            column = pl.multiple_of(column, 128)
                        n = len(copies)
                        copies.append(
                            pltpu.make_async_copy(
                                ins[i].at[(*index, slice(None), pl.ds(column, width))],
                                held[n],
                                in_sems.at[n],
                            )
                        )
                        copies[-1].start()
        n, writes = 0, []
        for o, (kind, parts) in enumerate(plans):
            row = 0
            for count, segments in parts:
                column = 0
                for width, sources in segments:
                    total = None
                    for unused in sources:
                        copies[n].wait()
                        value = held[n][...].astype(F32)
                        total = value if total is None else total + value
                        n += 1
                    made[o][row : row + count, :, column : column + width] = total.astype(kind)
                    column += width
                row += count
            writes.append(pltpu.make_async_copy(made[o], outs[o], out_sems.at[o]))
            writes[-1].start()
        for write in writes:
            write.wait()

    return pl.pallas_call(
        kernel,
        out_shape=[jax.ShapeDtypeStruct(s, kind) for s, (kind, unused) in zip(shapes, drafts)],
        in_specs=[SMEM] + [ANY] * len(arrays),
        out_specs=[ANY] * len(shapes),
        scratch_shapes=buffers
        + [pltpu.VMEM(s, kind) for s, (kind, unused) in zip(shapes, drafts)]
        + [pltpu.SemaphoreType.DMA((len(buffers),)), pltpu.SemaphoreType.DMA((len(shapes),))],
        compiler_params=limit(60),
        cost_estimate=cost,
        name=name,
    )(place, *arrays)


def shards(tokens, lengths, g1, s1, wqkv, qb, vb, wo, ob, g2, s2, w1, bi1, w2, b2, cotangent):
    y, z, x, core, sign = here()
    place = jnp.stack([core, lax.axis_index("dp") * 64 + lax.axis_index("fsdp"), y, z, x])
    lengths = lengths.T
    pieces, backs, place = gather(
        lambda: pack((g1, s1, qb, vb, ob, g2, s2, b2), bi1, wqkv, w1, wo), w2, place
    )
    proj, mixed, logsum, in_bias, rows = run_first(place, lengths, tokens, pieces)
    hidden, d_middle, d_mixed, grads_two, in_bias_grad, *grads = run_feed(
        place, tokens, mixed, cotangent, rows, in_bias, pieces, backs
    )
    give_i, keep_i, give_b, keep_b, give_o, keep_o = grads
    got_i, got_b, got_o = send(give_i, CORES), send(give_b, CORES), send(give_o, CORES)
    d_proj = run_attend_back(place, lengths, proj, logsum, d_mixed)
    d_proj, got_i, got_b, got_o = all_done(d_proj, got_i, got_b, got_o)
    d_over, tokens_over = send(d_proj, CORES), send(tokens, CORES)

    blocks = lambda a, *lead: a.reshape(*lead, HALF, a.shape[-1])
    whole = (slice(None),)
    wide = ((FF, (0, 1)), (WIDTH, (2, 3)))

    def own_in(at):
        return [(4, [(n, [(i, (pl.ds(at * 4, 4),), 0) for i in ids]) for n, ids in wide])]

    def own_back(at, *more):
        sources = [(i, (slice(None), at), 0) for i in (0, 1)] + [(i, whole, 0) for i in more]
        return [(BF16, [(8, [(WIDTH, sources)])])]

    sums_in = [blocks(a, 8) for a in (keep_i, got_i, keep_o, got_o)]
    sums_back = [blocks(a, 8, 4) for a in (keep_b, got_b)]
    (theirs,) = run_split(
        "sum_cores_in", place, sums_in, lambda y, z, x, sign: [(BF16, own_in(1 - y))]
    )
    from_y = send(theirs, Y_RING)
    (back_1,) = run_split(
        "sum_cores_back", place, sums_back, lambda y, z, x, sign: own_back(around(x, -sign))
    )
    d_proj, d_over, tokens_over, back_1 = all_done(d_proj, d_over, tokens_over, back_1)
    from_x = send(back_1, X_RING)
    d_act, theirs, mine_q, give_v, keep_v = run_project_back(
        place, tokens, tokens_over, d_proj, d_over, rows, grads_two, in_bias_grad, pieces
    )
    d_act, theirs, mine_q, give_v, from_y, from_x = all_done(
        d_act, theirs, mine_q, give_v, from_y, from_x
    )

    from_y_q = send(blocks(theirs, 4), Y_RING)
    got_v = send(give_v, CORES)
    add = lambda a, b: (a.astype(F32) + b.astype(F32)).astype(BF16)
    (back_2,) = run_split(
        "sum_x_2",
        place,
        (*sums_back, from_x),
        lambda y, z, x, sign: own_back(around(x, -2 * sign), 2),
    )
    from_x = send(back_2, X_RING)

    def after_y(y, z, x, sign):
        def both(at):
            own = (pl.ds(y * 4 + at, 1),)
            segments = []
            for (n, ids), column in zip(wide, (0, FF)):
                sources = [(i, own, 0) for i in ids] + [(4, (pl.ds(at, 1),), column)]
                segments.append((n, sources))
            return [(1, segments)]

        return [(BF16, both(around(z, k))) for k in (1, 3, 2, 0)]

    *parts, own_i = run_split("sum_y", place, (*sums_in, from_y), after_y)
    d_act, got_v, own_i, *parts = all_done(d_act, got_v, own_i, *parts)
    from_z_i = [send(p, Z_BY[k]) for p, k in zip(parts, (1, 3, 2))]
    kept_v = add(keep_v, got_v).reshape(2, 4, HALF, 128)
    mine_v, from_y_v = pick(kept_v, y), send(pick(kept_v, 1 - y), Y_RING)
    (back_3,) = run_split(
        "sum_x_3",
        place,
        (*sums_back, from_x),
        lambda y, z, x, sign: own_back(around(x, -3 * sign), 2),
    )
    from_x = send(back_3, X_RING)
    mine_v, from_y, from_y_v = all_done(mine_v, from_y_q, from_y_v)

    def along_z(y, z, x, sign):
        pair = lambda n, ids, at: (n, [(i, (pl.ds(at, 1),), 0) for i in ids])
        part = lambda at: [(1, [pair(3 * WIDTH, (0, 1), at), pair(128, (2, 3), at)])]
        return [(BF16, part(around(z, k))) for k in (1, 3, 2, 0)]

    *parts, own = run_split(
        "sum_y_rest", place, (blocks(mine_q, 4), from_y, mine_v, from_y_v), along_z
    )
    from_z = [send(p, Z_BY[k]) for p, k in zip(parts, (1, 3, 2))]

    def back_along_z(y, z, x, sign):
        def part(at):
            sources = [(i, (pl.ds(at, 1), x), 0) for i in (0, 1)] + [(2, (pl.ds(at, 1),), 0)]
            return (1, [(WIDTH, sources)])

        return [(BF16, [part(around(z, k)), part(4 + around(z, k))]) for k in (1, 3, 2, 0)]

    *parts, own_b = run_split("sum_x", place, (*sums_back, from_x), back_along_z)
    from_z_b = [send(p, Z_BY[k]) for p, k in zip(parts, (1, 3, 2))]
    d_input = run_input_grad(tokens, d_act, d_middle, rows)
    place = run_after(place, *from_z_i)
    place, d_input, own, own_b, *done = all_done(place, d_input, own, own_b, *from_z, *from_z_b)
    from_z, from_z_b = done[:3], done[3:]

    def last_sum(y, z, x, sign):
        total = lambda width, ids: (width, [(i, whole, 0) for i in ids])
        back = lambda at: [(1, [(WIDTH, [(i, (pl.ds(at, 1),), 0) for i in range(8, 12)])])]
        return [
            (BF16, [(1, [total(CHUNK_ONE, range(4)), total(CHUNK_TWO, range(4, 8))])]),
            (BF16, back(1 - y)),
            (BF16, back(y)),
        ]

    share, theirs, mine = run_split("sum_z", place, (own, *from_z, own_i, *from_z_i, own_b, *from_z_b), last_sum)
    from_y = send(theirs, Y_RING)
    share = to_owner(share)
    back_share = (mine.astype(F32) + from_y.astype(F32)).reshape(HALF, WIDTH)
    share, back_share = all_done(share, back_share)
    share, back_share = over_replicas(share), over_replicas(back_share)
    own = share[:, 3 * WIDTH : CHUNK_ONE]
    return (
        hidden,
        d_input,
        own[:, 0],
        own[:, 1],
        share[:, : 3 * WIDTH],
        own[:, 2],
        own[:, 3],
        share[:, CHUNK_ONE + FF :],
        own[:, 4],
        own[:, 5],
        own[:, 6],
        share[:, CHUNK_ONE : CHUNK_ONE + FF],
        own[0, 16:64],
        back_share,
        own[:, 7],
    )


def solution(mesh):
    rows, whole = P(AXES, None), P()
    vector, matrix = P("fsdp"), P("fsdp", None)
    weights = (
        vector, vector, matrix, vector, vector, matrix, vector,
        vector, vector, matrix, vector, matrix, vector,
    )
    return jax.shard_map(
        shards,
        mesh=mesh,
        in_specs=(rows, whole, *weights, rows),
        out_specs=(rows, rows, *weights),
        check_vma=False,
    )
```

```python
import itertools

import jax
import jax.numpy as jnp
import numpy as np
from jax import lax
from jax.experimental import pallas as pl
from jax.experimental.pallas import tpu as pltpu
from jax.sharding import PartitionSpec as P

HEADS = 12
HEAD_DIM = 64
LEN = 512
WIDTH = 768
FF = 3072
AXES = ("dp", "fsdp")
F32 = jnp.float32
BF16 = jnp.bfloat16

EVERY = [(y, z, x, c) for y in range(4) for z in range(4) for x in range(4) for c in range(2)]


def index_of(y, z, x, c):
    y, z, x, c = y % 4, z % 4, x % 4, c % 2
    return (y // 2) * 64 + (((y % 2) * 4 + z) * 4 + x) * 2 + c


def moves(by, by_second=None):
    steps = (by, by if by_second is None else by_second)
    return [(index_of(*at), index_of(*(a + s for a, s in zip(at, steps[at[3]])))) for at in EVERY]


Y_RING = moves((1, 0, 0, 0), (-1, 0, 0, 0))
Z_RING = moves((0, 1, 0, 0), (0, -1, 0, 0))
X_RING = moves((0, 0, 1, 0), (0, 0, -1, 0))
Z_BY = {k: moves((0, k, 0, 0)) for k in (1, 2, 3)}
CORES = moves((0, 0, 0, 1))
REPLICA = moves((2, 0, 0, 0))


def send(array, pairs):
    return lax.ppermute(array, AXES, pairs)


def here():
    at = lax.axis_index("fsdp")
    core, x, z, y = at % 2, (at // 2) % 4, (at // 8) % 4, at // 32
    return y, z, x, core, 1 - 2 * core


def pick(array, at, axis=0):
    return lax.dynamic_index_in_dim(array, at, axis, keepdims=False)


YZ = [(row, z) for row in range(2) for z in range(4)]
YZ_ORDER = [(0, 2), (1, 0), (0, 1), (0, 3), (1, 1), (1, 3), (1, 2), (0, 0)]
YZ_BY = {(row, z): moves((row, z, 0, 0), (-row, z, 0, 0)) for row, z in YZ}
X_BY = {k: moves((0, 0, k, 0)) for k in (1, 2, 3)}


def half_block(shard):
    y, z, x, core, sign = here()
    got = [send(shard, X_BY[k]) for k in (3, 2, 1)]
    ring = jnp.stack([*got, shard, *got])
    mine, give = (
        lax.dynamic_slice_in_dim(ring, (7 - x + 2 * c) % 4, 2, 0) for c in (core, 1 - core)
    )
    got = send(give, CORES)
    low = core == 0
    both = jnp.stack([jnp.where(low, mine, got), jnp.where(low, got, mine)], axis=1)
    return both.reshape(48, shard.shape[1])


def all_done(*arrays):
    return lax.optimization_barrier(arrays)


PAD = 16


def gather(pack_shard, back, place):
    by_z = [send(back, Z_BY[k]) for k in (1, 2, 3)]
    shard, place, *by_z = all_done(pack_shard(), place, *by_z)
    quad = jnp.concatenate([back, *by_z], axis=0)
    by_y = send(quad, Y_RING)
    own = [half_block(shard)]
    quads = [jnp.concatenate([quad, by_y, jnp.zeros((PAD, WIDTH), BF16)], axis=0)]
    side, over_own, over_side = [], [], []
    for t in range(4):
        now = [own[t], *side[t - 1 : t]]
        if t < 3:
            now.append(quads[t])
        now = all_done(*now)
        if t < 3:
            quads.append(send(now[-1], X_RING))
            own.append(send(now[0], Z_RING))
        side.append(send(now[0], Y_RING))
        if t:
            over_side.append(send(now[1], CORES))
        over_own.append(send(now[0], CORES))
        done = [own[-1], side[-1], over_own[-1]]
        if t < 3:
            done.append(quads[-1])
        if t:
            done.append(over_side[-1])
        done = list(all_done(*done))
        own[-1], side[-1], over_own[-1] = done[:3]
        if t < 3:
            quads[-1] = done[3]
        if t:
            over_side[-1] = done[-1]
    over_side.append(send(side[3], CORES))
    over_side[3], *quads = all_done(over_side[3], *quads)
    backs = quads + [send(q, CORES) for q in quads]
    return own + side + over_own + over_side, backs, place


def over_replicas(share):
    share = lax.reduce_precision(share, 8, 7)
    return share + send(share.astype(BF16), REPLICA).astype(F32)


def to_owner(total):
    y, z, x, core, sign = here()
    parts = total.reshape(2, 2, 12, total.shape[-1])
    keep, got = pick(parts, core, 1), send(pick(parts, 1 - core, 1), CORES)
    low = core == 0
    ring = jnp.concatenate([jnp.where(low, keep, got), jnp.where(low, got, keep)], axis=0)
    share = pick(ring, x).astype(F32)
    for k in (1, 2, 3):
        share = share + send(pick(ring, (x + k) % 4), X_BY[k]).astype(F32)
    return share


HALF = 48
BLOCKS = WIDTH // (2 * HALF)
WINDOWS = (0, 0, 64, 128, 192, 256, 320, 320)
SPAN = 192
GROUP = 4 * HEAD_DIM
VMEM = pl.BlockSpec(memory_space=pltpu.VMEM)
SMEM = pl.BlockSpec(memory_space=pltpu.SMEM)
ANY = pl.BlockSpec(memory_space=pl.ANY)


def limit(mib):
    return pltpu.CompilerParams(vmem_limit_bytes=mib * 1024 * 1024)


COST = pl.CostEstimate(flops=10**6, bytes_accessed=10**5, transcendentals=0)
URGENT = pl.CostEstimate(flops=3 * 10**10, bytes_accessed=10**5, transcendentals=0)
CHUNK_ONE = 3 * WIDTH + 128
CHUNK_TWO = FF + WIDTH


def dot(a, b):
    return lax.dot_general(a, b, (((1,), (0,)), ((), ())), preferred_element_type=F32)


def dot_nt(a, b):
    return lax.dot_general(a, b, (((1,), (1,)), ((), ())), preferred_element_type=F32)


def dot_tn(a, b):
    return lax.dot_general(a, b, (((0,), (0,)), ((), ())), preferred_element_type=F32)


def normed(values):
    centre = values - jnp.mean(values, axis=-1, keepdims=True)
    scale = lax.rsqrt(jnp.mean(centre * centre, axis=-1, keepdims=True) + 1e-05)
    return centre * scale, scale


def norm_back(d_out, hat, scale, gain):
    expand = d_out * gain
    d_in = scale * (
        expand
        - jnp.mean(expand, axis=-1, keepdims=True)
        - hat * jnp.mean(expand * hat, axis=-1, keepdims=True)
    )
    gain_grad = jnp.sum(d_out * hat, axis=0, keepdims=True)
    return d_in, gain_grad, jnp.sum(d_out, axis=0, keepdims=True)


def rows_at(start, size, step=16):
    return pl.ds(pl.multiple_of(start, step), size)


def places(place_ref):
    core, y, z, x = (place_ref[n] for n in (0, 2, 3, 4))
    return core, y, z, x, 1 - 2 * core


def around(at, step):
    return lax.rem(at + step + 8, 4)


def row_slots(place_ref):
    core, y, z, x, sign = places(place_ref)
    return [
        (row * 4 + around(z, -way * t)) * 2 + half
        for half, way in ((core, sign), (1 - core, -sign))
        for row in (y, 1 - y)
        for t in range(4)
    ]


def back_slots(place_ref):
    core, y, z, x, sign = places(place_ref)
    return [
        ((row * 4 + around(z, -k)) * 4 + around(x, -way * t)) * 2 + half
        for half, way in ((core, sign), (1 - core, -sign))
        for t in range(4)
        for row in (y, 1 - y)
        for k in range(4)
    ]


def piece_copies(slots, pieces, target, sems, first, columns=None):
    copies = []
    each = len(slots) // len(pieces)
    for n, slot in enumerate(slots):
        source = pieces[n // each].at[pl.ds(n % each * HALF, HALF), :]
        if columns is not None:
            source = source.at[:, pl.ds(*columns)]
        copies.append(
            pltpu.make_async_copy(
                source, target.at[rows_at(slot * HALF, HALF)], sems.at[first + n]
            )
        )
    return copies


def split_rows(place_ref, made):
    columns = made.shape[1]
    parts = made.astype(BF16).reshape(BLOCKS, 2, HALF, columns)
    first, second = (parts[:, n].reshape(BLOCKS * HALF, columns) for n in range(2))
    low = place_ref[0] == 0
    return lax.select(low, second, first), lax.select(low, first, second)


def head_of(rows):
    return lax.broadcasted_iota(jnp.int32, (rows, GROUP), 1) // HEAD_DIM


def four_heads(group):
    head, zero = head_of(group.shape[0]), jnp.zeros_like(group)
    return jnp.concatenate([jnp.where(head == h, group, zero) for h in range(4)], axis=0)


def one_of_four(wide):
    n = wide.shape[0] // 4
    head, result = head_of(n), wide[:n]
    for h in range(1, 4):
        result = jnp.where(head == h, wide[h * n : (h + 1) * n], result)
    return result


def fill_bias(place_ref, lengths_ref, bias):
    ends, total = [], jnp.int32(0)
    for k in range(16):
        total = total + lengths_ref[k, place_ref[1]]
        ends.append(total)

    def ids(at):
        return sum((at >= end).astype(jnp.int32) for end in ends)

    keys = ids(lax.broadcasted_iota(jnp.int32, (LEN, 1), 0))
    lane = lax.broadcasted_iota(jnp.int32, (1, GROUP), 1) % HEAD_DIM
    for i, start in enumerate(WINDOWS):
        same = keys[start : start + SPAN] == ids(lane + i * 64)
        bias[i] = jnp.where(same, 0.0, -1e30).astype(F32)


def pack_kernel(*refs):
    vectors, in_bias, w_qkv, w_in, w_out, out, made = refs[:8], *refs[8:]
    rows = w_qkv.shape[0]
    same = lax.broadcasted_iota(jnp.int32, (rows, rows), 0) == lax.broadcasted_iota(
        jnp.int32, (rows, rows), 1
    )
    lane = lax.broadcasted_iota(jnp.int32, (rows, 128), 1)
    total = jnp.zeros((rows, 128), F32)
    for i, ref in enumerate(vectors):
        wide = jnp.broadcast_to(ref[...].astype(F32), (rows, rows))
        column = jnp.sum(jnp.where(same, wide, 0.0), axis=1, keepdims=True)
        total = jnp.where(lane == i, column, total)
    made[...] = total
    made[0:1, 16:64] = in_bias[...].astype(F32)
    out[:, : 3 * WIDTH] = w_qkv[...]
    out[:, 3 * WIDTH : CHUNK_ONE] = made[...].astype(BF16)
    out[:, CHUNK_ONE : CHUNK_ONE + FF] = w_in[...]
    out[:, CHUNK_ONE + FF :] = w_out[...]


def pack(vectors, in_bias, w_qkv, w_in, w_out):
    return pl.pallas_call(
        pack_kernel,
        out_shape=jax.ShapeDtypeStruct((12, CHUNK_ONE + CHUNK_TWO), BF16),
        in_specs=[VMEM] * 12,
        out_specs=VMEM,
        scratch_shapes=[pltpu.VMEM((12, 128), F32)],
        name="pack",
    )(*(v.reshape(1, 12) for v in vectors), in_bias.reshape(1, 48), w_qkv, w_in, w_out)


def first_kernel(place, lengths, tokens, *refs):
    pieces = refs[:16]
    proj_out, mixed, logsum, in_bias, rows, proj, weight, vec, wide, bias, sems = refs[16:]
    slots = row_slots(place)
    copies = piece_copies(slots, pieces, weight, sems, 0, (0, 3 * WIDTH))
    copies += piece_copies(slots, pieces, vec, sems, 16, (3 * WIDTH, 128))
    for copy in copies:
        copy.start()
    fill_bias(place, lengths, bias)
    hat, unused = normed(tokens[...].astype(F32))
    for copy in copies:
        copy.wait()
    wide[...] = vec[...].astype(F32)
    rows[...] = wide[...].T[:16]
    for n in range(64):
        in_bias[:, n * 48 : (n + 1) * 48] = wide[n * 12 : n * 12 + 1, 16:64]
    act = (hat * rows[0:1, :] + rows[1:2, :]).astype(BF16)
    for n in range(9):
        at = pl.ds(n * 256, 256)
        made = dot(act, weight[:, at])
        if n // 3 != 1:
            made = made + rows[2 + n // 6 : 3 + n // 6, (n % 3) * 256 : (n % 3 + 1) * 256]
        proj[:, at] = made.astype(BF16)
    out_copy = pltpu.make_async_copy(proj, proj_out, sems.at[32])
    out_copy.start()
    for p in range(HEADS // 4):
        query_at, keys_at, vals_at = (pl.ds(n * WIDTH + p * GROUP, GROUP) for n in range(3))
        for i, start in enumerate(WINDOWS):
            here_rows, near = pl.ds(i * 64, 64), pl.ds(start, SPAN)
            query = four_heads(proj[here_rows, query_at] * HEAD_DIM ** (-0.5))
            scores = dot_nt(proj[near, keys_at], query) + bias[i]
            top = jnp.max(scores, axis=0, keepdims=True)
            expo = jnp.exp(scores - top)
            total = jnp.sum(expo, axis=0, keepdims=True)
            probs = (expo * (1.0 / total)).astype(BF16)
            mixed[here_rows, query_at] = one_of_four(dot_tn(probs, proj[near, vals_at])).astype(BF16)
            logsum[p * 8 + i : p * 8 + i + 1, :] = top + jnp.log(total)
    out_copy.wait()


def run_first(place, lengths, tokens, pieces):
    return pl.pallas_call(
        first_kernel,
        out_shape=[
            jax.ShapeDtypeStruct((LEN, 3 * WIDTH), BF16),
            jax.ShapeDtypeStruct((LEN, WIDTH), BF16),
            jax.ShapeDtypeStruct((24, 256), F32),
            jax.ShapeDtypeStruct((1, FF), F32),
            jax.ShapeDtypeStruct((16, WIDTH), F32),
        ],
        in_specs=[SMEM, SMEM, VMEM] + [ANY] * 16,
        out_specs=[ANY] + [VMEM] * 4,
        scratch_shapes=[
            pltpu.VMEM((LEN, 3 * WIDTH), BF16),
            pltpu.VMEM((WIDTH, 3 * WIDTH), BF16),
            pltpu.VMEM((WIDTH, 128), BF16),
            pltpu.VMEM((WIDTH, 128), F32),
            pltpu.VMEM((8, SPAN, GROUP), F32),
            pltpu.SemaphoreType.DMA((33,)),
        ],
        compiler_params=limit(60),
        cost_estimate=COST,
        name="attention_forward",
    )(place, lengths, tokens, *pieces)


def gelu_pair(x):
    phi = 0.5 + 0.5 * lax.erf(x * 0.5**0.5)
    return x * phi, phi + x * (jnp.exp(x * (x * -0.5)) * 0.3989422804014327)


def feed_kernel(place, tokens, mixed, cot, rows, in_bias, *refs):
    pieces, backs = refs[:16], refs[16:24]
    hidden, g1, d_mixed, vector_grads, in_bias_grad = refs[24:29]
    give, keep, give_back, keep_back, give_out, keep_out = refs[29:35]
    w_out, w_in, w_back, x1, hat, scale, act, acc, d_act = refs[35:44]
    gact_0, gact_1, d_pre_0, d_pre_1 = refs[44:48]
    made_give, made_keep, made_give_back, made_keep_back, sems, out_sems = refs[48:]
    gact, d_pre = (gact_0, gact_1), (d_pre_0, d_pre_1)
    slots = row_slots(place)
    out_copies = piece_copies(slots, pieces, w_out, sems, 0, (CHUNK_ONE + FF, WIDTH))
    in_copies = piece_copies(slots, pieces, w_in, sems, 16, (CHUNK_ONE, FF))
    back_copies = piece_copies(back_slots(place), backs, w_back, sems, 32)
    for copy in out_copies + in_copies + back_copies:
        copy.start()
    for copy in out_copies:
        copy.wait()
    for n in range(3):
        at = pl.ds(n * 256, 256)
        x1[:, at] = tokens[:, at].astype(F32) + (dot(mixed[...], w_out[:, at]) + rows[4:5, at])
    hat[...], scale[...] = normed(x1[...])
    act[...] = (hat[...] * rows[5:6, :] + rows[6:7, :]).astype(BF16)
    for copy in in_copies + back_copies:
        copy.wait()

    def units(j, n):
        local, at = pl.ds(n * 256, 256), pl.ds(j * WIDTH + n * 256, 256)
        value, slope = gelu_pair(dot(act[...], w_in[:, at]) + in_bias[:, at])
        gact[j % 2][:, local] = value.astype(BF16)
        d_low = (dot_nt(cot[...], w_back[at, :]) * slope).astype(BF16)
        d_pre[j % 2][:, local] = d_low
        in_bias_grad[:, at] = jnp.sum(d_low.astype(F32), axis=0, keepdims=True)

    def sums(j, n):
        at, block, half = pl.ds(n * 256, 256), pl.ds(j * WIDTH, WIDTH), pl.ds(j * 384, 384)
        forward = dot(gact[j % 2][...], w_back[block, at])
        backward = dot_nt(d_pre[j % 2][...], w_in[at, block])
        acc[:, at] = forward if j == 0 else acc[:, at] + forward
        d_act[:, at] = backward if j == 0 else d_act[:, at] + backward
        wide = pl.ds(j * WIDTH + n * 256, 256)
        made_give[:, wide], made_keep[:, wide] = split_rows(
            place, dot_tn(act[...], d_pre[j % 2][:, at])
        )
        made_give_back[half, at], made_keep_back[half, at] = split_rows(
            place, dot_tn(gact[j % 2][...], cot[:, at])
        )

    copies = []
    for j in range(5):
        for n in range(3):
            if j < 4:
                units(j, n)
            if j:
                sums(j - 1, n)
        if j:
            wide, half = pl.ds((j - 1) * WIDTH, WIDTH), pl.ds((j - 1) * 384, 384)
            for made, out, at in (
                (made_give, give, (slice(None), wide)),
                (made_give_back, give_back, (half, slice(None))),
                (made_keep, keep, (slice(None), wide)),
                (made_keep_back, keep_back, (half, slice(None))),
            ):
                copies.append(
                    pltpu.make_async_copy(made.at[at], out.at[at], out_sems.at[len(copies)])
                )
                copies[-1].start()
    hidden[...] = (x1[...] + (acc[...] + rows[7:8, :])).astype(BF16)
    cot_wide = cot[...].astype(F32)
    d_in, gain_grad, bias_grad = norm_back(d_act[...], hat[...], scale[...], rows[5:6, :])
    total = cot_wide + d_in
    g1[...] = total
    low = total.astype(BF16)
    for n in range(3):
        at = pl.ds(n * 256, 256)
        d_mixed[:, at] = dot_nt(low, w_out[at, :]).astype(BF16)
        give_out[:, at], keep_out[:, at] = split_rows(
            place, dot_tn(mixed[...], low[:, n * 256 : (n + 1) * 256])
        )
    vector_grads[...] = jnp.concatenate(
        [
            jnp.sum(low.astype(F32), axis=0, keepdims=True),
            gain_grad,
            bias_grad,
            jnp.sum(cot_wide, axis=0, keepdims=True),
            jnp.zeros((4, WIDTH), F32),
        ],
        axis=0,
    )
    for copy in copies:
        copy.wait()


def run_feed(place, tokens, mixed, cot, rows, in_bias, pieces, backs):
    wide, tall, low = (WIDTH // 2, FF), (FF // 2, WIDTH), (LEN, WIDTH)
    return pl.pallas_call(
        feed_kernel,
        out_shape=[
            jax.ShapeDtypeStruct(low, BF16),
            jax.ShapeDtypeStruct(low, F32),
            jax.ShapeDtypeStruct(low, BF16),
            jax.ShapeDtypeStruct((8, WIDTH), F32),
            jax.ShapeDtypeStruct((1, FF), F32),
            jax.ShapeDtypeStruct(wide, BF16),
            jax.ShapeDtypeStruct(wide, BF16),
            jax.ShapeDtypeStruct(tall, BF16),
            jax.ShapeDtypeStruct(tall, BF16),
            jax.ShapeDtypeStruct((WIDTH // 2, WIDTH), BF16),
            jax.ShapeDtypeStruct((WIDTH // 2, WIDTH), BF16),
        ],
        in_specs=[SMEM] + [VMEM] * 5 + [ANY] * 24,
        out_specs=[VMEM] * 5 + [ANY] * 4 + [VMEM] * 2,
        scratch_shapes=[
            pltpu.VMEM((WIDTH, WIDTH), BF16),
            pltpu.VMEM((WIDTH, FF), BF16),
            pltpu.VMEM((FF, WIDTH), BF16),
            pltpu.VMEM(low, F32),
            pltpu.VMEM(low, F32),
            pltpu.VMEM((LEN, 1), F32),
            pltpu.VMEM(low, BF16),
            pltpu.VMEM(low, F32),
            pltpu.VMEM(low, F32),
        ]
        + [pltpu.VMEM(low, BF16)] * 4
        + [pltpu.VMEM(wide, BF16)] * 2
        + [pltpu.VMEM(tall, BF16)] * 2
        + [pltpu.SemaphoreType.DMA((96,)), pltpu.SemaphoreType.DMA((16,))],
        compiler_params=limit(60),
        cost_estimate=COST,
        name="feed_forward",
    )(place, tokens, mixed, cot, rows, in_bias, *pieces, *backs)


def attend_back_kernel(place, lengths, proj, logsum, d_mixed, d_proj, bias, d_keys, d_vals):
    fill_bias(place, lengths, bias)

    def attend(p, carry):
        query_at, keys_at, vals_at = (
            rows_at(n * WIDTH + p * GROUP, GROUP, GROUP) for n in range(3)
        )
        d_keys[...] = jnp.zeros_like(d_keys)
        d_vals[...] = jnp.zeros_like(d_vals)
        for i, start in enumerate(WINDOWS):
            here_rows, near = pl.ds(i * 64, 64), pl.ds(start, SPAN)
            query = four_heads(proj[here_rows, query_at] * HEAD_DIM ** (-0.5))
            keys, vals = proj[near, keys_at], proj[near, vals_at]
            d_mix = four_heads(d_mixed[here_rows, query_at])
            probs = jnp.exp(dot_nt(keys, query) + bias[i] - logsum[pl.ds(p * 8 + i, 1), :])
            d_probs = dot_nt(vals, d_mix)
            mean = jnp.sum(probs * d_probs, axis=0, keepdims=True)
            d_scores = (probs * (d_probs - mean)).astype(BF16)
            d_query = one_of_four(dot_tn(d_scores, keys)) * HEAD_DIM ** (-0.5)
            d_proj[here_rows, query_at] = d_query.astype(BF16)
            d_keys[near, :] += dot(d_scores, query)
            d_vals[near, :] += dot(probs.astype(BF16), d_mix)
        d_proj[:, keys_at] = d_keys[...].astype(BF16)
        d_proj[:, vals_at] = d_vals[...].astype(BF16)
        return carry

    lax.fori_loop(0, HEADS // 4, attend, 0)


def run_attend_back(place, lengths, proj, logsum, d_mixed):
    return pl.pallas_call(
        attend_back_kernel,
        out_shape=jax.ShapeDtypeStruct((LEN, 3 * WIDTH), BF16),
        in_specs=[SMEM, SMEM] + [VMEM] * 3,
        out_specs=VMEM,
        scratch_shapes=[
            pltpu.VMEM((8, SPAN, GROUP), F32),
            pltpu.VMEM((LEN, GROUP), F32),
            pltpu.VMEM((LEN, GROUP), F32),
        ],
        compiler_params=limit(60),
        cost_estimate=COST,
        name="attention_backward",
    )(place, lengths, proj, logsum, d_mixed)


FIRST_HALVES = np.arange(WIDTH, dtype=np.int32).reshape(BLOCKS, 2, HALF)[:, 0].reshape(1, -1)


def project_back_kernel(place, tokens, tokens_over, d_proj, d_over, rows, grads_two, in_bias, *refs):
    order, pieces = refs[0], refs[1:17]
    d_act, theirs, mine, give, keep, made_theirs, made_mine, weight, natural, sems = refs[17:]
    core, y, unused, unused, unused = places(place)
    copies = piece_copies(row_slots(place), pieces, weight, sems, 0, (0, 3 * WIDTH))
    for copy in copies:
        copy.start()
    half = order[...] + HALF * core
    half = (lax.broadcasted_iota(jnp.int32, (WIDTH, WIDTH // 2), 0) == half).astype(F32)
    half = half.astype(BF16)
    hat, unused = normed(tokens[...].astype(F32))
    hat_over, unused = normed(tokens_over[...].astype(F32))
    act, act_over = (
        dot((h * rows[0:1, :] + rows[1:2, :]).astype(BF16), half).astype(BF16)
        for h in (hat, hat_over)
    )
    outs = []
    for n in range(9):
        at = pl.ds(n * 256, 256)
        made = (dot_tn(act, d_proj[:, at]) + dot_tn(act_over, d_over[:, at])).astype(BF16)
        low, high = made[: 4 * HALF], made[4 * HALF :]
        made_theirs[:, at] = lax.select(y == 0, high, low)
        made_mine[:, at] = lax.select(y == 0, low, high)
        if n % 3 == 2:
            wide = pl.ds((n - 2) * 256, WIDTH)
            for made, out in ((made_theirs, theirs), (made_mine, mine)):
                outs.append(
                    pltpu.make_async_copy(
                        made.at[:, wide], out.at[:, wide], sems.at[16 + len(outs)]
                    )
                )
                outs[-1].start()
    for copy in copies:
        copy.wait()
    for n in range(3):
        at = pl.ds(n * 256, 256)
        d_act[:, at] = dot_nt(d_proj[...], weight[at, :])
    made = jnp.concatenate(
        [
            jnp.sum(d_act[...] * hat, axis=0, keepdims=True),
            jnp.sum(d_act[...], axis=0, keepdims=True),
            jnp.sum(d_proj[:, :WIDTH].astype(F32), axis=0, keepdims=True),
            jnp.sum(d_proj[:, 2 * WIDTH :].astype(F32), axis=0, keepdims=True),
            grads_two[:4, :],
            jnp.zeros((120, WIDTH), F32),
        ],
        axis=0,
    )
    natural[...] = made.T
    for n in range(64):
        natural[n * 12 : n * 12 + 1, 16:64] = in_bias[:, n * 48 : (n + 1) * 48]
    give[...], keep[...] = split_rows(place, natural[...])
    for copy in outs:
        copy.wait()


def run_project_back(place, tokens, tokens_over, d_proj, d_over, rows, grads_two, in_bias, pieces):
    part, vector = (4 * HALF, 3 * WIDTH), (WIDTH // 2, 128)
    return pl.pallas_call(
        project_back_kernel,
        out_shape=[
            jax.ShapeDtypeStruct((LEN, WIDTH), F32),
            jax.ShapeDtypeStruct(part, BF16),
            jax.ShapeDtypeStruct(part, BF16),
            jax.ShapeDtypeStruct(vector, BF16),
            jax.ShapeDtypeStruct(vector, BF16),
        ],
        in_specs=[SMEM] + [VMEM] * 8 + [ANY] * 16,
        out_specs=[VMEM, ANY, ANY, VMEM, VMEM],
        scratch_shapes=[
            pltpu.VMEM(part, BF16),
            pltpu.VMEM(part, BF16),
            pltpu.VMEM((WIDTH, 3 * WIDTH), BF16),
            pltpu.VMEM((WIDTH, 128), F32),
            pltpu.SemaphoreType.DMA((22,)),
        ],
        compiler_params=limit(60),
        cost_estimate=COST,
        name="project_backward",
    )(
        place,
        tokens,
        tokens_over,
        d_proj,
        d_over,
        rows,
        grads_two,
        in_bias,
        jnp.asarray(FIRST_HALVES),
        *pieces,
    )


def input_grad_kernel(tokens, d_act, g1, rows, d_input):
    hat, scale = normed(tokens[...].astype(F32))
    d_in, unused, unused = norm_back(d_act[...], hat, scale, rows[0:1, :])
    d_input[...] = g1[...] + d_in


def run_input_grad(tokens, d_act, g1, rows):
    return pl.pallas_call(
        input_grad_kernel,
        out_shape=jax.ShapeDtypeStruct((LEN, WIDTH), F32),
        in_specs=[VMEM] * 4,
        out_specs=VMEM,
        compiler_params=limit(60),
        cost_estimate=COST,
        name="input_gradient",
    )(tokens, d_act, g1, rows)


def after_kernel(place, *refs):
    for n in range(place.shape[0]):
        refs[-1][n] = place[n]


def run_after(place, *arrays):
    return pl.pallas_call(
        after_kernel,
        out_shape=jax.ShapeDtypeStruct(place.shape, place.dtype),
        in_specs=[SMEM] + [ANY] * len(arrays),
        out_specs=SMEM,
        cost_estimate=URGENT,
        name="after",
    )(place, *arrays)


def run_split(name, place, arrays, plan, cost=COST):
    drafts = plan(0, 0, 0, 1)
    shapes = [
        (sum(count for count, unused in parts), HALF, sum(width for width, unused in parts[0][1]))
        for unused, parts in drafts
    ]
    buffers = [
        pltpu.VMEM((count, HALF, width), arrays[i].dtype)
        for unused, parts in drafts
        for count, segments in parts
        for width, sources in segments
        for i, unused, unused in sources
    ]

    def kernel(place_ref, *refs):
        refs = list(refs)
        ins, outs, held, made = (
            [refs.pop(0) for unused in group] for group in (arrays, shapes, buffers, shapes)
        )
        in_sems, out_sems = refs
        unused, y, z, x, sign = places(place_ref)
        plans, copies = plan(y, z, x, sign), []
        for unused, parts in plans:
            for unused, segments in parts:
                for width, sources in segments:
                    for i, index, column in sources:
                        if not isinstance(column, int):
                            column = pl.multiple_of(column, 128)
                        n = len(copies)
                        copies.append(
                            pltpu.make_async_copy(
                                ins[i].at[(*index, slice(None), pl.ds(column, width))],
                                held[n],
                                in_sems.at[n],
                            )
                        )
                        copies[-1].start()
        n, writes = 0, []
        for o, (kind, parts) in enumerate(plans):
            row = 0
            for count, segments in parts:
                column = 0
                for width, sources in segments:
                    total = None
                    for unused in sources:
                        copies[n].wait()
                        value = held[n][...].astype(F32)
                        total = value if total is None else total + value
                        n += 1
                    made[o][row : row + count, :, column : column + width] = total.astype(kind)
                    column += width
                row += count
            writes.append(pltpu.make_async_copy(made[o], outs[o], out_sems.at[o]))
            writes[-1].start()
        for write in writes:
            write.wait()

    return pl.pallas_call(
        kernel,
        out_shape=[jax.ShapeDtypeStruct(s, kind) for s, (kind, unused) in zip(shapes, drafts)],
        in_specs=[SMEM] + [ANY] * len(arrays),
        out_specs=[ANY] * len(shapes),
        scratch_shapes=buffers
        + [pltpu.VMEM(s, kind) for s, (kind, unused) in zip(shapes, drafts)]
        + [pltpu.SemaphoreType.DMA((len(buffers),)), pltpu.SemaphoreType.DMA((len(shapes),))],
        compiler_params=limit(60),
        cost_estimate=cost,
        name=name,
    )(place, *arrays)


def shards(tokens, lengths, g1, s1, wqkv, qb, vb, wo, ob, g2, s2, w1, bi1, w2, b2, cotangent):
    y, z, x, core, sign = here()
    place = jnp.stack([core, lax.axis_index("dp") * 64 + lax.axis_index("fsdp"), y, z, x])
    lengths = lengths.T
    pieces, backs, place = gather(
        lambda: pack((g1, s1, qb, vb, ob, g2, s2, b2), bi1, wqkv, w1, wo), w2, place
    )
    proj, mixed, logsum, in_bias, rows = run_first(place, lengths, tokens, pieces)
    hidden, d_middle, d_mixed, grads_two, in_bias_grad, *grads = run_feed(
        place, tokens, mixed, cotangent, rows, in_bias, pieces, backs
    )
    give_i, keep_i, give_b, keep_b, give_o, keep_o = grads
    got_i, got_b, got_o = send(give_i, CORES), send(give_b, CORES), send(give_o, CORES)
    d_proj = run_attend_back(place, lengths, proj, logsum, d_mixed)
    d_proj, got_i, got_b, got_o = all_done(d_proj, got_i, got_b, got_o)
    d_over, tokens_over = send(d_proj, CORES), send(tokens, CORES)

    blocks = lambda a, *lead: a.reshape(*lead, HALF, a.shape[-1])
    whole = (slice(None),)
    wide = ((FF, (0, 1)), (WIDTH, (2, 3)))

    def own_in(at):
        return [(4, [(n, [(i, (pl.ds(at * 4, 4),), 0) for i in ids]) for n, ids in wide])]

    def own_back(at, *more):
        sources = [(i, (slice(None), at), 0) for i in (0, 1)] + [(i, whole, 0) for i in more]
        return [(BF16, [(8, [(WIDTH, sources)])])]

    sums_in = [blocks(a, 8) for a in (keep_i, got_i, keep_o, got_o)]
    sums_back = [blocks(a, 8, 4) for a in (keep_b, got_b)]
    (theirs,) = run_split(
        "sum_cores_in", place, sums_in, lambda y, z, x, sign: [(BF16, own_in(1 - y))]
    )
    from_y = send(theirs, Y_RING)
    (back_1,) = run_split(
        "sum_cores_back", place, sums_back, lambda y, z, x, sign: own_back(around(x, -sign))
    )
    d_proj, d_over, tokens_over, back_1 = all_done(d_proj, d_over, tokens_over, back_1)
    from_x = send(back_1, X_RING)
    d_act, theirs, mine_q, give_v, keep_v = run_project_back(
        place, tokens, tokens_over, d_proj, d_over, rows, grads_two, in_bias_grad, pieces
    )
    d_act, theirs, mine_q, give_v, from_y, from_x = all_done(
        d_act, theirs, mine_q, give_v, from_y, from_x
    )

    from_y_q = send(blocks(theirs, 4), Y_RING)
    got_v = send(give_v, CORES)
    add = lambda a, b: (a.astype(F32) + b.astype(F32)).astype(BF16)
    (back_2,) = run_split(
        "sum_x_2",
        place,
        (*sums_back, from_x),
        lambda y, z, x, sign: own_back(around(x, -2 * sign), 2),
    )
    from_x = send(back_2, X_RING)

    def after_y(y, z, x, sign):
        def both(at):
            own = (pl.ds(y * 4 + at, 1),)
            segments = []
            for (n, ids), column in zip(wide, (0, FF)):
                sources = [(i, own, 0) for i in ids] + [(4, (pl.ds(at, 1),), column)]
                segments.append((n, sources))
            return [(1, segments)]

        return [(BF16, both(around(z, k))) for k in (1, 3, 2, 0)]

    *parts, own_i = run_split("sum_y", place, (*sums_in, from_y), after_y)
    d_act, got_v, own_i, *parts = all_done(d_act, got_v, own_i, *parts)
    from_z_i = [send(p, Z_BY[k]) for p, k in zip(parts, (1, 3, 2))]
    kept_v = add(keep_v, got_v).reshape(2, 4, HALF, 128)
    mine_v, from_y_v = pick(kept_v, y), send(pick(kept_v, 1 - y), Y_RING)
    (back_3,) = run_split(
        "sum_x_3",
        place,
        (*sums_back, from_x),
        lambda y, z, x, sign: own_back(around(x, -3 * sign), 2),
    )
    from_x = send(back_3, X_RING)
    mine_v, from_y, from_y_v = all_done(mine_v, from_y_q, from_y_v)

    def along_z(y, z, x, sign):
        pair = lambda n, ids, at: (n, [(i, (pl.ds(at, 1),), 0) for i in ids])
        part = lambda at: [(1, [pair(3 * WIDTH, (0, 1), at), pair(128, (2, 3), at)])]
        return [(BF16, part(around(z, k))) for k in (1, 3, 2, 0)]

    *parts, own = run_split(
        "sum_y_rest", place, (blocks(mine_q, 4), from_y, mine_v, from_y_v), along_z
    )
    from_z = [send(p, Z_BY[k]) for p, k in zip(parts, (1, 3, 2))]

    def back_along_z(y, z, x, sign):
        def part(at):
            sources = [(i, (pl.ds(at, 1), x), 0) for i in (0, 1)] + [(2, (pl.ds(at, 1),), 0)]
            return (1, [(WIDTH, sources)])

        return [(BF16, [part(around(z, k)), part(4 + around(z, k))]) for k in (1, 3, 2, 0)]

    *parts, own_b = run_split("sum_x", place, (*sums_back, from_x), back_along_z)
    from_z_b = [send(p, Z_BY[k]) for p, k in zip(parts, (1, 3, 2))]
    d_input = run_input_grad(tokens, d_act, d_middle, rows)
    place = run_after(place, *from_z_i)
    place, d_input, own, own_b, *done = all_done(place, d_input, own, own_b, *from_z, *from_z_b)
    from_z, from_z_b = done[:3], done[3:]

    def last_sum(y, z, x, sign):
        total = lambda width, ids: (width, [(i, whole, 0) for i in ids])
        back = lambda at: [(1, [(WIDTH, [(i, (pl.ds(at, 1),), 0) for i in range(8, 12)])])]
        return [
            (BF16, [(1, [total(CHUNK_ONE, range(4)), total(CHUNK_TWO, range(4, 8))])]),
            (BF16, back(1 - y)),
            (BF16, back(y)),
        ]

    share, theirs, mine = run_split("sum_z", place, (own, *from_z, own_i, *from_z_i, own_b, *from_z_b), last_sum)
    from_y = send(theirs, Y_RING)
    share = to_owner(share)
    back_share = (mine.astype(F32) + from_y.astype(F32)).reshape(HALF, WIDTH)
    share, back_share = all_done(share, back_share)
    share, back_share = over_replicas(share), over_replicas(back_share)
    own = share[:, 3 * WIDTH : CHUNK_ONE]
    return (
        hidden,
        d_input,
        own[:, 0],
        own[:, 1],
        share[:, : 3 * WIDTH],
        own[:, 2],
        own[:, 3],
        share[:, CHUNK_ONE + FF :],
        own[:, 4],
        own[:, 5],
        own[:, 6],
        share[:, CHUNK_ONE : CHUNK_ONE + FF],
        own[0, 16:64],
        back_share,
        own[:, 7],
    )


def solution(mesh):
    rows, whole = P(AXES, None), P()
    vector, matrix = P("fsdp"), P("fsdp", None)
    weights = (
        vector, vector, matrix, vector, vector, matrix, vector,
        vector, vector, matrix, vector, matrix, vector,
    )
    return jax.shard_map(
        shards,
        mesh=mesh,
        in_specs=(rows, whole, *weights, rows),
        out_specs=(rows, rows, *weights),
        check_vma=False,
    )
```

```python
import itertools

import jax
import jax.numpy as jnp
import numpy as np
from jax import lax
from jax.experimental import pallas as pl
from jax.experimental.pallas import tpu as pltpu
from jax.sharding import PartitionSpec as P

HEADS = 12
HEAD_DIM = 64
LEN = 512
WIDTH = 768
FF = 3072
AXES = ("dp", "fsdp")
F32 = jnp.float32
BF16 = jnp.bfloat16

EVERY = [(y, z, x, c) for y in range(4) for z in range(4) for x in range(4) for c in range(2)]


def index_of(y, z, x, c):
    y, z, x, c = y % 4, z % 4, x % 4, c % 2
    return (y // 2) * 64 + (((y % 2) * 4 + z) * 4 + x) * 2 + c


def moves(by, by_second=None):
    steps = (by, by if by_second is None else by_second)
    return [(index_of(*at), index_of(*(a + s for a, s in zip(at, steps[at[3]])))) for at in EVERY]


Y_RING = moves((1, 0, 0, 0), (-1, 0, 0, 0))
Z_RING = moves((0, 1, 0, 0), (0, -1, 0, 0))
X_RING = moves((0, 0, 1, 0), (0, 0, -1, 0))
Z_BY = {k: moves((0, k, 0, 0)) for k in (1, 2, 3)}
CORES = moves((0, 0, 0, 1))
REPLICA = moves((2, 0, 0, 0))


def send(array, pairs):
    return lax.ppermute(array, AXES, pairs)


def here():
    at = lax.axis_index("fsdp")
    core, x, z, y = at % 2, (at // 2) % 4, (at // 8) % 4, at // 32
    return y, z, x, core, 1 - 2 * core


def pick(array, at, axis=0):
    return lax.dynamic_index_in_dim(array, at, axis, keepdims=False)


YZ = [(row, z) for row in range(2) for z in range(4)]
YZ_ORDER = [(0, 2), (1, 0), (0, 1), (0, 3), (1, 1), (1, 3), (1, 2), (0, 0)]
YZ_BY = {(row, z): moves((row, z, 0, 0), (-row, z, 0, 0)) for row, z in YZ}
X_BY = {k: moves((0, 0, k, 0)) for k in (1, 2, 3)}


def half_block(shard):
    y, z, x, core, sign = here()
    got = [send(shard, X_BY[k]) for k in (3, 2, 1)]
    ring = jnp.stack([*got, shard, *got])
    mine, give = (
        lax.dynamic_slice_in_dim(ring, (7 - x + 2 * c) % 4, 2, 0) for c in (core, 1 - core)
    )
    got = send(give, CORES)
    low = core == 0
    both = jnp.stack([jnp.where(low, mine, got), jnp.where(low, got, mine)], axis=1)
    return both.reshape(48, shard.shape[1])


def all_done(*arrays):
    return lax.optimization_barrier(arrays)


PAD = 16


def gather(pack_shard, back, place):
    by_z = [send(back, Z_BY[k]) for k in (1, 2, 3)]
    shard, place, *by_z = all_done(pack_shard(), place, *by_z)
    quad = jnp.concatenate([back, *by_z], axis=0)
    by_y = send(quad, Y_RING)
    own = [half_block(shard)]
    quads = [jnp.concatenate([quad, by_y, jnp.zeros((PAD, WIDTH), BF16)], axis=0)]
    side, over_own, over_side = [], [], []
    for t in range(4):
        now = [own[t], *side[t - 1 : t]]
        if t < 3:
            now.append(quads[t])
        now = all_done(*now)
        if t < 3:
            quads.append(send(now[-1], X_RING))
            own.append(send(now[0], Z_RING))
        side.append(send(now[0], Y_RING))
        if t:
            over_side.append(send(now[1], CORES))
        over_own.append(send(now[0], CORES))
        done = [own[-1], side[-1], over_own[-1]]
        if t < 3:
            done.append(quads[-1])
        if t:
            done.append(over_side[-1])
        done = list(all_done(*done))
        own[-1], side[-1], over_own[-1] = done[:3]
        if t < 3:
            quads[-1] = done[3]
        if t:
            over_side[-1] = done[-1]
    over_side.append(send(side[3], CORES))
    over_side[3], *quads = all_done(over_side[3], *quads)
    backs = quads + [send(q, CORES) for q in quads]
    return own + side + over_own + over_side, backs, place


def over_replicas(share):
    share = lax.reduce_precision(share, 8, 7)
    return share + send(share.astype(BF16), REPLICA).astype(F32)


def to_owner(total):
    y, z, x, core, sign = here()
    parts = total.reshape(2, 2, 12, total.shape[-1])
    keep, got = pick(parts, core, 1), send(pick(parts, 1 - core, 1), CORES)
    low = core == 0
    ring = jnp.concatenate([jnp.where(low, keep, got), jnp.where(low, got, keep)], axis=0)
    share = pick(ring, x).astype(F32)
    for k in (1, 2, 3):
        share = share + send(pick(ring, (x + k) % 4), X_BY[k]).astype(F32)
    return share


HALF = 48
BLOCKS = WIDTH // (2 * HALF)
WINDOWS = (0, 0, 64, 128, 192, 256, 320, 320)
SPAN = 192
GROUP = 4 * HEAD_DIM
VMEM = pl.BlockSpec(memory_space=pltpu.VMEM)
SMEM = pl.BlockSpec(memory_space=pltpu.SMEM)
ANY = pl.BlockSpec(memory_space=pl.ANY)


def limit(mib):
    return pltpu.CompilerParams(vmem_limit_bytes=mib * 1024 * 1024)


COST = pl.CostEstimate(flops=10**6, bytes_accessed=10**5, transcendentals=0)
URGENT = pl.CostEstimate(flops=3 * 10**10, bytes_accessed=10**5, transcendentals=0)
CHUNK_ONE = 3 * WIDTH + 128
CHUNK_TWO = FF + WIDTH


def dot(a, b):
    return lax.dot_general(a, b, (((1,), (0,)), ((), ())), preferred_element_type=F32)


def dot_nt(a, b):
    return lax.dot_general(a, b, (((1,), (1,)), ((), ())), preferred_element_type=F32)


def dot_tn(a, b):
    return lax.dot_general(a, b, (((0,), (0,)), ((), ())), preferred_element_type=F32)


def normed(values):
    centre = values - jnp.mean(values, axis=-1, keepdims=True)
    scale = lax.rsqrt(jnp.mean(centre * centre, axis=-1, keepdims=True) + 1e-05)
    return centre * scale, scale


def norm_back(d_out, hat, scale, gain):
    expand = d_out * gain
    d_in = scale * (
        expand
        - jnp.mean(expand, axis=-1, keepdims=True)
        - hat * jnp.mean(expand * hat, axis=-1, keepdims=True)
    )
    gain_grad = jnp.sum(d_out * hat, axis=0, keepdims=True)
    return d_in, gain_grad, jnp.sum(d_out, axis=0, keepdims=True)


def rows_at(start, size, step=16):
    return pl.ds(pl.multiple_of(start, step), size)


def places(place_ref):
    core, y, z, x = (place_ref[n] for n in (0, 2, 3, 4))
    return core, y, z, x, 1 - 2 * core


def around(at, step):
    return lax.rem(at + step + 8, 4)


def row_slots(place_ref):
    core, y, z, x, sign = places(place_ref)
    return [
        (row * 4 + around(z, -way * t)) * 2 + half
        for half, way in ((core, sign), (1 - core, -sign))
        for row in (y, 1 - y)
        for t in range(4)
    ]


def back_slots(place_ref):
    core, y, z, x, sign = places(place_ref)
    return [
        ((row * 4 + around(z, -k)) * 4 + around(x, -way * t)) * 2 + half
        for half, way in ((core, sign), (1 - core, -sign))
        for t in range(4)
        for row in (y, 1 - y)
        for k in range(4)
    ]


def piece_copies(slots, pieces, target, sems, first, columns=None):
    copies = []
    each = len(slots) // len(pieces)
    for n, slot in enumerate(slots):
        source = pieces[n // each].at[pl.ds(n % each * HALF, HALF), :]
        if columns is not None:
            source = source.at[:, pl.ds(*columns)]
        copies.append(
            pltpu.make_async_copy(
                source, target.at[rows_at(slot * HALF, HALF)], sems.at[first + n]
            )
        )
    return copies


def split_rows(place_ref, made):
    columns = made.shape[1]
    parts = made.astype(BF16).reshape(BLOCKS, 2, HALF, columns)
    first, second = (parts[:, n].reshape(BLOCKS * HALF, columns) for n in range(2))
    low = place_ref[0] == 0
    return lax.select(low, second, first), lax.select(low, first, second)


def head_of(rows):
    return lax.broadcasted_iota(jnp.int32, (rows, GROUP), 1) // HEAD_DIM


def four_heads(group):
    head, zero = head_of(group.shape[0]), jnp.zeros_like(group)
    return jnp.concatenate([jnp.where(head == h, group, zero) for h in range(4)], axis=0)


def one_of_four(wide):
    n = wide.shape[0] // 4
    head, result = head_of(n), wide[:n]
    for h in range(1, 4):
        result = jnp.where(head == h, wide[h * n : (h + 1) * n], result)
    return result


def fill_bias(place_ref, lengths_ref, bias):
    ends, total = [], jnp.int32(0)
    for k in range(16):
        total = total + lengths_ref[k, place_ref[1]]
        ends.append(total)

    def ids(at):
        return sum((at >= end).astype(jnp.int32) for end in ends)

    keys = ids(lax.broadcasted_iota(jnp.int32, (LEN, 1), 0))
    lane = lax.broadcasted_iota(jnp.int32, (1, GROUP), 1) % HEAD_DIM
    for i, start in enumerate(WINDOWS):
        same = keys[start : start + SPAN] == ids(lane + i * 64)
        bias[i] = jnp.where(same, 0.0, -1e30).astype(F32)


def pack_kernel(*refs):
    vectors, in_bias, w_qkv, w_in, w_out, out, made = refs[:8], *refs[8:]
    rows = w_qkv.shape[0]
    same = lax.broadcasted_iota(jnp.int32, (rows, rows), 0) == lax.broadcasted_iota(
        jnp.int32, (rows, rows), 1
    )
    lane = lax.broadcasted_iota(jnp.int32, (rows, 128), 1)
    total = jnp.zeros((rows, 128), F32)
    for i, ref in enumerate(vectors):
        wide = jnp.broadcast_to(ref[...].astype(F32), (rows, rows))
        column = jnp.sum(jnp.where(same, wide, 0.0), axis=1, keepdims=True)
        total = jnp.where(lane == i, column, total)
    made[...] = total
    made[0:1, 16:64] = in_bias[...].astype(F32)
    out[:, : 3 * WIDTH] = w_qkv[...]
    out[:, 3 * WIDTH : CHUNK_ONE] = made[...].astype(BF16)
    out[:, CHUNK_ONE : CHUNK_ONE + FF] = w_in[...]
    out[:, CHUNK_ONE + FF :] = w_out[...]


def pack(vectors, in_bias, w_qkv, w_in, w_out):
    return pl.pallas_call(
        pack_kernel,
        out_shape=jax.ShapeDtypeStruct((12, CHUNK_ONE + CHUNK_TWO), BF16),
        in_specs=[VMEM] * 12,
        out_specs=VMEM,
        scratch_shapes=[pltpu.VMEM((12, 128), F32)],
        name="pack",
    )(*(v.reshape(1, 12) for v in vectors), in_bias.reshape(1, 48), w_qkv, w_in, w_out)


def first_kernel(place, lengths, tokens, *refs):
    pieces = refs[:16]
    proj_out, mixed, logsum, in_bias, rows, proj, weight, vec, wide, bias, sems = refs[16:]
    slots = row_slots(place)
    copies = piece_copies(slots, pieces, weight, sems, 0, (0, 3 * WIDTH))
    copies += piece_copies(slots, pieces, vec, sems, 16, (3 * WIDTH, 128))
    for copy in copies:
        copy.start()
    fill_bias(place, lengths, bias)
    hat, unused = normed(tokens[...].astype(F32))
    for copy in copies:
        copy.wait()
    wide[...] = vec[...].astype(F32)
    rows[...] = wide[...].T[:16]
    for n in range(64):
        in_bias[:, n * 48 : (n + 1) * 48] = wide[n * 12 : n * 12 + 1, 16:64]
    act = (hat * rows[0:1, :] + rows[1:2, :]).astype(BF16)
    for n in range(9):
        at = pl.ds(n * 256, 256)
        made = dot(act, weight[:, at])
        if n // 3 != 1:
            made = made + rows[2 + n // 6 : 3 + n // 6, (n % 3) * 256 : (n % 3 + 1) * 256]
        proj[:, at] = made.astype(BF16)
    out_copy = pltpu.make_async_copy(proj, proj_out, sems.at[32])
    out_copy.start()
    for p in range(HEADS // 4):
        query_at, keys_at, vals_at = (pl.ds(n * WIDTH + p * GROUP, GROUP) for n in range(3))
        for i, start in enumerate(WINDOWS):
            here_rows, near = pl.ds(i * 64, 64), pl.ds(start, SPAN)
            query = four_heads(proj[here_rows, query_at] * HEAD_DIM ** (-0.5))
            scores = dot_nt(proj[near, keys_at], query) + bias[i]
            top = jnp.max(scores, axis=0, keepdims=True)
            expo = jnp.exp(scores - top)
            total = jnp.sum(expo, axis=0, keepdims=True)
            probs = (expo * (1.0 / total)).astype(BF16)
            mixed[here_rows, query_at] = one_of_four(dot_tn(probs, proj[near, vals_at])).astype(BF16)
            logsum[p * 8 + i : p * 8 + i + 1, :] = top + jnp.log(total)
    out_copy.wait()


def run_first(place, lengths, tokens, pieces):
    return pl.pallas_call(
        first_kernel,
        out_shape=[
            jax.ShapeDtypeStruct((LEN, 3 * WIDTH), BF16),
            jax.ShapeDtypeStruct((LEN, WIDTH), BF16),
            jax.ShapeDtypeStruct((24, 256), F32),
            jax.ShapeDtypeStruct((1, FF), F32),
            jax.ShapeDtypeStruct((16, WIDTH), F32),
        ],
        in_specs=[SMEM, SMEM, VMEM] + [ANY] * 16,
        out_specs=[ANY] + [VMEM] * 4,
        scratch_shapes=[
            pltpu.VMEM((LEN, 3 * WIDTH), BF16),
            pltpu.VMEM((WIDTH, 3 * WIDTH), BF16),
            pltpu.VMEM((WIDTH, 128), BF16),
            pltpu.VMEM((WIDTH, 128), F32),
            pltpu.VMEM((8, SPAN, GROUP), F32),
            pltpu.SemaphoreType.DMA((33,)),
        ],
        compiler_params=limit(60),
        cost_estimate=COST,
        name="attention_forward",
    )(place, lengths, tokens, *pieces)


def gelu_pair(x):
    phi = 0.5 + 0.5 * lax.erf(x * 0.5**0.5)
    return x * phi, phi + x * (jnp.exp(x * (x * -0.5)) * 0.3989422804014327)


def feed_kernel(place, tokens, mixed, cot, rows, in_bias, *refs):
    pieces, backs = refs[:16], refs[16:24]
    hidden, g1, d_mixed, vector_grads, in_bias_grad = refs[24:29]
    give, keep, give_back, keep_back, give_out, keep_out = refs[29:35]
    w_out, w_in, w_back, x1, hat, scale, act, acc, d_act = refs[35:44]
    gact_0, gact_1, d_pre_0, d_pre_1 = refs[44:48]
    made_give, made_keep, made_give_back, made_keep_back, sems, out_sems = refs[48:]
    gact, d_pre = (gact_0, gact_1), (d_pre_0, d_pre_1)
    slots = row_slots(place)
    out_copies = piece_copies(slots, pieces, w_out, sems, 0, (CHUNK_ONE + FF, WIDTH))
    in_copies = piece_copies(slots, pieces, w_in, sems, 16, (CHUNK_ONE, FF))
    back_copies = piece_copies(back_slots(place), backs, w_back, sems, 32)
    for copy in out_copies + in_copies + back_copies:
        copy.start()
    for copy in out_copies:
        copy.wait()
    for n in range(3):
        at = pl.ds(n * 256, 256)
        x1[:, at] = tokens[:, at].astype(F32) + (dot(mixed[...], w_out[:, at]) + rows[4:5, at])
    hat[...], scale[...] = normed(x1[...])
    act[...] = (hat[...] * rows[5:6, :] + rows[6:7, :]).astype(BF16)
    for copy in in_copies + back_copies:
        copy.wait()

    def units(j, n):
        local, at = pl.ds(n * 256, 256), pl.ds(j * WIDTH + n * 256, 256)
        value, slope = gelu_pair(dot(act[...], w_in[:, at]) + in_bias[:, at])
        gact[j % 2][:, local] = value.astype(BF16)
        d_low = (dot_nt(cot[...], w_back[at, :]) * slope).astype(BF16)
        d_pre[j % 2][:, local] = d_low
        in_bias_grad[:, at] = jnp.sum(d_low.astype(F32), axis=0, keepdims=True)

    def sums(j, n):
        at, block, half = pl.ds(n * 256, 256), pl.ds(j * WIDTH, WIDTH), pl.ds(j * 384, 384)
        forward = dot(gact[j % 2][...], w_back[block, at])
        backward = dot_nt(d_pre[j % 2][...], w_in[at, block])
        acc[:, at] = forward if j == 0 else acc[:, at] + forward
        d_act[:, at] = backward if j == 0 else d_act[:, at] + backward
        wide = pl.ds(j * WIDTH + n * 256, 256)
        made_give[:, wide], made_keep[:, wide] = split_rows(
            place, dot_tn(act[...], d_pre[j % 2][:, at])
        )
        made_give_back[half, at], made_keep_back[half, at] = split_rows(
            place, dot_tn(gact[j % 2][...], cot[:, at])
        )

    copies = []
    for j in range(5):
        for n in range(3):
            if j < 4:
                units(j, n)
            if j:
                sums(j - 1, n)
        if j:
            wide, half = pl.ds((j - 1) * WIDTH, WIDTH), pl.ds((j - 1) * 384, 384)
            for made, out, at in (
                (made_give, give, (slice(None), wide)),
                (made_give_back, give_back, (half, slice(None))),
                (made_keep, keep, (slice(None), wide)),
                (made_keep_back, keep_back, (half, slice(None))),
            ):
                copies.append(
                    pltpu.make_async_copy(made.at[at], out.at[at], out_sems.at[len(copies)])
                )
                copies[-1].start()
    hidden[...] = (x1[...] + (acc[...] + rows[7:8, :])).astype(BF16)
    cot_wide = cot[...].astype(F32)
    d_in, gain_grad, bias_grad = norm_back(d_act[...], hat[...], scale[...], rows[5:6, :])
    total = cot_wide + d_in
    g1[...] = total
    low = total.astype(BF16)
    for n in range(3):
        at = pl.ds(n * 256, 256)
        d_mixed[:, at] = dot_nt(low, w_out[at, :]).astype(BF16)
        give_out[:, at], keep_out[:, at] = split_rows(
            place, dot_tn(mixed[...], low[:, n * 256 : (n + 1) * 256])
        )
    vector_grads[...] = jnp.concatenate(
        [
            jnp.sum(low.astype(F32), axis=0, keepdims=True),
            gain_grad,
            bias_grad,
            jnp.sum(cot_wide, axis=0, keepdims=True),
            jnp.zeros((4, WIDTH), F32),
        ],
        axis=0,
    )
    for copy in copies:
        copy.wait()


def run_feed(place, tokens, mixed, cot, rows, in_bias, pieces, backs):
    wide, tall, low = (WIDTH // 2, FF), (FF // 2, WIDTH), (LEN, WIDTH)
    return pl.pallas_call(
        feed_kernel,
        out_shape=[
            jax.ShapeDtypeStruct(low, BF16),
            jax.ShapeDtypeStruct(low, F32),
            jax.ShapeDtypeStruct(low, BF16),
            jax.ShapeDtypeStruct((8, WIDTH), F32),
            jax.ShapeDtypeStruct((1, FF), F32),
            jax.ShapeDtypeStruct(wide, BF16),
            jax.ShapeDtypeStruct(wide, BF16),
            jax.ShapeDtypeStruct(tall, BF16),
            jax.ShapeDtypeStruct(tall, BF16),
            jax.ShapeDtypeStruct((WIDTH // 2, WIDTH), BF16),
            jax.ShapeDtypeStruct((WIDTH // 2, WIDTH), BF16),
        ],
        in_specs=[SMEM] + [VMEM] * 5 + [ANY] * 24,
        out_specs=[VMEM] * 5 + [ANY] * 4 + [VMEM] * 2,
        scratch_shapes=[
            pltpu.VMEM((WIDTH, WIDTH), BF16),
            pltpu.VMEM((WIDTH, FF), BF16),
            pltpu.VMEM((FF, WIDTH), BF16),
            pltpu.VMEM(low, F32),
            pltpu.VMEM(low, F32),
            pltpu.VMEM((LEN, 1), F32),
            pltpu.VMEM(low, BF16),
            pltpu.VMEM(low, F32),
            pltpu.VMEM(low, F32),
        ]
        + [pltpu.VMEM(low, BF16)] * 4
        + [pltpu.VMEM(wide, BF16)] * 2
        + [pltpu.VMEM(tall, BF16)] * 2
        + [pltpu.SemaphoreType.DMA((96,)), pltpu.SemaphoreType.DMA((16,))],
        compiler_params=limit(60),
        cost_estimate=COST,
        name="feed_forward",
    )(place, tokens, mixed, cot, rows, in_bias, *pieces, *backs)


def attend_back_kernel(place, lengths, proj, logsum, d_mixed, d_proj, bias, d_keys, d_vals):
    fill_bias(place, lengths, bias)

    def attend(p, carry):
        query_at, keys_at, vals_at = (
            rows_at(n * WIDTH + p * GROUP, GROUP, GROUP) for n in range(3)
        )
        d_keys[...] = jnp.zeros_like(d_keys)
        d_vals[...] = jnp.zeros_like(d_vals)
        for i, start in enumerate(WINDOWS):
            here_rows, near = pl.ds(i * 64, 64), pl.ds(start, SPAN)
            query = four_heads(proj[here_rows, query_at] * HEAD_DIM ** (-0.5))
            keys, vals = proj[near, keys_at], proj[near, vals_at]
            d_mix = four_heads(d_mixed[here_rows, query_at])
            probs = jnp.exp(dot_nt(keys, query) + bias[i] - logsum[pl.ds(p * 8 + i, 1), :])
            d_probs = dot_nt(vals, d_mix)
            mean = jnp.sum(probs * d_probs, axis=0, keepdims=True)
            d_scores = (probs * (d_probs - mean)).astype(BF16)
            d_query = one_of_four(dot_tn(d_scores, keys)) * HEAD_DIM ** (-0.5)
            d_proj[here_rows, query_at] = d_query.astype(BF16)
            d_keys[near, :] += dot(d_scores, query)
            d_vals[near, :] += dot(probs.astype(BF16), d_mix)
        d_proj[:, keys_at] = d_keys[...].astype(BF16)
        d_proj[:, vals_at] = d_vals[...].astype(BF16)
        return carry

    lax.fori_loop(0, HEADS // 4, attend, 0)


def run_attend_back(place, lengths, proj, logsum, d_mixed):
    return pl.pallas_call(
        attend_back_kernel,
        out_shape=jax.ShapeDtypeStruct((LEN, 3 * WIDTH), BF16),
        in_specs=[SMEM, SMEM] + [VMEM] * 3,
        out_specs=VMEM,
        scratch_shapes=[
            pltpu.VMEM((8, SPAN, GROUP), F32),
            pltpu.VMEM((LEN, GROUP), F32),
            pltpu.VMEM((LEN, GROUP), F32),
        ],
        compiler_params=limit(60),
        cost_estimate=COST,
        name="attention_backward",
    )(place, lengths, proj, logsum, d_mixed)


FIRST_HALVES = np.arange(WIDTH, dtype=np.int32).reshape(BLOCKS, 2, HALF)[:, 0].reshape(1, -1)


def project_back_kernel(place, tokens, tokens_over, d_proj, d_over, rows, grads_two, in_bias, *refs):
    order, pieces = refs[0], refs[1:17]
    d_act, theirs, mine, give, keep, made_theirs, made_mine, weight, natural, sems = refs[17:]
    core, y, unused, unused, unused = places(place)
    copies = piece_copies(row_slots(place), pieces, weight, sems, 0, (0, 3 * WIDTH))
    for copy in copies:
        copy.start()
    half = order[...] + HALF * core
    half = (lax.broadcasted_iota(jnp.int32, (WIDTH, WIDTH // 2), 0) == half).astype(F32)
    half = half.astype(BF16)
    hat, unused = normed(tokens[...].astype(F32))
    hat_over, unused = normed(tokens_over[...].astype(F32))
    act, act_over = (
        dot((h * rows[0:1, :] + rows[1:2, :]).astype(BF16), half).astype(BF16)
        for h in (hat, hat_over)
    )
    outs = []
    for n in range(9):
        at = pl.ds(n * 256, 256)
        made = (dot_tn(act, d_proj[:, at]) + dot_tn(act_over, d_over[:, at])).astype(BF16)
        low, high = made[: 4 * HALF], made[4 * HALF :]
        made_theirs[:, at] = lax.select(y == 0, high, low)
        made_mine[:, at] = lax.select(y == 0, low, high)
        if n % 3 == 2:
            wide = pl.ds((n - 2) * 256, WIDTH)
            for made, out in ((made_theirs, theirs), (made_mine, mine)):
                outs.append(
                    pltpu.make_async_copy(
                        made.at[:, wide], out.at[:, wide], sems.at[16 + len(outs)]
                    )
                )
                outs[-1].start()
    for copy in copies:
        copy.wait()
    for n in range(3):
        at = pl.ds(n * 256, 256)
        d_act[:, at] = dot_nt(d_proj[...], weight[at, :])
    made = jnp.concatenate(
        [
            jnp.sum(d_act[...] * hat, axis=0, keepdims=True),
            jnp.sum(d_act[...], axis=0, keepdims=True),
            jnp.sum(d_proj[:, :WIDTH].astype(F32), axis=0, keepdims=True),
            jnp.sum(d_proj[:, 2 * WIDTH :].astype(F32), axis=0, keepdims=True),
            grads_two[:4, :],
            jnp.zeros((120, WIDTH), F32),
        ],
        axis=0,
    )
    natural[...] = made.T
    for n in range(64):
        natural[n * 12 : n * 12 + 1, 16:64] = in_bias[:, n * 48 : (n + 1) * 48]
    give[...], keep[...] = split_rows(place, natural[...])
    for copy in outs:
        copy.wait()


def run_project_back(place, tokens, tokens_over, d_proj, d_over, rows, grads_two, in_bias, pieces):
    part, vector = (4 * HALF, 3 * WIDTH), (WIDTH // 2, 128)
    return pl.pallas_call(
        project_back_kernel,
        out_shape=[
            jax.ShapeDtypeStruct((LEN, WIDTH), F32),
            jax.ShapeDtypeStruct(part, BF16),
            jax.ShapeDtypeStruct(part, BF16),
            jax.ShapeDtypeStruct(vector, BF16),
            jax.ShapeDtypeStruct(vector, BF16),
        ],
        in_specs=[SMEM] + [VMEM] * 8 + [ANY] * 16,
        out_specs=[VMEM, ANY, ANY, VMEM, VMEM],
        scratch_shapes=[
            pltpu.VMEM(part, BF16),
            pltpu.VMEM(part, BF16),
            pltpu.VMEM((WIDTH, 3 * WIDTH), BF16),
            pltpu.VMEM((WIDTH, 128), F32),
            pltpu.SemaphoreType.DMA((22,)),
        ],
        compiler_params=limit(60),
        cost_estimate=COST,
        name="project_backward",
    )(
        place,
        tokens,
        tokens_over,
        d_proj,
        d_over,
        rows,
        grads_two,
        in_bias,
        jnp.asarray(FIRST_HALVES),
        *pieces,
    )


def input_grad_kernel(tokens, d_act, g1, rows, d_input):
    hat, scale = normed(tokens[...].astype(F32))
    d_in, unused, unused = norm_back(d_act[...], hat, scale, rows[0:1, :])
    d_input[...] = g1[...] + d_in


def run_input_grad(tokens, d_act, g1, rows):
    return pl.pallas_call(
        input_grad_kernel,
        out_shape=jax.ShapeDtypeStruct((LEN, WIDTH), F32),
        in_specs=[VMEM] * 4,
        out_specs=VMEM,
        compiler_params=limit(60),
        cost_estimate=COST,
        name="input_gradient",
    )(tokens, d_act, g1, rows)


def after_kernel(place, *refs):
    for n in range(place.shape[0]):
        refs[-1][n] = place[n]


def run_after(place, *arrays):
    return pl.pallas_call(
        after_kernel,
        out_shape=jax.ShapeDtypeStruct(place.shape, place.dtype),
        in_specs=[SMEM] + [ANY] * len(arrays),
        out_specs=SMEM,
        cost_estimate=URGENT,
        name="after",
    )(place, *arrays)


def run_split(name, place, arrays, plan, cost=COST):
    drafts = plan(0, 0, 0, 1)
    shapes = [
        (sum(count for count, unused in parts), HALF, sum(width for width, unused in parts[0][1]))
        for unused, parts in drafts
    ]
    buffers = [
        pltpu.VMEM((count, HALF, width), arrays[i].dtype)
        for unused, parts in drafts
        for count, segments in parts
        for width, sources in segments
        for i, unused, unused in sources
    ]

    def kernel(place_ref, *refs):
        refs = list(refs)
        ins, outs, held, made = (
            [refs.pop(0) for unused in group] for group in (arrays, shapes, buffers, shapes)
        )
        in_sems, out_sems = refs
        unused, y, z, x, sign = places(place_ref)
        plans, copies = plan(y, z, x, sign), []
        for unused, parts in plans:
            for unused, segments in parts:
                for width, sources in segments:
                    for i, index, column in sources:
                        if not isinstance(column, int):
                            column = pl.multiple_of(column, 128)
                        n = len(copies)
                        copies.append(
                            pltpu.make_async_copy(
                                ins[i].at[(*index, slice(None), pl.ds(column, width))],
                                held[n],
                                in_sems.at[n],
                            )
                        )
                        copies[-1].start()
        n, writes = 0, []
        for o, (kind, parts) in enumerate(plans):
            row = 0
            for count, segments in parts:
                column = 0
                for width, sources in segments:
                    total = None
                    for unused in sources:
                        copies[n].wait()
                        value = held[n][...].astype(F32)
                        total = value if total is None else total + value
                        n += 1
                    made[o][row : row + count, :, column : column + width] = total.astype(kind)
                    column += width
                row += count
            writes.append(pltpu.make_async_copy(made[o], outs[o], out_sems.at[o]))
            writes[-1].start()
        for write in writes:
            write.wait()

    return pl.pallas_call(
        kernel,
        out_shape=[jax.ShapeDtypeStruct(s, kind) for s, (kind, unused) in zip(shapes, drafts)],
        in_specs=[SMEM] + [ANY] * len(arrays),
        out_specs=[ANY] * len(shapes),
        scratch_shapes=buffers
        + [pltpu.VMEM(s, kind) for s, (kind, unused) in zip(shapes, drafts)]
        + [pltpu.SemaphoreType.DMA((len(buffers),)), pltpu.SemaphoreType.DMA((len(shapes),))],
        compiler_params=limit(60),
        cost_estimate=cost,
        name=name,
    )(place, *arrays)


def shards(tokens, lengths, g1, s1, wqkv, qb, vb, wo, ob, g2, s2, w1, bi1, w2, b2, cotangent):
    y, z, x, core, sign = here()
    place = jnp.stack([core, lax.axis_index("dp") * 64 + lax.axis_index("fsdp"), y, z, x])
    lengths = lengths.T
    pieces, backs, place = gather(
        lambda: pack((g1, s1, qb, vb, ob, g2, s2, b2), bi1, wqkv, w1, wo), w2, place
    )
    proj, mixed, logsum, in_bias, rows = run_first(place, lengths, tokens, pieces)
    hidden, d_middle, d_mixed, grads_two, in_bias_grad, *grads = run_feed(
        place, tokens, mixed, cotangent, rows, in_bias, pieces, backs
    )
    give_i, keep_i, give_b, keep_b, give_o, keep_o = grads
    got_i, got_b, got_o = send(give_i, CORES), send(give_b, CORES), send(give_o, CORES)
    d_proj = run_attend_back(place, lengths, proj, logsum, d_mixed)
    d_proj, got_i, got_b, got_o = all_done(d_proj, got_i, got_b, got_o)
    d_over, tokens_over = send(d_proj, CORES), send(tokens, CORES)

    blocks = lambda a, *lead: a.reshape(*lead, HALF, a.shape[-1])
    whole = (slice(None),)
    wide = ((FF, (0, 1)), (WIDTH, (2, 3)))

    def own_in(at):
        return [(4, [(n, [(i, (pl.ds(at * 4, 4),), 0) for i in ids]) for n, ids in wide])]

    sums_in = [blocks(a, 8) for a in (keep_i, got_i, keep_o, got_o)]
    sums_back = [blocks(a, 8, 4) for a in (keep_b, got_b)]
    (theirs,) = run_split(
        "sum_cores_in", place, sums_in, lambda y, z, x, sign: [(BF16, own_in(1 - y))]
    )
    from_y = send(theirs, Y_RING)
    def back(at, first, count, *more):
        sources = [(i, (pl.ds(first, count), at), 0) for i in (0, 1)]
        return (count, [(WIDTH, sources + [(i, whole, 0) for i in more])])

    far_up, far_down = run_split(
        "sum_cores_back",
        place,
        sums_back,
        lambda y, z, x, sign: [
            (BF16, [back(around(x, 2), 0, 4)]),
            (BF16, [back(around(x, 2), 4, 4)]),
        ],
    )
    d_proj, d_over, tokens_over, far_up, far_down = all_done(
        d_proj, d_over, tokens_over, far_up, far_down
    )
    from_x = [send(far_up, X_BY[1]), send(far_down, X_BY[3])]
    d_act, theirs, mine_q, give_v, keep_v = run_project_back(
        place, tokens, tokens_over, d_proj, d_over, rows, grads_two, in_bias_grad, pieces
    )
    d_act, theirs, mine_q, give_v, from_y, *from_x = all_done(
        d_act, theirs, mine_q, give_v, from_y, *from_x
    )

    from_y_q = send(blocks(theirs, 4), Y_RING)
    got_v = send(give_v, CORES)
    add = lambda a, b: (a.astype(F32) + b.astype(F32)).astype(BF16)
    up, down = run_split(
        "sum_x_2",
        place,
        (*sums_back, *from_x),
        lambda y, z, x, sign: [
            (BF16, [back(around(x, 1), 0, 4, 2), back(around(x, 1), 4, 4)]),
            (BF16, [back(around(x, 3), 0, 4), back(around(x, 3), 4, 4, 3)]),
        ],
    )
    from_x = [send(up, X_BY[1]), send(down, X_BY[3])]

    def after_y(y, z, x, sign):
        def both(at):
            own = (pl.ds(y * 4 + at, 1),)
            segments = []
            for (n, ids), column in zip(wide, (0, FF)):
                sources = [(i, own, 0) for i in ids] + [(4, (pl.ds(at, 1),), column)]
                segments.append((n, sources))
            return [(1, segments)]

        return [(BF16, both(around(z, k))) for k in (1, 3, 2, 0)]

    *parts, own_i = run_split("sum_y", place, (*sums_in, from_y), after_y)
    d_act, got_v, own_i, *parts = all_done(d_act, got_v, own_i, *parts)
    from_z_i = [send(p, Z_BY[k]) for p, k in zip(parts, (1, 3, 2))]
    kept_v = add(keep_v, got_v).reshape(2, 4, HALF, 128)
    mine_v, from_y_v = pick(kept_v, y), send(pick(kept_v, 1 - y), Y_RING)
    mine_v, from_y, from_y_v = all_done(mine_v, from_y_q, from_y_v)

    def along_z(y, z, x, sign):
        pair = lambda n, ids, at: (n, [(i, (pl.ds(at, 1),), 0) for i in ids])
        part = lambda at: [(1, [pair(3 * WIDTH, (0, 1), at), pair(128, (2, 3), at)])]
        return [(BF16, part(around(z, k))) for k in (1, 3, 2, 0)]

    *parts, own = run_split(
        "sum_y_rest", place, (blocks(mine_q, 4), from_y, mine_v, from_y_v), along_z
    )
    from_z = [send(p, Z_BY[k]) for p, k in zip(parts, (1, 3, 2))]

    def back_along_z(y, z, x, sign):
        def part(at):
            sources = [(i, (pl.ds(at, 1), x), 0) for i in (0, 1)]
            sources += [(i, (pl.ds(at, 1),), 0) for i in (2, 3)]
            return (1, [(WIDTH, sources)])

        return [(BF16, [part(around(z, k)), part(4 + around(z, k))]) for k in (1, 3, 2, 0)]

    *parts, own_b = run_split("sum_x", place, (*sums_back, *from_x), back_along_z)
    from_z_b = [send(p, Z_BY[k]) for p, k in zip(parts, (1, 3, 2))]
    d_input = run_input_grad(tokens, d_act, d_middle, rows)
    place = run_after(place, *from_z_i)
    place, d_input, own, own_b, *done = all_done(place, d_input, own, own_b, *from_z, *from_z_b)
    from_z, from_z_b = done[:3], done[3:]

    def last_sum(y, z, x, sign):
        total = lambda width, ids: (width, [(i, whole, 0) for i in ids])
        back = lambda at: [(1, [(WIDTH, [(i, (pl.ds(at, 1),), 0) for i in range(8, 12)])])]
        return [
            (BF16, [(1, [total(CHUNK_ONE, range(4)), total(CHUNK_TWO, range(4, 8))])]),
            (BF16, back(1 - y)),
            (BF16, back(y)),
        ]

    share, theirs, mine = run_split("sum_z", place, (own, *from_z, own_i, *from_z_i, own_b, *from_z_b), last_sum)
    from_y = send(theirs, Y_RING)
    share = to_owner(share)
    back_share = (mine.astype(F32) + from_y.astype(F32)).reshape(HALF, WIDTH)
    share, back_share = all_done(share, back_share)
    share, back_share = over_replicas(share), over_replicas(back_share)
    own = share[:, 3 * WIDTH : CHUNK_ONE]
    return (
        hidden,
        d_input,
        own[:, 0],
        own[:, 1],
        share[:, : 3 * WIDTH],
        own[:, 2],
        own[:, 3],
        share[:, CHUNK_ONE + FF :],
        own[:, 4],
        own[:, 5],
        own[:, 6],
        share[:, CHUNK_ONE : CHUNK_ONE + FF],
        own[0, 16:64],
        back_share,
        own[:, 7],
    )


def solution(mesh):
    rows, whole = P(AXES, None), P()
    vector, matrix = P("fsdp"), P("fsdp", None)
    weights = (
        vector, vector, matrix, vector, vector, matrix, vector,
        vector, vector, matrix, vector, matrix, vector,
    )
    return jax.shard_map(
        shards,
        mesh=mesh,
        in_specs=(rows, whole, *weights, rows),
        out_specs=(rows, rows, *weights),
        check_vma=False,
    )
```

```python
import itertools

import jax
import jax.numpy as jnp
import numpy as np
from jax import lax
from jax.experimental import pallas as pl
from jax.experimental.pallas import tpu as pltpu
from jax.sharding import PartitionSpec as P

HEADS = 12
HEAD_DIM = 64
LEN = 512
WIDTH = 768
FF = 3072
AXES = ("dp", "fsdp")
F32 = jnp.float32
BF16 = jnp.bfloat16

EVERY = [(y, z, x, c) for y in range(4) for z in range(4) for x in range(4) for c in range(2)]


def index_of(y, z, x, c):
    y, z, x, c = y % 4, z % 4, x % 4, c % 2
    return (y // 2) * 64 + (((y % 2) * 4 + z) * 4 + x) * 2 + c


def moves(by, by_second=None):
    steps = (by, by if by_second is None else by_second)
    return [(index_of(*at), index_of(*(a + s for a, s in zip(at, steps[at[3]])))) for at in EVERY]


Y_RING = moves((1, 0, 0, 0), (-1, 0, 0, 0))
Z_RING = moves((0, 1, 0, 0), (0, -1, 0, 0))
X_RING = moves((0, 0, 1, 0), (0, 0, -1, 0))
Z_BY = {k: moves((0, k, 0, 0)) for k in (1, 2, 3)}
CORES = moves((0, 0, 0, 1))
REPLICA = moves((2, 0, 0, 0))


def send(array, pairs):
    return lax.ppermute(array, AXES, pairs)


def here():
    at = lax.axis_index("fsdp")
    core, x, z, y = at % 2, (at // 2) % 4, (at // 8) % 4, at // 32
    return y, z, x, core, 1 - 2 * core


def pick(array, at, axis=0):
    return lax.dynamic_index_in_dim(array, at, axis, keepdims=False)


YZ = [(row, z) for row in range(2) for z in range(4)]
YZ_ORDER = [(0, 2), (1, 0), (0, 1), (0, 3), (1, 1), (1, 3), (1, 2), (0, 0)]
YZ_BY = {(row, z): moves((row, z, 0, 0), (-row, z, 0, 0)) for row, z in YZ}
X_BY = {k: moves((0, 0, k, 0)) for k in (1, 2, 3)}


def half_block(shard):
    y, z, x, core, sign = here()
    got = [send(shard, X_BY[k]) for k in (3, 2, 1)]
    ring = jnp.stack([*got, shard, *got])
    mine, give = (
        lax.dynamic_slice_in_dim(ring, (7 - x + 2 * c) % 4, 2, 0) for c in (core, 1 - core)
    )
    got = send(give, CORES)
    low = core == 0
    both = jnp.stack([jnp.where(low, mine, got), jnp.where(low, got, mine)], axis=1)
    return both.reshape(48, shard.shape[1])


def all_done(*arrays):
    return lax.optimization_barrier(arrays)


PAD = 16


def gather(pack_shard, back, place):
    by_z = [send(back, Z_BY[k]) for k in (1, 2, 3)]
    shard, place, *by_z = all_done(pack_shard(), place, *by_z)
    quad = jnp.concatenate([back, *by_z], axis=0)
    by_y = send(quad, Y_RING)
    own = [half_block(shard)]
    quads = [jnp.concatenate([quad, by_y, jnp.zeros((PAD, WIDTH), BF16)], axis=0)]
    side, over_own, over_side = [], [], []
    for t in range(4):
        now = [own[t], *side[t - 1 : t]]
        if t < 3:
            now.append(quads[t])
        now = all_done(*now)
        if t < 3:
            quads.append(send(now[-1], X_RING))
            own.append(send(now[0], Z_RING))
        side.append(send(now[0], Y_RING))
        if t:
            over_side.append(send(now[1], CORES))
        over_own.append(send(now[0], CORES))
        done = [own[-1], side[-1], over_own[-1]]
        if t < 3:
            done.append(quads[-1])
        if t:
            done.append(over_side[-1])
        done = list(all_done(*done))
        own[-1], side[-1], over_own[-1] = done[:3]
        if t < 3:
            quads[-1] = done[3]
        if t:
            over_side[-1] = done[-1]
    over_side.append(send(side[3], CORES))
    over_side[3], *quads = all_done(over_side[3], *quads)
    backs = quads + [send(q, CORES) for q in quads]
    return own + side + over_own + over_side, backs, place


def over_replicas(share):
    share = lax.reduce_precision(share, 8, 7)
    return share + send(share.astype(BF16), REPLICA).astype(F32)


def to_owner(total):
    y, z, x, core, sign = here()
    parts = total.reshape(2, 2, 12, total.shape[-1])
    keep, got = pick(parts, core, 1), send(pick(parts, 1 - core, 1), CORES)
    low = core == 0
    ring = jnp.concatenate([jnp.where(low, keep, got), jnp.where(low, got, keep)], axis=0)
    share = pick(ring, x).astype(F32)
    for k in (1, 2, 3):
        share = share + send(pick(ring, (x + k) % 4), X_BY[k]).astype(F32)
    return share


HALF = 48
BLOCKS = WIDTH // (2 * HALF)
WINDOWS = (0, 0, 64, 128, 192, 256, 320, 320)
SPAN = 192
GROUP = 4 * HEAD_DIM
VMEM = pl.BlockSpec(memory_space=pltpu.VMEM)
SMEM = pl.BlockSpec(memory_space=pltpu.SMEM)
ANY = pl.BlockSpec(memory_space=pl.ANY)


def limit(mib):
    return pltpu.CompilerParams(vmem_limit_bytes=mib * 1024 * 1024)


COST = pl.CostEstimate(flops=10**6, bytes_accessed=10**5, transcendentals=0)
URGENT = pl.CostEstimate(flops=3 * 10**10, bytes_accessed=10**5, transcendentals=0)
CHUNK_ONE = 3 * WIDTH + 128
CHUNK_TWO = FF + WIDTH


def dot(a, b):
    return lax.dot_general(a, b, (((1,), (0,)), ((), ())), preferred_element_type=F32)


def dot_nt(a, b):
    return lax.dot_general(a, b, (((1,), (1,)), ((), ())), preferred_element_type=F32)


def dot_tn(a, b):
    return lax.dot_general(a, b, (((0,), (0,)), ((), ())), preferred_element_type=F32)


def normed(values):
    centre = values - jnp.mean(values, axis=-1, keepdims=True)
    scale = lax.rsqrt(jnp.mean(centre * centre, axis=-1, keepdims=True) + 1e-05)
    return centre * scale, scale


def norm_back(d_out, hat, scale, gain):
    expand = d_out * gain
    d_in = scale * (
        expand
        - jnp.mean(expand, axis=-1, keepdims=True)
        - hat * jnp.mean(expand * hat, axis=-1, keepdims=True)
    )
    gain_grad = jnp.sum(d_out * hat, axis=0, keepdims=True)
    return d_in, gain_grad, jnp.sum(d_out, axis=0, keepdims=True)


def rows_at(start, size, step=16):
    return pl.ds(pl.multiple_of(start, step), size)


def places(place_ref):
    core, y, z, x = (place_ref[n] for n in (0, 2, 3, 4))
    return core, y, z, x, 1 - 2 * core


def around(at, step):
    return lax.rem(at + step + 8, 4)


def row_slots(place_ref):
    core, y, z, x, sign = places(place_ref)
    return [
        (row * 4 + around(z, -way * t)) * 2 + half
        for half, way in ((core, sign), (1 - core, -sign))
        for row in (y, 1 - y)
        for t in range(4)
    ]


def back_slots(place_ref):
    core, y, z, x, sign = places(place_ref)
    return [
        ((row * 4 + around(z, -k)) * 4 + around(x, -way * t)) * 2 + half
        for half, way in ((core, sign), (1 - core, -sign))
        for t in range(4)
        for row in (y, 1 - y)
        for k in range(4)
    ]


def piece_copies(slots, pieces, target, sems, first, columns=None):
    copies = []
    each = len(slots) // len(pieces)
    for n, slot in enumerate(slots):
        source = pieces[n // each].at[pl.ds(n % each * HALF, HALF), :]
        if columns is not None:
            source = source.at[:, pl.ds(*columns)]
        copies.append(
            pltpu.make_async_copy(
                source, target.at[rows_at(slot * HALF, HALF)], sems.at[first + n]
            )
        )
    return copies


def split_rows(place_ref, made):
    columns = made.shape[1]
    parts = made.astype(BF16).reshape(BLOCKS, 2, HALF, columns)
    first, second = (parts[:, n].reshape(BLOCKS * HALF, columns) for n in range(2))
    low = place_ref[0] == 0
    return lax.select(low, second, first), lax.select(low, first, second)


def head_of(rows):
    return lax.broadcasted_iota(jnp.int32, (rows, GROUP), 1) // HEAD_DIM


def four_heads(group):
    head, zero = head_of(group.shape[0]), jnp.zeros_like(group)
    return jnp.concatenate([jnp.where(head == h, group, zero) for h in range(4)], axis=0)


def one_of_four(wide):
    n = wide.shape[0] // 4
    head, result = head_of(n), wide[:n]
    for h in range(1, 4):
        result = jnp.where(head == h, wide[h * n : (h + 1) * n], result)
    return result


def fill_bias(place_ref, lengths_ref, bias):
    ends, total = [], jnp.int32(0)
    for k in range(16):
        total = total + lengths_ref[k, place_ref[1]]
        ends.append(total)

    def ids(at):
        return sum((at >= end).astype(jnp.int32) for end in ends)

    keys = ids(lax.broadcasted_iota(jnp.int32, (LEN, 1), 0))
    lane = lax.broadcasted_iota(jnp.int32, (1, GROUP), 1) % HEAD_DIM
    for i, start in enumerate(WINDOWS):
        same = keys[start : start + SPAN] == ids(lane + i * 64)
        bias[i] = jnp.where(same, 0.0, -1e30).astype(F32)


def pack_kernel(*refs):
    vectors, in_bias, w_qkv, w_in, w_out, out, made = refs[:8], *refs[8:]
    rows = w_qkv.shape[0]
    same = lax.broadcasted_iota(jnp.int32, (rows, rows), 0) == lax.broadcasted_iota(
        jnp.int32, (rows, rows), 1
    )
    lane = lax.broadcasted_iota(jnp.int32, (rows, 128), 1)
    total = jnp.zeros((rows, 128), F32)
    for i, ref in enumerate(vectors):
        wide = jnp.broadcast_to(ref[...].astype(F32), (rows, rows))
        column = jnp.sum(jnp.where(same, wide, 0.0), axis=1, keepdims=True)
        total = jnp.where(lane == i, column, total)
    made[...] = total
    made[0:1, 16:64] = in_bias[...].astype(F32)
    out[:, : 3 * WIDTH] = w_qkv[...]
    out[:, 3 * WIDTH : CHUNK_ONE] = made[...].astype(BF16)
    out[:, CHUNK_ONE : CHUNK_ONE + FF] = w_in[...]
    out[:, CHUNK_ONE + FF :] = w_out[...]


def pack(vectors, in_bias, w_qkv, w_in, w_out):
    return pl.pallas_call(
        pack_kernel,
        out_shape=jax.ShapeDtypeStruct((12, CHUNK_ONE + CHUNK_TWO), BF16),
        in_specs=[VMEM] * 12,
        out_specs=VMEM,
        scratch_shapes=[pltpu.VMEM((12, 128), F32)],
        name="pack",
    )(*(v.reshape(1, 12) for v in vectors), in_bias.reshape(1, 48), w_qkv, w_in, w_out)


def first_kernel(place, lengths, tokens, *refs):
    pieces = refs[:16]
    proj_out, mixed, logsum, in_bias, rows, proj, weight, vec, wide, bias, sems = refs[16:]
    slots = row_slots(place)
    copies = piece_copies(slots, pieces, weight, sems, 0, (0, 3 * WIDTH))
    copies += piece_copies(slots, pieces, vec, sems, 16, (3 * WIDTH, 128))
    for copy in copies:
        copy.start()
    fill_bias(place, lengths, bias)
    hat, unused = normed(tokens[...].astype(F32))
    for copy in copies:
        copy.wait()
    wide[...] = vec[...].astype(F32)
    rows[...] = wide[...].T[:16]
    for n in range(64):
        in_bias[:, n * 48 : (n + 1) * 48] = wide[n * 12 : n * 12 + 1, 16:64]
    act = (hat * rows[0:1, :] + rows[1:2, :]).astype(BF16)
    for n in range(9):
        at = pl.ds(n * 256, 256)
        made = dot(act, weight[:, at])
        if n // 3 != 1:
            made = made + rows[2 + n // 6 : 3 + n // 6, (n % 3) * 256 : (n % 3 + 1) * 256]
        proj[:, at] = made.astype(BF16)
    out_copy = pltpu.make_async_copy(proj, proj_out, sems.at[32])
    out_copy.start()
    for p in range(HEADS // 4):
        query_at, keys_at, vals_at = (pl.ds(n * WIDTH + p * GROUP, GROUP) for n in range(3))
        for i, start in enumerate(WINDOWS):
            here_rows, near = pl.ds(i * 64, 64), pl.ds(start, SPAN)
            query = four_heads(proj[here_rows, query_at] * HEAD_DIM ** (-0.5))
            scores = dot_nt(proj[near, keys_at], query) + bias[i]
            top = jnp.max(scores, axis=0, keepdims=True)
            expo = jnp.exp(scores - top)
            total = jnp.sum(expo, axis=0, keepdims=True)
            probs = (expo * (1.0 / total)).astype(BF16)
            mixed[here_rows, query_at] = one_of_four(dot_tn(probs, proj[near, vals_at])).astype(BF16)
            logsum[p * 8 + i : p * 8 + i + 1, :] = top + jnp.log(total)
    out_copy.wait()


def run_first(place, lengths, tokens, pieces):
    return pl.pallas_call(
        first_kernel,
        out_shape=[
            jax.ShapeDtypeStruct((LEN, 3 * WIDTH), BF16),
            jax.ShapeDtypeStruct((LEN, WIDTH), BF16),
            jax.ShapeDtypeStruct((24, 256), F32),
            jax.ShapeDtypeStruct((1, FF), F32),
            jax.ShapeDtypeStruct((16, WIDTH), F32),
        ],
        in_specs=[SMEM, SMEM, VMEM] + [ANY] * 16,
        out_specs=[ANY] + [VMEM] * 4,
        scratch_shapes=[
            pltpu.VMEM((LEN, 3 * WIDTH), BF16),
            pltpu.VMEM((WIDTH, 3 * WIDTH), BF16),
            pltpu.VMEM((WIDTH, 128), BF16),
            pltpu.VMEM((WIDTH, 128), F32),
            pltpu.VMEM((8, SPAN, GROUP), F32),
            pltpu.SemaphoreType.DMA((33,)),
        ],
        compiler_params=limit(60),
        cost_estimate=COST,
        name="attention_forward",
    )(place, lengths, tokens, *pieces)


def gelu_pair(x):
    phi = 0.5 + 0.5 * lax.erf(x * 0.5**0.5)
    return x * phi, phi + x * (jnp.exp(x * (x * -0.5)) * 0.3989422804014327)


def feed_kernel(place, tokens, mixed, cot, rows, in_bias, *refs):
    pieces, backs = refs[:16], refs[16:24]
    hidden, g1, d_mixed, vector_grads, in_bias_grad = refs[24:29]
    give, keep, give_back, keep_back, give_out, keep_out = refs[29:35]
    w_out, w_in, w_back, x1, hat, scale, act, acc, d_act = refs[35:44]
    gact_0, gact_1, d_pre_0, d_pre_1 = refs[44:48]
    made_give, made_keep, made_give_back, made_keep_back, sems, out_sems = refs[48:]
    gact, d_pre = (gact_0, gact_1), (d_pre_0, d_pre_1)
    slots = row_slots(place)
    out_copies = piece_copies(slots, pieces, w_out, sems, 0, (CHUNK_ONE + FF, WIDTH))
    in_copies = piece_copies(slots, pieces, w_in, sems, 16, (CHUNK_ONE, FF))
    back_copies = piece_copies(back_slots(place), backs, w_back, sems, 32)
    for copy in out_copies + in_copies + back_copies:
        copy.start()
    for copy in out_copies:
        copy.wait()
    for n in range(3):
        at = pl.ds(n * 256, 256)
        x1[:, at] = tokens[:, at].astype(F32) + (dot(mixed[...], w_out[:, at]) + rows[4:5, at])
    hat[...], scale[...] = normed(x1[...])
    act[...] = (hat[...] * rows[5:6, :] + rows[6:7, :]).astype(BF16)
    for copy in in_copies + back_copies:
        copy.wait()

    def units(j, n):
        local, at = pl.ds(n * 256, 256), pl.ds(j * WIDTH + n * 256, 256)
        value, slope = gelu_pair(dot(act[...], w_in[:, at]) + in_bias[:, at])
        gact[j % 2][:, local] = value.astype(BF16)
        d_low = (dot_nt(cot[...], w_back[at, :]) * slope).astype(BF16)
        d_pre[j % 2][:, local] = d_low
        in_bias_grad[:, at] = jnp.sum(d_low.astype(F32), axis=0, keepdims=True)

    def sums(j, n):
        at, block, half = pl.ds(n * 256, 256), pl.ds(j * WIDTH, WIDTH), pl.ds(j * 384, 384)
        forward = dot(gact[j % 2][...], w_back[block, at])
        backward = dot_nt(d_pre[j % 2][...], w_in[at, block])
        acc[:, at] = forward if j == 0 else acc[:, at] + forward
        d_act[:, at] = backward if j == 0 else d_act[:, at] + backward
        wide = pl.ds(j * WIDTH + n * 256, 256)
        made_give[:, wide], made_keep[:, wide] = split_rows(
            place, dot_tn(act[...], d_pre[j % 2][:, at])
        )
        made_give_back[half, at], made_keep_back[half, at] = split_rows(
            place, dot_tn(gact[j % 2][...], cot[:, at])
        )

    copies = []
    for j in range(5):
        for n in range(3):
            if j < 4:
                units(j, n)
            if j:
                sums(j - 1, n)
        if j:
            wide, half = pl.ds((j - 1) * WIDTH, WIDTH), pl.ds((j - 1) * 384, 384)
            for made, out, at in (
                (made_give, give, (slice(None), wide)),
                (made_give_back, give_back, (half, slice(None))),
                (made_keep, keep, (slice(None), wide)),
                (made_keep_back, keep_back, (half, slice(None))),
            ):
                copies.append(
                    pltpu.make_async_copy(made.at[at], out.at[at], out_sems.at[len(copies)])
                )
                copies[-1].start()
    hidden[...] = (x1[...] + (acc[...] + rows[7:8, :])).astype(BF16)
    cot_wide = cot[...].astype(F32)
    d_in, gain_grad, bias_grad = norm_back(d_act[...], hat[...], scale[...], rows[5:6, :])
    total = cot_wide + d_in
    g1[...] = total
    low = total.astype(BF16)
    for n in range(3):
        at = pl.ds(n * 256, 256)
        d_mixed[:, at] = dot_nt(low, w_out[at, :]).astype(BF16)
        give_out[:, at], keep_out[:, at] = split_rows(
            place, dot_tn(mixed[...], low[:, n * 256 : (n + 1) * 256])
        )
    vector_grads[...] = jnp.concatenate(
        [
            jnp.sum(low.astype(F32), axis=0, keepdims=True),
            gain_grad,
            bias_grad,
            jnp.sum(cot_wide, axis=0, keepdims=True),
            jnp.zeros((4, WIDTH), F32),
        ],
        axis=0,
    )
    for copy in copies:
        copy.wait()


def run_feed(place, tokens, mixed, cot, rows, in_bias, pieces, backs):
    wide, tall, low = (WIDTH // 2, FF), (FF // 2, WIDTH), (LEN, WIDTH)
    return pl.pallas_call(
        feed_kernel,
        out_shape=[
            jax.ShapeDtypeStruct(low, BF16),
            jax.ShapeDtypeStruct(low, F32),
            jax.ShapeDtypeStruct(low, BF16),
            jax.ShapeDtypeStruct((8, WIDTH), F32),
            jax.ShapeDtypeStruct((1, FF), F32),
            jax.ShapeDtypeStruct(wide, BF16),
            jax.ShapeDtypeStruct(wide, BF16),
            jax.ShapeDtypeStruct(tall, BF16),
            jax.ShapeDtypeStruct(tall, BF16),
            jax.ShapeDtypeStruct((WIDTH // 2, WIDTH), BF16),
            jax.ShapeDtypeStruct((WIDTH // 2, WIDTH), BF16),
        ],
        in_specs=[SMEM] + [VMEM] * 5 + [ANY] * 24,
        out_specs=[VMEM] * 5 + [ANY] * 4 + [VMEM] * 2,
        scratch_shapes=[
            pltpu.VMEM((WIDTH, WIDTH), BF16),
            pltpu.VMEM((WIDTH, FF), BF16),
            pltpu.VMEM((FF, WIDTH), BF16),
            pltpu.VMEM(low, F32),
            pltpu.VMEM(low, F32),
            pltpu.VMEM((LEN, 1), F32),
            pltpu.VMEM(low, BF16),
            pltpu.VMEM(low, F32),
            pltpu.VMEM(low, F32),
        ]
        + [pltpu.VMEM(low, BF16)] * 4
        + [pltpu.VMEM(wide, BF16)] * 2
        + [pltpu.VMEM(tall, BF16)] * 2
        + [pltpu.SemaphoreType.DMA((96,)), pltpu.SemaphoreType.DMA((16,))],
        compiler_params=limit(60),
        cost_estimate=COST,
        name="feed_forward",
    )(place, tokens, mixed, cot, rows, in_bias, *pieces, *backs)


def attend_back_kernel(
    place, lengths, proj, logsum, d_mixed, d_out, d_proj, bias, d_keys, d_vals, sems
):
    fill_bias(place, lengths, bias)

    def write(p, n):
        at = rows_at(n * WIDTH + p * GROUP, GROUP, GROUP)
        return pltpu.make_async_copy(d_proj.at[:, at], d_out.at[:, at], sems.at[p * 3 + n])

    def attend(p, carry):
        query_at, keys_at, vals_at = (
            rows_at(n * WIDTH + p * GROUP, GROUP, GROUP) for n in range(3)
        )
        d_keys[...] = jnp.zeros_like(d_keys)
        d_vals[...] = jnp.zeros_like(d_vals)
        for i, start in enumerate(WINDOWS):
            here_rows, near = pl.ds(i * 64, 64), pl.ds(start, SPAN)
            query = four_heads(proj[here_rows, query_at] * HEAD_DIM ** (-0.5))
            keys, vals = proj[near, keys_at], proj[near, vals_at]
            d_mix = four_heads(d_mixed[here_rows, query_at])
            probs = jnp.exp(dot_nt(keys, query) + bias[i] - logsum[pl.ds(p * 8 + i, 1), :])
            d_probs = dot_nt(vals, d_mix)
            mean = jnp.sum(probs * d_probs, axis=0, keepdims=True)
            d_scores = (probs * (d_probs - mean)).astype(BF16)
            d_query = one_of_four(dot_tn(d_scores, keys)) * HEAD_DIM ** (-0.5)
            d_proj[here_rows, query_at] = d_query.astype(BF16)
            d_keys[near, :] += dot(d_scores, query)
            d_vals[near, :] += dot(probs.astype(BF16), d_mix)
        d_proj[:, keys_at] = d_keys[...].astype(BF16)
        d_proj[:, vals_at] = d_vals[...].astype(BF16)
        for n in range(3):
            write(p, n).start()
        return carry

    lax.fori_loop(0, HEADS // 4, attend, 0)
    for p in range(HEADS // 4):
        for n in range(3):
            write(p, n).wait()


def run_attend_back(place, lengths, proj, logsum, d_mixed):
    return pl.pallas_call(
        attend_back_kernel,
        out_shape=jax.ShapeDtypeStruct((LEN, 3 * WIDTH), BF16),
        in_specs=[SMEM, SMEM] + [VMEM] * 3,
        out_specs=ANY,
        scratch_shapes=[
            pltpu.VMEM((LEN, 3 * WIDTH), BF16),
            pltpu.VMEM((8, SPAN, GROUP), F32),
            pltpu.VMEM((LEN, GROUP), F32),
            pltpu.VMEM((LEN, GROUP), F32),
            pltpu.SemaphoreType.DMA((9,)),
        ],
        compiler_params=limit(60),
        cost_estimate=COST,
        name="attention_backward",
    )(place, lengths, proj, logsum, d_mixed)


FIRST_HALVES = np.arange(WIDTH, dtype=np.int32).reshape(BLOCKS, 2, HALF)[:, 0].reshape(1, -1)


def project_back_kernel(place, tokens, tokens_over, d_proj, d_over, rows, grads_two, in_bias, *refs):
    order, pieces = refs[0], refs[1:17]
    d_act, theirs, mine, give, keep, made_theirs, made_mine, weight, natural, sems = refs[17:]
    core, y, unused, unused, unused = places(place)
    copies = piece_copies(row_slots(place), pieces, weight, sems, 0, (0, 3 * WIDTH))
    for copy in copies:
        copy.start()
    half = order[...] + HALF * core
    half = (lax.broadcasted_iota(jnp.int32, (WIDTH, WIDTH // 2), 0) == half).astype(F32)
    half = half.astype(BF16)
    hat, unused = normed(tokens[...].astype(F32))
    hat_over, unused = normed(tokens_over[...].astype(F32))
    act, act_over = (
        dot((h * rows[0:1, :] + rows[1:2, :]).astype(BF16), half).astype(BF16)
        for h in (hat, hat_over)
    )
    outs = []
    for n in range(9):
        at = pl.ds(n * 256, 256)
        made = (dot_tn(act, d_proj[:, at]) + dot_tn(act_over, d_over[:, at])).astype(BF16)
        low, high = made[: 4 * HALF], made[4 * HALF :]
        made_theirs[:, at] = lax.select(y == 0, high, low)
        made_mine[:, at] = lax.select(y == 0, low, high)
        if n % 3 == 2:
            wide = pl.ds((n - 2) * 256, WIDTH)
            for made, out in ((made_theirs, theirs), (made_mine, mine)):
                outs.append(
                    pltpu.make_async_copy(
                        made.at[:, wide], out.at[:, wide], sems.at[16 + len(outs)]
                    )
                )
                outs[-1].start()
    for copy in copies:
        copy.wait()
    for n in range(3):
        at = pl.ds(n * 256, 256)
        d_act[:, at] = dot_nt(d_proj[...], weight[at, :])
    made = jnp.concatenate(
        [
            jnp.sum(d_act[...] * hat, axis=0, keepdims=True),
            jnp.sum(d_act[...], axis=0, keepdims=True),
            jnp.sum(d_proj[:, :WIDTH].astype(F32), axis=0, keepdims=True),
            jnp.sum(d_proj[:, 2 * WIDTH :].astype(F32), axis=0, keepdims=True),
            grads_two[:4, :],
            jnp.zeros((120, WIDTH), F32),
        ],
        axis=0,
    )
    natural[...] = made.T
    for n in range(64):
        natural[n * 12 : n * 12 + 1, 16:64] = in_bias[:, n * 48 : (n + 1) * 48]
    give[...], keep[...] = split_rows(place, natural[...])
    for copy in outs:
        copy.wait()


def run_project_back(place, tokens, tokens_over, d_proj, d_over, rows, grads_two, in_bias, pieces):
    part, vector = (4 * HALF, 3 * WIDTH), (WIDTH // 2, 128)
    return pl.pallas_call(
        project_back_kernel,
        out_shape=[
            jax.ShapeDtypeStruct((LEN, WIDTH), F32),
            jax.ShapeDtypeStruct(part, BF16),
            jax.ShapeDtypeStruct(part, BF16),
            jax.ShapeDtypeStruct(vector, BF16),
            jax.ShapeDtypeStruct(vector, BF16),
        ],
        in_specs=[SMEM] + [VMEM] * 8 + [ANY] * 16,
        out_specs=[VMEM, ANY, ANY, VMEM, VMEM],
        scratch_shapes=[
            pltpu.VMEM(part, BF16),
            pltpu.VMEM(part, BF16),
            pltpu.VMEM((WIDTH, 3 * WIDTH), BF16),
            pltpu.VMEM((WIDTH, 128), F32),
            pltpu.SemaphoreType.DMA((22,)),
        ],
        compiler_params=limit(60),
        cost_estimate=COST,
        name="project_backward",
    )(
        place,
        tokens,
        tokens_over,
        d_proj,
        d_over,
        rows,
        grads_two,
        in_bias,
        jnp.asarray(FIRST_HALVES),
        *pieces,
    )


def input_grad_kernel(tokens, d_act, g1, rows, d_input):
    hat, scale = normed(tokens[...].astype(F32))
    d_in, unused, unused = norm_back(d_act[...], hat, scale, rows[0:1, :])
    d_input[...] = g1[...] + d_in


def run_input_grad(tokens, d_act, g1, rows):
    return pl.pallas_call(
        input_grad_kernel,
        out_shape=jax.ShapeDtypeStruct((LEN, WIDTH), F32),
        in_specs=[VMEM] * 4,
        out_specs=VMEM,
        compiler_params=limit(60),
        cost_estimate=COST,
        name="input_gradient",
    )(tokens, d_act, g1, rows)


def after_kernel(place, *refs):
    for n in range(place.shape[0]):
        refs[-1][n] = place[n]


def run_after(place, *arrays):
    return pl.pallas_call(
        after_kernel,
        out_shape=jax.ShapeDtypeStruct(place.shape, place.dtype),
        in_specs=[SMEM] + [ANY] * len(arrays),
        out_specs=SMEM,
        cost_estimate=URGENT,
        name="after",
    )(place, *arrays)


def run_split(name, place, arrays, plan, cost=COST):
    drafts = plan(0, 0, 0, 1)
    shapes = [
        (sum(count for count, unused in parts), HALF, sum(width for width, unused in parts[0][1]))
        for unused, parts in drafts
    ]
    buffers = [
        pltpu.VMEM((count, HALF, width), arrays[i].dtype)
        for unused, parts in drafts
        for count, segments in parts
        for width, sources in segments
        for i, unused, unused in sources
    ]

    def kernel(place_ref, *refs):
        refs = list(refs)
        ins, outs, held, made = (
            [refs.pop(0) for unused in group] for group in (arrays, shapes, buffers, shapes)
        )
        in_sems, out_sems = refs
        unused, y, z, x, sign = places(place_ref)
        plans, copies = plan(y, z, x, sign), []
        for unused, parts in plans:
            for unused, segments in parts:
                for width, sources in segments:
                    for i, index, column in sources:
                        if not isinstance(column, int):
                            column = pl.multiple_of(column, 128)
                        n = len(copies)
                        copies.append(
                            pltpu.make_async_copy(
                                ins[i].at[(*index, slice(None), pl.ds(column, width))],
                                held[n],
                                in_sems.at[n],
                            )
                        )
                        copies[-1].start()
        n, writes = 0, []
        for o, (kind, parts) in enumerate(plans):
            row = 0
            for count, segments in parts:
                column = 0
                for width, sources in segments:
                    total = None
                    for unused in sources:
                        copies[n].wait()
                        value = held[n][...].astype(F32)
                        total = value if total is None else total + value
                        n += 1
                    made[o][row : row + count, :, column : column + width] = total.astype(kind)
                    column += width
                row += count
            writes.append(pltpu.make_async_copy(made[o], outs[o], out_sems.at[o]))
            writes[-1].start()
        for write in writes:
            write.wait()

    return pl.pallas_call(
        kernel,
        out_shape=[jax.ShapeDtypeStruct(s, kind) for s, (kind, unused) in zip(shapes, drafts)],
        in_specs=[SMEM] + [ANY] * len(arrays),
        out_specs=[ANY] * len(shapes),
        scratch_shapes=buffers
        + [pltpu.VMEM(s, kind) for s, (kind, unused) in zip(shapes, drafts)]
        + [pltpu.SemaphoreType.DMA((len(buffers),)), pltpu.SemaphoreType.DMA((len(shapes),))],
        compiler_params=limit(60),
        cost_estimate=cost,
        name=name,
    )(place, *arrays)


def shards(tokens, lengths, g1, s1, wqkv, qb, vb, wo, ob, g2, s2, w1, bi1, w2, b2, cotangent):
    y, z, x, core, sign = here()
    place = jnp.stack([core, lax.axis_index("dp") * 64 + lax.axis_index("fsdp"), y, z, x])
    lengths = lengths.T
    pieces, backs, place = gather(
        lambda: pack((g1, s1, qb, vb, ob, g2, s2, b2), bi1, wqkv, w1, wo), w2, place
    )
    proj, mixed, logsum, in_bias, rows = run_first(place, lengths, tokens, pieces)
    hidden, d_middle, d_mixed, grads_two, in_bias_grad, *grads = run_feed(
        place, tokens, mixed, cotangent, rows, in_bias, pieces, backs
    )
    give_i, keep_i, give_b, keep_b, give_o, keep_o = grads
    got_i, got_b, got_o = send(give_i, CORES), send(give_b, CORES), send(give_o, CORES)
    d_proj = run_attend_back(place, lengths, proj, logsum, d_mixed)
    d_proj, got_i, got_b, got_o = all_done(d_proj, got_i, got_b, got_o)
    d_over, tokens_over = send(d_proj, CORES), send(tokens, CORES)

    blocks = lambda a, *lead: a.reshape(*lead, HALF, a.shape[-1])
    whole = (slice(None),)
    wide = ((FF, (0, 1)), (WIDTH, (2, 3)))

    def own_in(at):
        return [(4, [(n, [(i, (pl.ds(at * 4, 4),), 0) for i in ids]) for n, ids in wide])]

    sums_in = [blocks(a, 8) for a in (keep_i, got_i, keep_o, got_o)]
    sums_back = [blocks(a, 8, 4) for a in (keep_b, got_b)]
    (theirs,) = run_split(
        "sum_cores_in", place, sums_in, lambda y, z, x, sign: [(BF16, own_in(1 - y))]
    )
    from_y = send(theirs, Y_RING)
    def back(at, first, count, *more):
        sources = [(i, (pl.ds(first, count), at), 0) for i in (0, 1)]
        return (count, [(WIDTH, sources + [(i, whole, 0) for i in more])])

    far_up, far_down = run_split(
        "sum_cores_back",
        place,
        sums_back,
        lambda y, z, x, sign: [
            (BF16, [back(around(x, 2), 0, 4)]),
            (BF16, [back(around(x, 2), 4, 4)]),
        ],
    )
    d_proj, d_over, tokens_over, far_up, far_down = all_done(
        d_proj, d_over, tokens_over, far_up, far_down
    )
    from_x = [send(far_up, X_BY[1]), send(far_down, X_BY[3])]
    d_act, theirs, mine_q, give_v, keep_v = run_project_back(
        place, tokens, tokens_over, d_proj, d_over, rows, grads_two, in_bias_grad, pieces
    )
    d_act, theirs, mine_q, give_v, from_y, *from_x = all_done(
        d_act, theirs, mine_q, give_v, from_y, *from_x
    )

    from_y_q = send(blocks(theirs, 4), Y_RING)
    got_v = send(give_v, CORES)
    add = lambda a, b: (a.astype(F32) + b.astype(F32)).astype(BF16)
    up, down = run_split(
        "sum_x_2",
        place,
        (*sums_back, *from_x),
        lambda y, z, x, sign: [
            (BF16, [back(around(x, 1), 0, 4, 2), back(around(x, 1), 4, 4)]),
            (BF16, [back(around(x, 3), 0, 4), back(around(x, 3), 4, 4, 3)]),
        ],
    )
    from_x = [send(up, X_BY[1]), send(down, X_BY[3])]

    def after_y(y, z, x, sign):
        def both(at):
            own = (pl.ds(y * 4 + at, 1),)
            segments = []
            for (n, ids), column in zip(wide, (0, FF)):
                sources = [(i, own, 0) for i in ids] + [(4, (pl.ds(at, 1),), column)]
                segments.append((n, sources))
            return [(1, segments)]

        return [(BF16, both(around(z, k))) for k in (1, 3, 2, 0)]

    *parts, own_i = run_split("sum_y", place, (*sums_in, from_y), after_y)
    d_act, got_v, own_i, *parts = all_done(d_act, got_v, own_i, *parts)
    from_z_i = [send(p, Z_BY[k]) for p, k in zip(parts, (1, 3, 2))]
    kept_v = add(keep_v, got_v).reshape(2, 4, HALF, 128)
    mine_v, from_y_v = pick(kept_v, y), send(pick(kept_v, 1 - y), Y_RING)
    mine_v, from_y, from_y_v = all_done(mine_v, from_y_q, from_y_v)

    def along_z(y, z, x, sign):
        pair = lambda n, ids, at: (n, [(i, (pl.ds(at, 1),), 0) for i in ids])
        part = lambda at: [(1, [pair(3 * WIDTH, (0, 1), at), pair(128, (2, 3), at)])]
        return [(BF16, part(around(z, k))) for k in (1, 3, 2, 0)]

    *parts, own = run_split(
        "sum_y_rest", place, (blocks(mine_q, 4), from_y, mine_v, from_y_v), along_z
    )
    from_z = [send(p, Z_BY[k]) for p, k in zip(parts, (1, 3, 2))]

    def back_along_z(y, z, x, sign):
        def part(at):
            sources = [(i, (pl.ds(at, 1), x), 0) for i in (0, 1)]
            sources += [(i, (pl.ds(at, 1),), 0) for i in (2, 3)]
            return (1, [(WIDTH, sources)])

        return [(BF16, [part(around(z, k)), part(4 + around(z, k))]) for k in (1, 3, 2, 0)]

    *parts, own_b = run_split("sum_x", place, (*sums_back, *from_x), back_along_z)
    from_z_b = [send(p, Z_BY[k]) for p, k in zip(parts, (1, 3, 2))]
    d_input = run_input_grad(tokens, d_act, d_middle, rows)
    place = run_after(place, *from_z_i)
    place, d_input, own, own_b, *done = all_done(place, d_input, own, own_b, *from_z, *from_z_b)
    from_z, from_z_b = done[:3], done[3:]

    def last_sum(y, z, x, sign):
        total = lambda width, ids: (width, [(i, whole, 0) for i in ids])
        back = lambda at: [(1, [(WIDTH, [(i, (pl.ds(at, 1),), 0) for i in range(8, 12)])])]
        return [
            (BF16, [(1, [total(CHUNK_ONE, range(4)), total(CHUNK_TWO, range(4, 8))])]),
            (BF16, back(1 - y)),
            (BF16, back(y)),
        ]

    share, theirs, mine = run_split("sum_z", place, (own, *from_z, own_i, *from_z_i, own_b, *from_z_b), last_sum)
    from_y = send(theirs, Y_RING)
    share = to_owner(share)
    back_share = (mine.astype(F32) + from_y.astype(F32)).reshape(HALF, WIDTH)
    share, back_share = all_done(share, back_share)
    share, back_share = over_replicas(share), over_replicas(back_share)
    own = share[:, 3 * WIDTH : CHUNK_ONE]
    return (
        hidden,
        d_input,
        own[:, 0],
        own[:, 1],
        share[:, : 3 * WIDTH],
        own[:, 2],
        own[:, 3],
        share[:, CHUNK_ONE + FF :],
        own[:, 4],
        own[:, 5],
        own[:, 6],
        share[:, CHUNK_ONE : CHUNK_ONE + FF],
        own[0, 16:64],
        back_share,
        own[:, 7],
    )


def solution(mesh):
    rows, whole = P(AXES, None), P()
    vector, matrix = P("fsdp"), P("fsdp", None)
    weights = (
        vector, vector, matrix, vector, vector, matrix, vector,
        vector, vector, matrix, vector, matrix, vector,
    )
    return jax.shard_map(
        shards,
        mesh=mesh,
        in_specs=(rows, whole, *weights, rows),
        out_specs=(rows, rows, *weights),
        check_vma=False,
    )
```
